32 devices in a mesh: dp: 4 (over y, x), group: 8 (over z, core).
Axes of the slice: x: 2, y: 2, z: 4, core: 2. Of those that a mesh axis runs over, the one named last changes fastest.
Arguments:
- hidden_in: bfloat16 [4, 2048, 2048], P('dp', 'group'), may hold values from -6 to 6
- cotangent: bfloat16 [4, 2048, 2048], P('dp', 'group'), may hold values from -6 to 6
- segment_ids: int32 [4, 2048], P('dp'), may hold values from 0 to 3, never falling along the last dimension, each value on 1 to 1024 neighbouring positions
- weight_in: bfloat16 [32, 448, 2048], P(('dp', 'group')), may hold values from -0.125 to 0.125
- weight_back: bfloat16 [32, 320, 2048], P(('dp', 'group')), may hold values from -1 to 1
- moment_in: float32 [32, 448, 2048], P(('dp', 'group')), may hold values from -112 to 112
- moment_back: float32 [32, 320, 2048], P(('dp', 'group')), may hold values from -160 to 160
- norm_gain: float32 [2048], replicated, may hold values from 0.5 to 1.5
- norm_shift: float32 [2048], replicated, may hold values from -1.75 to 1.75
- bias_in: float32 [14336], replicated, may hold values from -3 to 3
- bias_out: float32 [2048], replicated, may hold values from -3 to 3
- vector_moment: float32 [20480], replicated, may hold values from -256 to 256
Outputs:
- block_out: bfloat16 [4, 2048, 2048], P('dp', 'group')
- grad_hidden: float32 [4, 2048, 2048], P('dp', 'group')
- grad_in: float32 [32, 448, 2048], P(('dp', 'group'))
- grad_back: float32 [32, 320, 2048], P(('dp', 'group'))
- moment_in_new: float32 [32, 448, 2048], P(('dp', 'group'))
- moment_back_new: float32 [32, 320, 2048], P(('dp', 'group'))
- step_in: float32 [32, 448, 2048], P(('dp', 'group'))
- step_back: float32 [32, 320, 2048], P(('dp', 'group'))
- vector_grad: float32 [20480], replicated
- vector_moment_new: float32 [20480], replicated
- vector_step: float32 [20480], replicated
- bias_out_grad: float32 [2048], replicated
The draws below stay inside these ranges and needn't reach their ends.
Inputs may be any that keep to these rules, and one draw needn't show every extreme that they name: `segment_ids`: in each pack the numbers never fall; every sequence has 1 to 1024 tokens and one has exactly 1024.
All inputs are finite; a program needn't handle non-finite values.
Results may differ from the reference program's by a relative error of at most 0.04.
Values may be sent and summed in bfloat16 or wider, within the bound.
No kernel may reach another device: no remote copies, remote signals or barrier semaphores. Data moves between devices by JAX's collectives and lax.ppermute only.
A program may use at most 832 MiB of HBM per device.

```python
import math
import jax
import jax.numpy as jnp
import numpy as np
from jax import lax

D = 2048
HEADS = 32
HEAD = 64
ROT = 32
FF = 8192
SEQ_MAX = 1024
NS_ITERS = 5
PACK = 2048
TOKENS = 8192
SEGS = 4
IN_DEV = 448
BACK_DEV = 320
VEC = 20480
N_DP = 4
DEVICES = 32


def draw_weight_back(key, part):
    row_index = jnp.arange(BACK_DEV, dtype=jnp.int32)[None, :, None]
    row_scale = jnp.where(row_index < D // DEVICES, 8.0 / math.sqrt(D), 1.0 / math.sqrt(FF))
    standard = jax.random.normal(key, (DEVICES, BACK_DEV, D), jnp.float32)
    return jnp.clip(standard * row_scale, -1.0, 1.0).astype(jnp.bfloat16)


def shard_levels(key, shape, split, least, top_value):
    def one(axis_at, shards_of):
        draws = jax.random.uniform(jax.random.fold_in(jax.random.fold_in(key, 6), axis_at), (shards_of,), jnp.float32, least / len(split), top_value / len(split))
        return jnp.repeat(jnp.exp(draws), shape[axis_at] // shards_of).reshape((-1,) + (1,) * (len(shape) - axis_at - 1))

    factor_of = one(*split[0])
    for cut in split[1:]:
        factor_of = factor_of * one(*cut)
    return factor_of


def length_profile(number_of, total, bound, skew):
    weights = [(1 << 20) // math.isqrt(standing ** skew) + 1 for standing in range(2, number_of + 1)]
    surplus, counts = total - bound - (number_of - 1), [1] * (number_of - 1)
    while surplus > 0:
        candidates = [i for i in range(number_of - 1) if counts[i] < bound]
        pool, budget = sum([weights[i] for i in candidates]), surplus
        for i in candidates:
            addition = min(bound - counts[i], max(1, budget * weights[i] // pool), surplus)
            counts[i] = counts[i] + addition
            surplus = surplus - addition
    return np.array([bound] + counts)


def ragged(own_key, number_of, total, limit, lean):
    if number_of == 2:
        one = jax.random.randint(own_key, (), max(1, total - limit), min(limit, total - 1) + 1)
        return jnp.stack([one, total - one])
    lengths = jnp.asarray(length_profile(number_of, total, limit, lean), jnp.int32)
    couples = (number_of - 1) // 2
    donor, receiver = lengths[1:1 + 2 * couples:2], lengths[2:2 + 2 * couples:2]
    room = jnp.minimum(donor - 1, limit - receiver)
    passed = jax.random.randint(jax.random.fold_in(own_key, 1), (couples,), 0, 1 << 20) % (room + 1)
    lengths = lengths.at[1:1 + 2 * couples:2].set(donor - passed).at[2:2 + 2 * couples:2].set(receiver + passed)
    return lengths[jax.random.permutation(jax.random.fold_in(own_key, 2), number_of)]


def centred(own_key, shape, scale, reach, shards=(), held_as=jnp.bfloat16):
    drawn = scale * jax.random.normal(own_key, shape, jnp.float32)
    if shards:
        drawn = drawn * shard_levels(own_key, shape, shards, -0.22, 0.18)
    return jnp.clip(drawn, -reach, reach).astype(held_as)


def setup_inputs(seed: int = 0) -> dict:
    arg_keys = jax.random.split(jax.random.key(seed), 13)
    hidden_in = centred(arg_keys[0], (N_DP, PACK, D), 1.0, 6.0, ((0, 4), (1, 8)))
    cotangent = centred(arg_keys[1], (N_DP, PACK, D), 1.0, 6.0, ((0, 4), (1, 8)))
    segment_ids = jax.vmap(lambda own: jnp.searchsorted(jnp.cumsum(ragged(own, SEGS, PACK, SEQ_MAX, 2)), jnp.arange(PACK), side="right"))(jax.random.split(arg_keys[2], N_DP)).reshape((N_DP, PACK)).astype(jnp.int32)
    weight_in = centred(arg_keys[3], (DEVICES, IN_DEV, D), D ** -0.5, 0.125, ((0, 32),))
    weight_back = draw_weight_back(jax.random.fold_in(arg_keys[12], 71), 0)
    moment_in = centred(arg_keys[5], (DEVICES, IN_DEV, D), (0.2 * TOKENS ** 0.5), 112.0, ((0, 32),), jnp.float32)
    moment_back = centred(arg_keys[6], (DEVICES, BACK_DEV, D), (0.3 * TOKENS ** 0.5), 160.0, ((0, 32),), jnp.float32)
    norm_gain = jnp.clip(1.0 + 0.1 * jax.random.normal(arg_keys[7], (D,), jnp.float32), 0.5, 1.5)
    norm_shift = centred(arg_keys[8], (D,), 0.3, 1.75, (), jnp.float32)
    bias_in = centred(arg_keys[9], (3 * D + FF,), 0.5, 3.0, (), jnp.float32)
    bias_out = centred(arg_keys[10], (D,), 0.5, 3.0, (), jnp.float32)
    vector_moment = centred(arg_keys[11], (VEC,), (0.5 * TOKENS ** 0.5), 256.0, (), jnp.float32)
    return {"hidden_in": hidden_in, "cotangent": cotangent, "segment_ids": segment_ids, "weight_in": weight_in, "weight_back": weight_back, "moment_in": moment_in, "moment_back": moment_back, "norm_gain": norm_gain, "norm_shift": norm_shift, "bias_in": bias_in, "bias_out": bias_out, "vector_moment": vector_moment}


HIGH = lax.Precision.HIGHEST
NEG = -1e+30
NS_A = 3.4445
NS_B = -4.775
NS_C = 2.0315
MOMENTUM = 0.95

@jax.custom_vjp
def low(v):
    return lax.optimization_barrier(v.astype(jnp.bfloat16)).astype(jnp.float32)

@jax.custom_vjp
def low_back(v):
    return v

def low_keep(v):
    return (low(v), None)

def low_pass(kept, grad):
    return (grad,)

def back_keep(v):
    return (v, None)

def back_low(kept, grad):
    return (low(grad),)
low.defvjp(low_keep, low_pass)
low_back.defvjp(back_keep, back_low)

def rounded(values):
    return lax.optimization_barrier(values.astype(jnp.bfloat16)).astype(jnp.float32)

def positions(segments):
    index_all = jnp.arange(segments.shape[0], dtype=jnp.int32)
    previous = jnp.concatenate([jnp.full((1,), -1, jnp.int32), segments[:-1]])
    starts = jnp.where(segments != previous, index_all, 0)
    return index_all - lax.cummax(starts, axis=0)

def rotary_tables(position):
    half_rot = ROT // 2
    freq = jnp.exp(jnp.arange(half_rot, dtype=jnp.float32) * (-2.0 * math.log(10000.0) / ROT))
    angle = position.astype(jnp.float32)[:, None] * freq[None, :]
    return (jnp.cos(angle)[:, None, :], jnp.sin(angle)[:, None, :])

def rotate(values, cos_tab, sin_tab):
    half_rot = ROT // 2
    first = values[..., :half_rot]
    second = values[..., half_rot:ROT]
    return jnp.concatenate([first * cos_tab - second * sin_tab, second * cos_tab + first * sin_tab, values[..., ROT:]], axis=-1)

def gelu_tanh(values):
    inner = 0.7978845608028654 * (values + 0.044715 * values * values * values)
    return 0.5 * values * (1.0 + jnp.tanh(inner))

def layer(params, inputs, segments):
    weight_qkv, weight_up, weight_out, weight_down, gain, shift, bias_in, bias_out = params
    pack_len = inputs.shape[0]
    centre = inputs - lax.optimization_barrier(jnp.mean(inputs, axis=-1, keepdims=True))
    spread = lax.optimization_barrier(jnp.mean(centre * centre, axis=-1, keepdims=True))
    normed = low(centre * lax.rsqrt(spread + 1e-05) * gain + shift)
    pre_qkv = low_back(jnp.dot(normed, weight_qkv.T, precision=HIGH) + bias_in[:3 * D])
    pre_up = low_back(jnp.dot(normed, weight_up.T, precision=HIGH) + bias_in[3 * D:])
    cos_tab, sin_tab = rotary_tables(positions(segments))
    query = low(rotate(pre_qkv[:, :D].reshape(pack_len, HEADS, HEAD), cos_tab, sin_tab))
    keys = low(rotate(pre_qkv[:, D:2 * D].reshape(pack_len, HEADS, HEAD), cos_tab, sin_tab))
    values = low(pre_qkv[:, 2 * D:].reshape(pack_len, HEADS, HEAD))
    index_all = jnp.arange(pack_len, dtype=jnp.int32)
    query_block = min(512, pack_len)
    block_count = pack_len // query_block

    def attend(block_item):
        query_part, seg_part, index_part = block_item
        scores = low_back(jnp.einsum('qhe,khe->hqk', query_part, keys, precision=HIGH) * HEAD ** (-0.5))
        allowed = (seg_part[:, None] == segments[None, :]) & (index_all[None, :] <= index_part[:, None])
        scores = jnp.where(allowed[None], scores, NEG)
        probability = low(jax.nn.softmax(scores, axis=-1))
        return jnp.einsum('hqk,khe->qhe', probability, values, precision=HIGH)
    mixed = lax.map(jax.checkpoint(attend), (query.reshape(block_count, query_block, HEADS, HEAD), segments.reshape(block_count, query_block), index_all.reshape(block_count, query_block)))
    attended = low_back(low(mixed.reshape(pack_len, D)))
    activated = low(gelu_tanh(pre_up))
    return inputs + jnp.dot(attended, weight_out, precision=HIGH) + jnp.dot(activated, weight_down, precision=HIGH) + bias_out

def orthogonalize(matrix):
    current = rounded(matrix / (jnp.sqrt(jnp.sum(matrix * matrix)) + 1e-07))
    for iteration in range(NS_ITERS):
        gram = rounded(jnp.dot(current.T, current, precision=HIGH))
        poly = rounded(NS_B * gram + NS_C * jnp.dot(gram, gram, precision=HIGH))
        current = rounded(NS_A * current + jnp.dot(current, poly, precision=HIGH))
    return current

def reference(hidden_in, cotangent, segment_ids, weight_in, weight_back, moment_in, moment_back, norm_gain, norm_shift, bias_in, bias_out, vector_moment):
    qkv_rows = 3 * D // DEVICES
    ff_rows = FF // DEVICES
    out_rows = D // DEVICES
    full_in = weight_in.astype(jnp.float32)
    full_back = weight_back.astype(jnp.float32)
    weight_qkv = full_in[:, :qkv_rows].reshape(3 * D, D)
    weight_up = full_in[:, qkv_rows:].reshape(FF, D)
    weight_out = full_back[:, :out_rows].reshape(D, D)
    weight_down = full_back[:, out_rows:].reshape(FF, D)
    params = (weight_qkv, weight_up, weight_out, weight_down, norm_gain, norm_shift, bias_in, bias_out)

    def one_pack(running, pack_item):
        inputs, grads_out, segments = pack_item
        outputs, pull = jax.vjp(lambda chosen, values: layer(chosen, values, segments), params, inputs.astype(jnp.float32))
        grad_params, grad_inputs = pull(grads_out.astype(jnp.float32))
        running = jax.tree.map(lambda left, right: left + right, running, grad_params)
        return (running, (outputs.astype(jnp.bfloat16), grad_inputs))
    zero_grads = jax.tree.map(jnp.zeros_like, params)
    grads, (block_out, grad_hidden) = lax.scan(one_pack, zero_grads, (hidden_in, cotangent, segment_ids))
    grad_qkv, grad_up, grad_out, grad_down, grad_gain, grad_shift, grad_bias_in, grad_bias_out = grads
    grad_in = jnp.concatenate([grad_qkv.reshape(DEVICES, qkv_rows, D), grad_up.reshape(DEVICES, ff_rows, D)], axis=1)
    grad_back = jnp.concatenate([grad_out.reshape(DEVICES, out_rows, D), grad_down.reshape(DEVICES, ff_rows, D)], axis=1)
    moment_in_new = MOMENTUM * moment_in + grad_in
    moment_back_new = MOMENTUM * moment_back + grad_back
    ortho_qkv = orthogonalize(moment_in_new[:, :qkv_rows].reshape(3 * D, D))
    ortho_up = orthogonalize(moment_in_new[:, qkv_rows:].reshape(FF, D))
    ortho_out = orthogonalize(moment_back_new[:, :out_rows].reshape(D, D))
    ortho_down = orthogonalize(moment_back_new[:, out_rows:].reshape(FF, D))
    step_in = jnp.concatenate([-math.sqrt(3.0 * D) * ortho_qkv.reshape(DEVICES, qkv_rows, D), -math.sqrt(1.0 * FF) * ortho_up.reshape(DEVICES, ff_rows, D)], axis=1)
    step_back = jnp.concatenate([-math.sqrt(1.0 * D) * ortho_out.reshape(DEVICES, out_rows, D), -math.sqrt(1.0 * FF) * ortho_down.reshape(DEVICES, ff_rows, D)], axis=1)
    vector_grad = jnp.concatenate([grad_gain, grad_shift, grad_bias_in, grad_bias_out])
    bias_out_grad = vector_grad[VEC - D:]
    vector_moment_new = MOMENTUM * vector_moment + vector_grad
    vector_step = -(0.2 / math.sqrt(TOKENS)) * vector_moment_new
    return (block_out, grad_hidden, grad_in, grad_back, moment_in_new, moment_back_new, step_in, step_back, vector_grad, vector_moment_new, vector_step, bias_out_grad)
```

```python
import functools
import math

import jax
import jax.numpy as jnp
from jax import lax
from jax.experimental import pallas as pl
from jax.experimental.pallas import tpu as pltpu
from jax.sharding import PartitionSpec as P

HEADS = 32
HEAD = 64
ROT = 32
FF = 8192
SEQ_MAX = 1024
NEG = -1e30
NS_A = 3.4445
NS_B = -4.775
NS_C = 2.0315
MOMENTUM = 0.95
F32 = jnp.float32
BF16 = jnp.bfloat16
CHUNK = 256
PANEL = 512
VMEM_BYTES = 61 * 2**20


def positions(segments):
    index_all = jnp.arange(segments.shape[0], dtype=jnp.int32)
    previous = jnp.concatenate([jnp.full((1,), -1, jnp.int32), segments[:-1]])
    starts = jnp.where(segments != previous, index_all, 0)
    return index_all - lax.cummax(starts, axis=0)


def gelu_tanh(values):
    inner = 0.7978845608028654 * (values + 0.044715 * values * values * values)
    return 0.5 * values * (1.0 + jnp.tanh(inner))


def rotary_lanes(position, heads):
    half_rot = ROT // 2
    freq = jnp.exp(jnp.arange(half_rot, dtype=F32) * (-2.0 * math.log(10000.0) / ROT))
    angle = position.astype(F32)[:, None] * freq[None, :]
    cos, sin = jnp.cos(angle), jnp.sin(angle)
    rest = (position.shape[0], HEAD - ROT)
    cos_head = jnp.concatenate([cos, cos, jnp.ones(rest, F32)], axis=1)
    sin_head = jnp.concatenate([-sin, sin, jnp.zeros(rest, F32)], axis=1)
    return jnp.tile(cos_head, (1, heads)), jnp.tile(sin_head, (1, heads))


def after(values, *others):
    return pl.pallas_call(
        lambda *refs: None,
        out_shape=jax.ShapeDtypeStruct(values.shape, values.dtype),
        in_specs=[pl.BlockSpec(memory_space=pl.ANY)] * (1 + len(others)),
        out_specs=pl.BlockSpec(memory_space=pl.ANY),
        input_output_aliases={0: 0},
        name="after",
    )(values, *others)


def rows_at(index, size):
    return pl.ds(pl.multiple_of(index * size, size), size)


def attention_body(
    first_ref, pre_ref, grad_ref, start_ref, cos_ref, sin_ref, att_ref, out_ref, q_s, k_s, v_s, dk_s, dv_s, o_s, dq_s
):
    pack_len, width = grad_ref.shape
    heads = width // HEAD
    blocks = pack_len // CHUNK
    lane = lax.broadcasted_iota(jnp.int32, (CHUNK, width), 1)
    low_half = lane % HEAD < ROT // 2
    head_of = lane // HEAD

    def turn(values, rows, sign):
        swapped = jnp.where(
            low_half, pltpu.roll(values, width - ROT // 2, 1), pltpu.roll(values, ROT // 2, 1)
        )
        return values * cos_ref[rows, :] + (sign * sin_ref[rows, :]) * swapped

    def prepare(block, carry):
        rows = rows_at(block, CHUNK)
        query = turn(pre_ref[rows, :width], rows, 1.0).astype(BF16)
        q_s[rows, :] = (query.astype(F32) * HEAD ** (-0.5)).astype(BF16)
        k_s[rows, :] = turn(pre_ref[rows, width : 2 * width], rows, 1.0).astype(BF16)
        v_s[rows, :] = pre_ref[rows, 2 * width :].astype(BF16)
        dk_s[rows, :] = jnp.zeros((CHUNK, width), F32)
        dv_s[rows, :] = jnp.zeros((CHUNK, width), F32)
        return carry

    lax.fori_loop(0, blocks, prepare, 0)
    over_last = (((1,), (1,)), ((), ()))
    over_first = (((0,), (0,)), ((), ()))

    def window(block, count):
        rows = rows_at(block, CHUNK)
        span = pl.ds(pl.multiple_of((block + 1 - count) * CHUNK, CHUNK), count * CHUNK)
        shape = (CHUNK, count * CHUNK)
        column = (block + 1 - count) * CHUNK + lax.broadcasted_iota(jnp.int32, shape, 1)
        row = block * CHUNK + lax.broadcasted_iota(jnp.int32, shape, 0)
        allowed = (column >= start_ref[rows, :]) & (column <= row)
        o_s[...] = jnp.zeros((CHUNK, width), F32)
        dq_s[...] = jnp.zeros((CHUNK, width), F32)

        def one_head(head, carry):
            mine = head_of == head
            query = jnp.where(mine, q_s[rows, :], jnp.zeros((), BF16))
            grad = jnp.where(mine, grad_ref[rows, :], jnp.zeros((), BF16))
            keys, values = k_s[span, :], v_s[span, :]
            scores = lax.dot_general(query, keys, over_last, preferred_element_type=F32)
            scores = jnp.where(allowed, scores, NEG)
            prob = jnp.exp(scores - jnp.max(scores, axis=1, keepdims=True))
            prob = prob * (1.0 / jnp.sum(prob, axis=1, keepdims=True))
            prob_low = prob.astype(BF16)
            grad_prob = lax.dot_general(grad, values, over_last, preferred_element_type=F32)
            delta = jnp.sum(prob * grad_prob, axis=1, keepdims=True)
            grad_scores = (prob * (grad_prob - delta)).astype(BF16)
            o_s[...] += jnp.where(mine, jnp.dot(prob_low, values, preferred_element_type=F32), 0.0)
            dq_s[...] += jnp.where(mine, jnp.dot(grad_scores, keys, preferred_element_type=F32), 0.0)
            dk_s[span, :] += lax.dot_general(
                grad_scores, query, over_first, preferred_element_type=F32
            )
            dv_s[span, :] += lax.dot_general(prob_low, grad, over_first, preferred_element_type=F32)
            return carry

        lax.fori_loop(0, heads, one_head, 0)
        att_ref[rows, :] = o_s[...].astype(BF16)
        out_ref[rows, :width] = turn(dq_s[...] * HEAD ** (-0.5), rows, -1.0).astype(BF16)

    def one_block(block, carry):
        used = block + 1 - first_ref[block]
        for count in range(1, min(blocks, -(-(SEQ_MAX - 1) // CHUNK) + 1) + 1):
            pl.when(used == count)(functools.partial(window, block, count))
        return carry

    lax.fori_loop(0, blocks, one_block, 0)

    def finish(block, carry):
        rows = rows_at(block, CHUNK)
        out_ref[rows, width : 2 * width] = turn(dk_s[rows, :], rows, -1.0).astype(BF16)
        out_ref[rows, 2 * width :] = dv_s[rows, :].astype(BF16)
        return carry

    lax.fori_loop(0, blocks, finish, 0)


def attention(pre_qkv, grad_attended, position, part, width):
    pack_len = grad_attended.shape[0]
    start = jnp.arange(pack_len, dtype=jnp.int32) - position
    first = start[::CHUNK] // CHUNK
    cos_tab, sin_tab = rotary_lanes(position, width // HEAD)
    whole = pl.BlockSpec(memory_space=pltpu.VMEM)
    pairs = pack_len * SEQ_MAX * (width // HEAD)
    return pl.pallas_call(
        attention_body,
        grid=(1,),
        out_shape=(
            jax.ShapeDtypeStruct((pack_len, width), BF16),
            jax.ShapeDtypeStruct((pack_len, 3 * width), BF16),
        ),
        in_specs=[
            pl.BlockSpec(memory_space=pltpu.SMEM),
            pl.BlockSpec((pack_len, 3 * width), lambda step: (0, part), memory_space=pltpu.VMEM),
            pl.BlockSpec((pack_len, width), lambda step: (0, part), memory_space=pltpu.VMEM),
            whole,
            whole,
            whole,
        ],
        out_specs=(whole, whole),
        scratch_shapes=[pltpu.VMEM((pack_len, width), BF16)] * 3
        + [pltpu.VMEM((pack_len, width), F32)] * 2
        + [pltpu.VMEM((CHUNK, width), F32)] * 2,
        compiler_params=pltpu.CompilerParams(vmem_limit_bytes=VMEM_BYTES),
        cost_estimate=pl.CostEstimate(
            flops=pairs * 10 * HEAD * 4, bytes_accessed=16 * pack_len * width, transcendentals=pairs
        ),
        name="attention",
    )(first, pre_qkv, grad_attended, start[:, None], cos_tab, sin_tab)


def tri(index):
    return index * (index + 1) // 2


def packed_rows(size):
    return tri(size // CHUNK) * CHUNK


def panels(size):
    for panel in range(size // PANEL):
        yield panel, (panel + 1) * PANEL, slice(panel * PANEL, (panel + 1) * PANEL)


def symmetric(lhs, rhs, size, epilogue):
    for panel, height, columns in panels(size):
        epilogue(
            panel, height, columns, jnp.dot(lhs[:height, :], rhs[:, columns], preferred_element_type=F32)
        )


def put_mirrored(ref, height, columns, values):
    ref[:height, columns] = values
    if height > PANEL:
        ref[columns, : height - PANEL] = values[: height - PANEL, :].T


def gram_packed(x, xt_ref, size, packed_ref):
    depth = x.shape[0]
    for block in range(depth // CHUNK):
        part = slice(block * CHUNK, (block + 1) * CHUNK)
        xt_ref[:, part] = x[part, :].T
    for panel, height, columns in panels(size):
        product = jnp.dot(xt_ref[:height, :depth], x[:, columns], preferred_element_type=F32).astype(BF16)
        for half in range(PANEL // CHUNK):
            column = panel * (PANEL // CHUNK) + half
            rows = (column + 1) * CHUNK
            packed_ref[tri(column) * CHUNK : tri(column) * CHUNK + rows, :] = product[
                :rows, half * CHUNK : (half + 1) * CHUNK
            ]


def gram_body(x_ref, before_ref, packed_ref, xt_s):
    gram_packed(x_ref, xt_s, x_ref.shape[1], packed_ref)


def unpack(packed_ref, size, scale, exact_s, low_s):
    per_panel = PANEL // CHUNK
    for column in range(size // CHUNK):
        rows = (column + 1) * CHUNK
        at = tri(column) * CHUNK
        panel, half = column // per_panel, column % per_panel
        base = tri(panel) * PANEL
        lanes = slice(half * CHUNK, (half + 1) * CHUNK)
        cols = slice(column * CHUNK, (column + 1) * CHUNK)
        values = packed_ref[at : at + rows, :].astype(F32) * scale
        exact_s[base : base + rows, lanes] = values
        low = values.astype(BF16)
        low_s[:rows, cols] = low
        if column:
            low_s[cols, : rows - CHUNK] = low[: rows - CHUNK, :].T
        for other in range(half):
            left = panel * per_panel + other
            exact_s[base + column * CHUNK : base + rows, other * CHUNK : (other + 1) * CHUNK] = values[
                left * CHUNK : (left + 1) * CHUNK, :
            ].T


def iterate(x_s, exact_s, low_s, poly_s, mix_s, size, count):
    def one(step, carry):
        source, target = step % 2, (step + 1) % 2

        def poly_end(panel, height, columns, product):
            at = tri(panel) * PANEL
            values = NS_B * exact_s[at : at + height, :] + NS_C * product
            put_mirrored(poly_s, height, columns, values.astype(BF16))

        symmetric(low_s, low_s, size, poly_end)

        def x_columns(panel, inner):
            columns = rows_at(panel, PANEL)
            product = jnp.dot(x_s[source], poly_s[:, columns], preferred_element_type=F32)
            x_s[target, :, columns] = (NS_A * x_s[source, :, columns].astype(F32) + product).astype(BF16)
            return inner

        lax.fori_loop(0, size // PANEL, x_columns, 0)

        @pl.when(step < count - 1)
        def next_gram():
            def mix_end(panel, height, columns, product):
                at = tri(panel) * PANEL
                exact_s[at : at + height, :] = (NS_A * NS_A) * exact_s[at : at + height, :] + (
                    2.0 * NS_A
                ) * product
                put_mirrored(mix_s, height, columns, product.astype(BF16))

            symmetric(low_s, poly_s, size, mix_end)

            def gram_end(panel, height, columns, product):
                at = tri(panel) * PANEL
                values = exact_s[at : at + height, :] + product
                exact_s[at : at + height, :] = values
                put_mirrored(low_s, height, columns, values.astype(BF16))

            symmetric(mix_s, poly_s, size, gram_end)

        return carry

    lax.fori_loop(0, count, one, 0)


def first_body(count, packed_ref, x_ref, x_out, packed_out, x_s, exact_s, low_s, poly_s, mix_s, packed_s, sems):
    size = x_ref.shape[1]
    load_x = pltpu.make_async_copy(x_ref, x_s.at[0], sems.at[0])
    load_packed = pltpu.make_async_copy(packed_ref, packed_s, sems.at[1])
    load_x.start()
    load_packed.start()
    load_packed.wait()
    trace = jnp.zeros((1, 1), F32)
    eye = lax.broadcasted_iota(jnp.int32, (CHUNK, CHUNK), 0) == lax.broadcasted_iota(
        jnp.int32, (CHUNK, CHUNK), 1
    )
    for column in range(size // CHUNK):
        at = tri(column) * CHUNK + column * CHUNK
        block = jnp.where(eye, packed_s[at : at + CHUNK, :].astype(F32), 0.0)
        trace = trace + jnp.sum(jnp.sum(block, axis=1, keepdims=True), axis=0, keepdims=True)
    inverse = 1.0 / (jnp.sqrt(trace) + 1e-7)
    unpack(packed_s, size, inverse * inverse, exact_s, low_s)
    load_x.wait()
    iterate(x_s, exact_s, low_s, poly_s, mix_s, size, count)
    depth = x_ref.shape[0]

    def scale_rows(block, carry):
        rows = rows_at(block, CHUNK)
        x_s[count % 2, rows, :] = (x_s[count % 2, rows, :].astype(F32) * inverse).astype(BF16)
        return carry

    lax.fori_loop(0, depth // CHUNK, scale_rows, 0)
    store_x = pltpu.make_async_copy(x_s.at[count % 2], x_out, sems.at[0])
    store_x.start()
    gram_packed(x_s.at[count % 2], poly_s, size, packed_s)
    store_packed = pltpu.make_async_copy(packed_s, packed_out, sems.at[1])
    store_packed.start()
    store_x.wait()
    store_packed.wait()


def second_body(count, packed_ref, x_ref, x_out, x_s, exact_s, low_s, poly_s, mix_s, packed_s, sems):
    size = x_ref.shape[1]
    load_x = pltpu.make_async_copy(x_ref, x_s.at[0], sems.at[0])
    load_packed = pltpu.make_async_copy(packed_ref, packed_s, sems.at[1])
    load_x.start()
    load_packed.start()
    load_packed.wait()
    unpack(packed_s, size, 1.0, exact_s, low_s)
    load_x.wait()
    iterate(x_s, exact_s, low_s, poly_s, mix_s, size, count)
    store_x = pltpu.make_async_copy(x_s.at[count % 2], x_out, sems.at[0])
    store_x.start()
    store_x.wait()


def ns_scratch(depth, size):
    return [
        pltpu.VMEM((2, depth, size), BF16),
        pltpu.VMEM((tri(size // PANEL) * PANEL, PANEL), F32),
        pltpu.VMEM((size, size), BF16),
        pltpu.VMEM((size, size), BF16),
        pltpu.VMEM((size, size), BF16),
        pltpu.VMEM((packed_rows(size), CHUNK), BF16),
        pltpu.SemaphoreType.DMA((2,)),
    ]


def orthogonalize(rows, before, before_sum, beside_first, beside_last):
    depth, size = rows.shape
    group_count = lax.axis_size("group")
    packed_shape = jax.ShapeDtypeStruct((packed_rows(size), CHUNK), BF16)
    x_shape = jax.ShapeDtypeStruct((depth, size), BF16)
    vmem = pl.BlockSpec(memory_space=pltpu.VMEM)
    hbm = pl.BlockSpec(memory_space=pl.ANY)
    params = pltpu.CompilerParams(vmem_limit_bytes=VMEM_BYTES)

    def cost(products, x_steps):
        return pl.CostEstimate(
            flops=products * size**3 * 5 // 4 + x_steps * 2 * depth * size * size,
            bytes_accessed=size * size * 4,
            transcendentals=0,
        )

    def summed(packed):
        part = lax.psum_scatter(packed, "group", scatter_dimension=0, tiled=True)
        return lax.all_gather(part, "group", axis=0, tiled=True)

    packed = pl.pallas_call(
        gram_body,
        out_shape=packed_shape,
        in_specs=[vmem, hbm],
        out_specs=vmem,
        scratch_shapes=[pltpu.VMEM((size, depth), BF16)],
        compiler_params=params,
        cost_estimate=cost(0, 1),
        name="gram",
    )(rows, before)
    gathered = summed(after(packed, before_sum))
    first_result = beside_first(gathered)
    half_way, packed = pl.pallas_call(
        functools.partial(first_body, 2),
        out_shape=(x_shape, packed_shape),
        in_specs=[hbm, hbm],
        out_specs=(hbm, hbm),
        scratch_shapes=ns_scratch(depth, size),
        compiler_params=params,
        cost_estimate=cost(4, 3),
        name="first_steps",
    )(gathered, rows)
    gathered = summed(after(packed, first_result))
    last_result = beside_last(first_result, gathered)
    result = pl.pallas_call(
        functools.partial(second_body, 3),
        out_shape=x_shape,
        in_specs=[hbm, hbm],
        out_specs=hbm,
        scratch_shapes=ns_scratch(depth, size),
        compiler_params=params,
        cost_estimate=cost(7, 3),
        name="last_steps",
    )(gathered, half_way)
    return result, last_result


def flip(bit):
    return [(index, index ^ bit) for index in range(4)]


def send(values, bit):
    return lax.ppermute(values, "dp", flip(bit))


def two_by_two():
    return lax.axis_size("dp") == 4


def by_distance(parts):
    if not two_by_two():
        return parts
    me = lax.axis_index("dp")
    return jnp.stack([lax.dynamic_index_in_dim(parts, me ^ r, 0, keepdims=False) for r in range(4)])


def gather_near(own):
    if not two_by_two():
        return lax.all_gather(own, "dp", axis=0, tiled=False)
    return own, send(own, 1), send(own, 2)


def gather_far(near):
    if not two_by_two():
        return near
    own, from_x, from_y = near
    half = own.shape[0] // 2
    first, second = send(from_y[:half], 1), send(from_x[half:], 2)
    return jnp.stack([own, from_x, from_y, jnp.concatenate([first, second], axis=0)])


def came(near):
    return near[1:] if two_by_two() else (near,)


def gather_dp(own):
    return gather_far(gather_near(own))


def scatter_start(parts):
    if not two_by_two():
        return lax.psum_scatter(parts, "dp", scatter_dimension=0, tiled=False).astype(F32)
    half = parts.shape[1] // 2
    terms = parts.reshape(2, 2, parts.shape[1], parts.shape[2])
    left, right = terms[:, :, :half], terms[:, :, half:]
    return terms, send(left[:, 1], 1), send(right[1], 2)


def scatter_next(state, *others):
    if not two_by_two():
        return state
    terms, left_in, right_in = state
    half = terms.shape[2] // 2
    terms = after(terms, *others)
    left, right = terms[:, 0, :half], terms[0, :, half:]
    left_sum = left.astype(F32) + left_in.astype(F32)
    right_sum = right.astype(F32) + right_in.astype(F32)
    return left_sum[0], left_sum[1].astype(BF16), right_sum[0], right_sum[1].astype(BF16)


def scatter_end(state, *others):
    if not two_by_two():
        return state
    left, left_out, right, right_out = state
    left_in, right_in = send(left_out, 2), send(right_out, 1)
    if others:
        left = after(left, *others)
    return jnp.concatenate([left + left_in.astype(F32), right + right_in.astype(F32)], axis=0)


def flying(state):
    return state[1::2] if two_by_two() else (state,)


def owners_start(slots, owners):
    me = lax.axis_index("dp")
    half = slots.shape[1] // 2

    def slot_for(distance):
        picked = slots[0]
        for k, owner in enumerate(owners[1:], 1):
            picked = jnp.where((me ^ distance) == owner, slots[k], picked)
        return picked

    far = slot_for(3)
    first_hop = hop(far[:half], 1, [t ^ 2 for t in owners])
    second_hop = hop(far[half:], 2, [t ^ 1 for t in owners])
    return slot_for(0), hop(slot_for(1), 1, owners), hop(slot_for(2), 2, owners), first_hop, second_hop


def owners_end(state, owners, *others):
    own, from_x, from_y, first_hop, second_hop = state
    if others:
        first_hop = after(first_hop, *others)
    first, second = hop(first_hop, 2, owners), hop(second_hop, 1, owners)
    return jnp.stack([own, from_x, from_y, jnp.concatenate([first, second], axis=0)])


def hop(values, bit, targets):
    return lax.ppermute(values, "dp", [(t ^ bit, t) for t in targets])


def exchange_dp(slots):
    if not two_by_two():
        return lax.all_to_all(slots, "dp", split_axis=0, concat_axis=0, tiled=True)
    half = slots.shape[1] // 2
    first_hop, second_hop = send(slots[3, :half], 1), send(slots[3, half:], 2)
    from_x, from_y = send(slots[1], 1), send(slots[2], 2)
    first, second = send(first_hop, 2), send(second_hop, 1)
    return jnp.stack([slots[0], from_x, from_y, jnp.concatenate([first, second], axis=0)])


def heads_aligned(unit):
    return unit == HEAD and lax.axis_size("group") % 3 != 0


def spread_qkv(own, unit):
    group_count = lax.axis_size("group")
    me = lax.axis_index("group")
    moved = jnp.stack(
        [
            lax.ppermute(
                own[j * unit : (j + 1) * unit], "group", [(g, (3 * g + j) % group_count) for g in range(group_count)]
            )
            for j in range(3)
        ]
    )
    return jnp.concatenate(
        [lax.dynamic_index_in_dim(moved, (me + group_count * i) % 3, 0, keepdims=False) for i in range(3)]
    )


def return_qkv(rows, unit):
    group_count = lax.axis_size("group")
    me = lax.axis_index("group")
    inverse = pow(group_count, -1, 3)
    parts = rows.reshape(3, unit, rows.shape[1])
    return jnp.concatenate(
        [
            lax.ppermute(
                lax.dynamic_index_in_dim(parts, ((j - me) * inverse) % 3, 0, keepdims=False),
                "group",
                [((3 * g + j) % group_count, g) for g in range(group_count)],
            )
            for j in range(3)
        ]
    )


def head_rows(matrix, heads):
    group_count = lax.axis_size("group")
    lead = matrix.shape[:-2]
    split = matrix.reshape(lead + (heads, group_count, HEAD, matrix.shape[-1]))
    picked = lax.dynamic_index_in_dim(split, lax.axis_index("group"), len(lead) + 1, keepdims=False)
    return picked.reshape(lead + (heads * HEAD, matrix.shape[-1]))


def spread_heads(rows, heads):
    group_count = lax.axis_size("group")
    lead = rows.shape[:-2]
    width = rows.shape[-1]
    part = rows.reshape(lead + (heads, 1, HEAD, width))
    empty = jnp.zeros(lead + (heads, group_count, HEAD, width), rows.dtype)
    placed = lax.dynamic_update_slice_in_dim(empty, part, lax.axis_index("group"), len(lead) + 1)
    return placed.reshape(lead + (heads * group_count * HEAD, width))


def shards(
    hidden_in,
    cotangent,
    segment_ids,
    weight_in,
    weight_back,
    moment_in,
    moment_back,
    norm_gain,
    norm_shift,
    bias_in,
    bias_out,
    vector_moment,
):
    model_width = hidden_in.shape[2]
    tokens = hidden_in.shape[1]
    data_count = lax.axis_size("dp")
    group_count = lax.axis_size("group")
    devices = data_count * group_count
    me_group = lax.axis_index("group")
    unit = model_width // devices
    qkv_rows = 3 * unit
    ff_rows = FF // devices
    out_rows = unit
    heads = HEADS // group_count
    width = heads * HEAD
    aligned = heads_aligned(unit)
    everywhere = ("dp", "group")

    def dot(left, right):
        return jnp.dot(left, right, preferred_element_type=F32)

    def dot_last(left, right):
        return lax.dot_general(left, right, (((1,), (1,)), ((), ())), preferred_element_type=F32)

    def dot_first(left, right):
        return lax.dot_general(left, right, (((0,), (0,)), ((), ())), preferred_element_type=F32)

    x_float = hidden_in[0].astype(F32)
    centre = x_float - jnp.mean(x_float, axis=-1, keepdims=True)
    inverse_std = lax.rsqrt(jnp.mean(centre * centre, axis=-1, keepdims=True) + 1e-05)
    x_hat = centre * inverse_std
    normed_low = (x_hat * norm_gain + norm_shift).astype(BF16)
    grad_y = cotangent[0]
    parts = max(1, width // 128)
    lanes = width // parts
    normed_all = lax.all_gather(normed_low, "group", axis=0, tiled=True)
    w_in, w_back = weight_in[0], weight_back[0]
    w_up = gather_dp(w_in[qkv_rows:])
    if aligned:
        near_qkv = gather_near(spread_qkv(w_in[:qkv_rows], unit))
        grad_all = lax.all_gather(after(grad_y, normed_all, w_up, *came(near_qkv)), "group", axis=0, tiled=True)
        w_qkv = by_distance(gather_far(near_qkv))
        all_back = gather_dp(after(w_back, *came(near_qkv)))
        w_out = by_distance(all_back[:, :out_rows]).reshape(width, model_width)
        w_down = all_back[:, out_rows:].reshape(data_count * ff_rows, model_width)
    else:
        grad_all = lax.all_gather(grad_y, "group", axis=0, tiled=True)
        all_qkv = lax.all_gather(w_in[:qkv_rows], everywhere, axis=0, tiled=True)
        w_qkv = head_rows(all_qkv.reshape(3, model_width, model_width), heads)
        w_out = head_rows(lax.all_gather(w_back[:out_rows], everywhere, axis=0, tiled=True), heads)
        w_down = gather_dp(w_back[out_rows:]).reshape(data_count * ff_rows, model_width)
    w_up = w_up.reshape(data_count * ff_rows, model_width)

    def to_parts(rows):
        split = rows.reshape((3, parts, lanes) + rows.shape[1:])
        return jnp.swapaxes(split, 0, 1).reshape(rows.shape)

    def from_parts(rows):
        split = rows.reshape((parts, 3, lanes) + rows.shape[1:])
        return jnp.swapaxes(split, 0, 1).reshape(rows.shape)

    w_qkv = to_parts(w_qkv.reshape(3 * width, model_width))

    bias_up = lax.dynamic_index_in_dim(
        bias_in[3 * model_width :].reshape(data_count, group_count, ff_rows), me_group, 1, keepdims=False
    )
    bias_up = by_distance(bias_up).reshape(data_count * ff_rows)
    bias_qkv = bias_in[: 3 * model_width].reshape(3 * heads, group_count, HEAD)
    bias_qkv = to_parts(lax.dynamic_index_in_dim(bias_qkv, me_group, 1, keepdims=False).reshape(3 * width))
    pre_up = dot_last(normed_all, w_up) + bias_up
    pre_qkv = dot_last(normed_all, w_qkv) + bias_qkv
    activated, gelu_pull = jax.vjp(gelu_tanh, pre_up)
    activated = activated.astype(BF16)
    grad_all = after(grad_all, activated, pre_qkv)

    term_down = dot_first(activated, grad_all).astype(BF16)
    sum_down = scatter_start(term_down.reshape(data_count, ff_rows, model_width))
    grad_pre_up = gelu_pull(dot_last(grad_all, after(w_down, term_down)))[0].astype(BF16)
    term_up = dot_first(grad_pre_up, normed_all).astype(BF16)
    sum_up = scatter_start(term_up.reshape(data_count, ff_rows, model_width))
    grad_attended = dot_last(grad_all, after(w_out, term_up)).astype(BF16)
    sum_down = scatter_next(sum_down, grad_attended)
    grad_w_down = scatter_end(sum_down)

    position = positions(segment_ids[0])
    attended, grad_pre_qkv = [], []
    ready = flying(sum_down)
    for part in range(parts):
        one, one_grad = attention(pre_qkv, after(grad_attended, *ready), position, part, lanes)
        attended.append(one)
        grad_pre_qkv.append(one_grad)
        if part == 0:
            sum_up = scatter_next(sum_up, one)
            ready = flying(sum_up)
        else:
            ready = (one,)
    grad_w_up = scatter_end(sum_up, attended[-1])
    attended = jnp.concatenate(attended, axis=1)
    grad_pre_qkv = jnp.concatenate(grad_pre_qkv, axis=1)

    def slot(rows):
        return jnp.pad(rows.astype(BF16), ((0, ff_rows - rows.shape[0]), (0, 0)))

    moment_up = MOMENTUM * moment_in[0, qkv_rows:] + grad_w_up
    moment_down = MOMENTUM * moment_back[0, out_rows:] + grad_w_down
    early = jnp.stack([slot(moment_up), slot(moment_down)])
    if two_by_two():
        early = owners_start(early, [1, 3])
        term_grad = after(grad_pre_qkv, *early)
    else:
        term_grad = grad_pre_qkv

    term_qkv = from_parts(dot_first(term_grad, normed_all).astype(BF16))
    term_out = dot_first(attended, grad_all).astype(BF16)
    if aligned:
        term_att = by_distance(
            jnp.concatenate(
                [
                    term_qkv.reshape(data_count, qkv_rows, model_width),
                    term_out.reshape(data_count, out_rows, model_width),
                ],
                axis=1,
            )
        )
        sum_att = scatter_start(term_att)
    else:
        term_att = term_qkv

    branch_part = (dot(after(attended, term_att), w_out) + dot(activated, w_down)).astype(BF16)
    branch = lax.psum_scatter(branch_part, "group", scatter_dimension=0, tiled=True)
    block_out = (x_float + branch.astype(F32) + bias_out).astype(BF16)
    if two_by_two():
        early = owners_end(early, [1, 3], branch_part)
    if aligned:
        sum_att = scatter_next(sum_att, branch_part)
        normed_part = dot(after(grad_pre_qkv, *flying(sum_att)), w_qkv)
        own_att = scatter_end(sum_att, normed_part)
        grad_w_qkv = own_att[:qkv_rows].astype(BF16)
        normed_part = (normed_part + dot(after(grad_pre_up, grad_w_qkv), w_up)).astype(BF16)
        grad_w_qkv = return_qkv(grad_w_qkv, unit).astype(F32)
        grad_w_out = own_att[qkv_rows:]
    else:
        normed_part = (dot(after(grad_pre_qkv, branch_part), w_qkv) + dot(grad_pre_up, w_up)).astype(BF16)
        grad_w_qkv = lax.psum_scatter(
            spread_heads(term_qkv.reshape(3, width, model_width), heads).reshape(3 * model_width, model_width),
            everywhere,
            scatter_dimension=0,
            tiled=True,
        ).astype(F32)
        grad_w_out = lax.psum_scatter(
            spread_heads(term_out, heads), everywhere, scatter_dimension=0, tiled=True
        ).astype(F32)
    grad_y_float = grad_y.astype(F32)

    grad_in = jnp.concatenate([grad_w_qkv, grad_w_up], axis=0)[None]
    grad_back = jnp.concatenate([grad_w_out, grad_w_down], axis=0)[None]
    moment_in_new = MOMENTUM * moment_in + grad_in
    moment_back_new = MOMENTUM * moment_back + grad_back
    moment_qkv = MOMENTUM * moment_in[0, :qkv_rows] + grad_w_qkv
    moment_out = MOMENTUM * moment_back[0, :out_rows] + grad_w_out
    if two_by_two():
        late = jnp.stack([moment_qkv.astype(BF16), jnp.pad(moment_out.astype(BF16), ((0, qkv_rows - out_rows), (0, 0)))])
        late = owners_end(owners_start(late, [0, 2]), [0, 2])
        late = jnp.pad(late, ((0, 0), (0, ff_rows - qkv_rows), (0, 0)))
        owned = jnp.where(lax.axis_index("dp") % 2 == 1, early, late)
    else:
        slots = [slot(moment_qkv), early[0], slot(moment_out), early[1]]
        slots = slots + [jnp.zeros_like(early[0])] * (data_count - 4)
        owned = exchange_dp(jnp.stack(slots))

    def sum_normed(gathered):
        return lax.psum_scatter(after(normed_part, gathered), "group", scatter_dimension=0, tiled=True)

    def placed(sums, lead, size):
        empty = jnp.zeros((lead, group_count, size), F32)
        return lax.dynamic_update_slice_in_dim(empty, sums.reshape(lead, 1, size), me_group, 1).reshape(-1)

    def sum_vectors(grad_normed, gathered):
        grad_normed = grad_normed.astype(F32)
        sums_up = jnp.sum(grad_pre_up.astype(F32), axis=0).reshape(data_count, ff_rows)
        vector_local = jnp.concatenate(
            [
                jnp.sum(grad_normed * x_hat, axis=0),
                jnp.sum(grad_normed, axis=0),
                placed(from_parts(jnp.sum(grad_pre_qkv.astype(F32), axis=0)), 3 * heads, HEAD),
                placed(by_distance(sums_up), data_count, ff_rows),
                jnp.sum(grad_y_float, axis=0),
            ]
        )
        return grad_normed, lax.psum(after(vector_local, gathered), everywhere)

    result, (grad_normed, vector_grad) = orthogonalize(
        owned.reshape(data_count * ff_rows, model_width), normed_part, branch, sum_normed, sum_vectors
    )
    result = after(result, vector_grad)
    returned = by_distance(exchange_dp(result.reshape(data_count, ff_rows, model_width)))

    grad_x_hat = grad_normed * norm_gain
    grad_hidden = grad_y_float + inverse_std * (
        grad_x_hat
        - jnp.mean(grad_x_hat, axis=-1, keepdims=True)
        - x_hat * jnp.mean(grad_x_hat * x_hat, axis=-1, keepdims=True)
    )

    def matrix_rows(matrix_index, row_count, scale):
        return -scale * returned[matrix_index, :row_count].astype(F32)

    scale_ff = math.sqrt(1.0 * FF)
    step_in = jnp.concatenate(
        [matrix_rows(0, qkv_rows, math.sqrt(3.0 * model_width)), matrix_rows(1, ff_rows, scale_ff)], axis=0
    )[None]
    step_back = jnp.concatenate(
        [matrix_rows(2, out_rows, math.sqrt(1.0 * model_width)), matrix_rows(3, ff_rows, scale_ff)], axis=0
    )[None]
    bias_out_grad = vector_grad[vector_grad.shape[0] - model_width :]
    vector_moment_new = MOMENTUM * vector_moment + vector_grad
    vector_step = -(0.2 / math.sqrt(tokens * devices)) * vector_moment_new
    return (
        block_out[None],
        grad_hidden[None],
        grad_in,
        grad_back,
        moment_in_new,
        moment_back_new,
        step_in,
        step_back,
        vector_grad,
        vector_moment_new,
        vector_step,
        bias_out_grad,
    )


def solution(mesh):
    tokens_spec = P("dp", "group", None)
    blocks_spec = P(("dp", "group"), None, None)
    in_specs = (
        (tokens_spec, tokens_spec, P("dp", None))
        + (blocks_spec,) * 4
        + (P(),) * 5
    )
    out_specs = (tokens_spec, tokens_spec) + (blocks_spec,) * 6 + (P(),) * 4
    return jax.shard_map(shards, mesh=mesh, in_specs=in_specs, out_specs=out_specs, check_vma=False)
```

```python
import functools
import math

import jax
import jax.numpy as jnp
from jax import lax
from jax.experimental import pallas as pl
from jax.experimental.pallas import tpu as pltpu
from jax.sharding import PartitionSpec as P

HEADS = 32
HEAD = 64
ROT = 32
FF = 8192
SEQ_MAX = 1024
NEG = -1e30
NS_A = 3.4445
NS_B = -4.775
NS_C = 2.0315
MOMENTUM = 0.95
F32 = jnp.float32
BF16 = jnp.bfloat16
CHUNK = 256
PANEL = 512
VMEM_BYTES = 61 * 2**20
MATMUL_BYTES = 60 * 2**20


def positions(segments):
    index_all = jnp.arange(segments.shape[0], dtype=jnp.int32)
    previous = jnp.concatenate([jnp.full((1,), -1, jnp.int32), segments[:-1]])
    starts = jnp.where(segments != previous, index_all, 0)
    return index_all - lax.cummax(starts, axis=0)


def gelu_and_slope(values):
    square = values * values
    bent = jnp.tanh(0.7978845608028654 * (values + 0.044715 * values * square))
    inner_slope = 0.7978845608028654 * (1.0 + 3.0 * 0.044715 * square)
    half = 0.5 * (1.0 + bent)
    return values * half, half + 0.5 * values * (1.0 - bent * bent) * inner_slope


def rotary_lanes(position, heads):
    half_rot = ROT // 2
    freq = jnp.exp(jnp.arange(half_rot, dtype=F32) * (-2.0 * math.log(10000.0) / ROT))
    angle = position.astype(F32)[:, None] * freq[None, :]
    cos, sin = jnp.cos(angle), jnp.sin(angle)
    rest = (position.shape[0], HEAD - ROT)
    cos_head = jnp.concatenate([cos, cos, jnp.ones(rest, F32)], axis=1)
    sin_head = jnp.concatenate([-sin, sin, jnp.zeros(rest, F32)], axis=1)
    return jnp.tile(cos_head, (1, heads)), jnp.tile(sin_head, (1, heads))


def after(values, *others):
    return pl.pallas_call(
        lambda *refs: None,
        out_shape=jax.ShapeDtypeStruct(values.shape, values.dtype),
        in_specs=[pl.BlockSpec(memory_space=pl.ANY)] * (1 + len(others)),
        out_specs=pl.BlockSpec(memory_space=pl.ANY),
        input_output_aliases={0: 0},
        name="after",
    )(values, *others)


def over(left, right, axes):
    return lax.dot_general(left, right, (axes, ((), ())), preferred_element_type=F32)


NOTHING = pl.CostEstimate(flops=0, bytes_accessed=0, transcendentals=0)
ROWS = ((1,), (1,))
TOKENS = ((0,), (0,))


def by_rows(body, blocked, whole, outs, rows, name):
    steps = blocked[0].shape[0] // rows
    return pl.pallas_call(
        body,
        grid=(steps,),
        in_specs=[pl.BlockSpec((rows, one.shape[1]), lambda step: (step, 0)) for one in blocked]
        + [
            pl.BlockSpec(one.shape, lambda step, rank=one.ndim: (0,) * rank, pipeline_mode=pl.Buffered(1))
            for one in whole
        ],
        out_specs=tuple(pl.BlockSpec((rows, width), lambda step: (step, 0)) for width, _ in outs),
        out_shape=tuple(jax.ShapeDtypeStruct((steps * rows, width), dtype) for width, dtype in outs),
        compiler_params=pltpu.CompilerParams(vmem_limit_bytes=MATMUL_BYTES),
        cost_estimate=NOTHING,
        name=name,
    )(*blocked, *whole)


def by_columns(body, whole, blocked, outs, columns, name, scratch=(), scalar=None):
    steps = blocked[0].shape[1] // columns
    return pl.pallas_call(
        body,
        grid=(steps,),
        in_specs=([] if scalar is None else [pl.BlockSpec(memory_space=pltpu.SMEM)])
        + [pl.BlockSpec(one.shape, lambda step: (0, 0), pipeline_mode=pl.Buffered(1)) for one in whole]
        + [pl.BlockSpec((one.shape[0], columns), lambda step: (0, step)) for one in blocked],
        out_specs=tuple(pl.BlockSpec((rows, columns), lambda step: (0, step)) for rows, _ in outs),
        out_shape=tuple(jax.ShapeDtypeStruct((rows, steps * columns), dtype) for rows, dtype in outs),
        scratch_shapes=list(scratch),
        compiler_params=pltpu.CompilerParams(vmem_limit_bytes=MATMUL_BYTES),
        cost_estimate=NOTHING,
        name=name,
    )(*([] if scalar is None else [scalar]), *whole, *blocked)


def in_vmem(body, ins, others, outs, name, scalar=None):
    vmem = pl.BlockSpec(memory_space=pltpu.VMEM)
    first = [] if scalar is None else [pl.BlockSpec(memory_space=pltpu.SMEM)]
    return pl.pallas_call(
        body,
        in_specs=first + [vmem] * len(ins) + [pl.BlockSpec(memory_space=pl.ANY)] * len(others),
        out_specs=[vmem] * len(outs),
        out_shape=[jax.ShapeDtypeStruct(shape, dtype) for shape, dtype in outs],
        compiler_params=pltpu.CompilerParams(vmem_limit_bytes=MATMUL_BYTES),
        cost_estimate=NOTHING,
        name=name,
    )(*([] if scalar is None else [scalar]), *ins, *others)


def up_forward(normed, w_up, bias):
    def body(x_ref, w_ref, b_ref, act_ref, slope_ref):
        act, slope = gelu_and_slope(over(x_ref[...], w_ref[...], ROWS) + b_ref[...])
        act_ref[...] = act.astype(BF16)
        slope_ref[...] = slope.astype(BF16)

    units = w_up.shape[0]
    return by_rows(body, [normed], [w_up, bias[None]], [(units, BF16), (units, BF16)], 256, "up_forward")


def up_backward(grad, slope, w_down):
    def body(g_ref, s_ref, w_ref, out_ref):
        out_ref[...] = (over(g_ref[...], w_ref[...], ROWS) * s_ref[...].astype(F32)).astype(BF16)

    return by_rows(body, [grad, slope], [w_down], [(w_down.shape[0], BF16)], 512, "up_backward")[0]


def project(x, w, bias, dtype, name):
    def body(x_ref, w_ref, b_ref, out_ref):
        out_ref[...] = (over(x_ref[...], w_ref[...], ROWS) + b_ref[...]).astype(dtype)

    return by_rows(body, [x], [w, bias[None]], [(w.shape[0], dtype)], 512, name)[0]


def weight_grad(left, right, name, split=False):
    tokens, rows = left.shape
    quarter = rows // 8 if split else rows

    def body(l_ref, r_ref, *refs):
        t_s = refs[-1]

        @pl.when(pl.program_id(0) == 0)
        def turn_over():
            for block in range(0, tokens, 256):
                t_s[:, block : block + 256] = l_ref[block : block + 256, :].T

        product = jnp.dot(t_s[...], r_ref[...], preferred_element_type=F32).astype(BF16)
        if not split:
            refs[0][...] = product
            return
        for block in range(4):
            for half in range(2):
                y, x = block // 2, block % 2
                sent, at = (x, y) if half == 0 else (y, x)
                source = (2 * block + half) * quarter
                refs[2 * half + 1 - sent][at * quarter : (at + 1) * quarter, :] = product[source : source + quarter, :]

    scratch = [pltpu.VMEM((rows, tokens), BF16)]
    outs = [(2 * quarter, BF16)] * 4 if split else [(rows, BF16)]
    results = by_columns(body, [left], [right], outs, 512, name, scratch)
    return results if split else results[0]


def weight_grads_plus(left, right, other_left, other_right, moment, other_moment, part, heads):
    tokens = left.shape[0]
    rows, other_rows = left.shape[1], other_left.shape[1]
    half, other_half = rows // 2, other_rows // 2
    per_part = other_rows // HEAD
    me = lax.axis_index("dp").astype(jnp.int32).reshape(1)

    def body(
        me_ref, l_ref, o_ref, r_ref, q_ref, m_ref, n_ref, out_ref, other_ref, sent_x, kept_x, sent_y, kept_y, t_s, f_s, g_s
    ):
        @pl.when(pl.program_id(0) == 0)
        def turn_over():
            for block in range(0, tokens, 256):
                t_s[:rows, block : block + 256] = l_ref[block : block + 256, :].T
                t_s[rows:, block : block + 256] = o_ref[block : block + 256, :].T

        f_s[...] = jnp.dot(t_s[:rows, :], r_ref[...], preferred_element_type=F32)
        out_ref[...] = f_s[...].astype(BF16)
        g_s[...] = jnp.dot(t_s[rows:, :], q_ref[...], preferred_element_type=F32)
        other_ref[...] = g_s[...].astype(BF16)
        for i in range(3):
            chunk = 3 * me_ref[0] + i
            kind, head = chunk // heads, chunk % heads

            @pl.when(head // per_part == part)
            def add_qkv(i=i, kind=kind, head=head):
                at = pl.ds(pl.multiple_of(kind * other_rows + (head % per_part) * HEAD, HEAD), HEAD)
                f_s[at, :] += m_ref[i * HEAD : (i + 1) * HEAD, :]

        @pl.when(me_ref[0] // per_part == part)
        def add_out():
            at = pl.ds(pl.multiple_of((me_ref[0] % per_part) * HEAD, HEAD), HEAD)
            g_s[at, :] += n_ref[...]

        full, other = f_s[...].astype(BF16), g_s[...].astype(BF16)
        nothing = jnp.zeros((half - other_half, other.shape[1]), BF16)
        for at, (sent, kept, mine) in enumerate(
            ((sent_x, kept_x, (me_ref[0] & 1) == 1), (sent_y, kept_y, (me_ref[0] & 2) == 0))
        ):
            first = full[at * half : (at + 1) * half]
            second = jnp.concatenate([other[at * other_half : (at + 1) * other_half], nothing], axis=0)
            sent[...] = jnp.where(mine, second, first)
            kept[...] = jnp.where(mine, first, second)

    columns = 512
    return by_columns(
        body,
        [left, other_left],
        [right, other_right, moment, other_moment],
        [(rows, BF16), (other_rows, BF16)] + [(half, BF16)] * 4,
        columns,
        "weight_grads_plus",
        [
            pltpu.VMEM((rows + other_rows, tokens), BF16),
            pltpu.VMEM((rows, columns), F32),
            pltpu.VMEM((other_rows, columns), F32),
        ],
        me,
    )


def rows_at(index, size):
    return pl.ds(pl.multiple_of(index * size, size), size)


def attention_body(
    first_ref, pre_ref, grad_ref, start_ref, cos_ref, sin_ref, att_ref, out_ref, q_s, k_s, v_s, dk_s, dv_s, o_s, dq_s
):
    pack_len, width = grad_ref.shape
    heads = width // HEAD
    blocks = pack_len // CHUNK
    lane = lax.broadcasted_iota(jnp.int32, (CHUNK, width), 1)
    low_half = lane % HEAD < ROT // 2
    head_of = lane // HEAD

    def turn(values, rows, sign):
        swapped = jnp.where(
            low_half, pltpu.roll(values, width - ROT // 2, 1), pltpu.roll(values, ROT // 2, 1)
        )
        return values * cos_ref[rows, :] + (sign * sin_ref[rows, :]) * swapped

    def prepare(block, carry):
        rows = rows_at(block, CHUNK)
        query = turn(pre_ref[rows, :width], rows, 1.0).astype(BF16)
        q_s[rows, :] = (query.astype(F32) * HEAD ** (-0.5)).astype(BF16)
        k_s[rows, :] = turn(pre_ref[rows, width : 2 * width], rows, 1.0).astype(BF16)
        v_s[rows, :] = pre_ref[rows, 2 * width :].astype(BF16)
        dk_s[rows, :] = jnp.zeros((CHUNK, width), F32)
        dv_s[rows, :] = jnp.zeros((CHUNK, width), F32)
        return carry

    lax.fori_loop(0, blocks, prepare, 0)
    over_last = (((1,), (1,)), ((), ()))
    over_first = (((0,), (0,)), ((), ()))

    def window(block, count):
        rows = rows_at(block, CHUNK)
        span = pl.ds(pl.multiple_of((block + 1 - count) * CHUNK, CHUNK), count * CHUNK)
        shape = (CHUNK, count * CHUNK)
        column = (block + 1 - count) * CHUNK + lax.broadcasted_iota(jnp.int32, shape, 1)
        row = block * CHUNK + lax.broadcasted_iota(jnp.int32, shape, 0)
        allowed = (column >= start_ref[rows, :]) & (column <= row)
        o_s[...] = jnp.zeros((CHUNK, width), F32)
        dq_s[...] = jnp.zeros((CHUNK, width), F32)

        def one_head(head, carry):
            mine = head_of == head
            query = jnp.where(mine, q_s[rows, :], jnp.zeros((), BF16))
            grad = jnp.where(mine, grad_ref[rows, :], jnp.zeros((), BF16))
            keys, values = k_s[span, :], v_s[span, :]
            scores = lax.dot_general(query, keys, over_last, preferred_element_type=F32)
            scores = jnp.where(allowed, scores, NEG)
            prob = jnp.exp(scores - jnp.max(scores, axis=1, keepdims=True))
            prob = prob * (1.0 / jnp.sum(prob, axis=1, keepdims=True))
            prob_low = prob.astype(BF16)
            grad_prob = lax.dot_general(grad, values, over_last, preferred_element_type=F32)
            delta = jnp.sum(prob * grad_prob, axis=1, keepdims=True)
            grad_scores = (prob * (grad_prob - delta)).astype(BF16)
            o_s[...] += jnp.where(mine, jnp.dot(prob_low, values, preferred_element_type=F32), 0.0)
            dq_s[...] += jnp.where(mine, jnp.dot(grad_scores, keys, preferred_element_type=F32), 0.0)
            dk_s[span, :] += lax.dot_general(
                grad_scores, query, over_first, preferred_element_type=F32
            )
            dv_s[span, :] += lax.dot_general(prob_low, grad, over_first, preferred_element_type=F32)
            return carry

        lax.fori_loop(0, heads, one_head, 0)
        att_ref[rows, :] = o_s[...].astype(BF16)
        out_ref[rows, :width] = turn(dq_s[...] * HEAD ** (-0.5), rows, -1.0).astype(BF16)

    def one_block(block, carry):
        used = block + 1 - first_ref[block]
        for count in range(1, min(blocks, -(-(SEQ_MAX - 1) // CHUNK) + 1) + 1):
            pl.when(used == count)(functools.partial(window, block, count))
        return carry

    lax.fori_loop(0, blocks, one_block, 0)

    def finish(block, carry):
        rows = rows_at(block, CHUNK)
        out_ref[rows, width : 2 * width] = turn(dk_s[rows, :], rows, -1.0).astype(BF16)
        out_ref[rows, 2 * width :] = dv_s[rows, :].astype(BF16)
        return carry

    lax.fori_loop(0, blocks, finish, 0)


def attention(pre_qkv, grad_attended, tables, part, width):
    pack_len = grad_attended.shape[0]
    whole = pl.BlockSpec(memory_space=pltpu.VMEM)
    return pl.pallas_call(
        attention_body,
        grid=(1,),
        out_shape=(
            jax.ShapeDtypeStruct((pack_len, width), BF16),
            jax.ShapeDtypeStruct((pack_len, 3 * width), BF16),
        ),
        in_specs=[
            pl.BlockSpec(memory_space=pltpu.SMEM),
            pl.BlockSpec((pack_len, 3 * width), lambda step: (0, part), memory_space=pltpu.VMEM),
            pl.BlockSpec((pack_len, width), lambda step: (0, part), memory_space=pltpu.VMEM),
            whole,
            whole,
            whole,
        ],
        out_specs=(whole, whole),
        scratch_shapes=[pltpu.VMEM((pack_len, width), BF16)] * 3
        + [pltpu.VMEM((pack_len, width), F32)] * 2
        + [pltpu.VMEM((CHUNK, width), F32)] * 2,
        compiler_params=pltpu.CompilerParams(vmem_limit_bytes=VMEM_BYTES),
        cost_estimate=NOTHING,
        name="attention",
    )(tables[0], pre_qkv, grad_attended, *tables[1:])


def tri(index):
    return index * (index + 1) // 2


def packed_rows(size):
    return tri(size // CHUNK) * CHUNK


def panels(size):
    for panel in range(size // PANEL):
        yield panel, (panel + 1) * PANEL, slice(panel * PANEL, (panel + 1) * PANEL)


def symmetric(lhs, rhs, size, epilogue):
    for panel, height, columns in panels(size):
        epilogue(
            panel, height, columns, jnp.dot(lhs[:height, :], rhs[:, columns], preferred_element_type=F32)
        )


def put_mirrored(ref, height, columns, values):
    ref[:height, columns] = values
    if height > PANEL:
        ref[columns, : height - PANEL] = values[: height - PANEL, :].T


def gram_packed(x, xt_ref, size, packed_ref):
    depth = x.shape[0]
    for block in range(depth // CHUNK):
        part = slice(block * CHUNK, (block + 1) * CHUNK)
        xt_ref[:, part] = x[part, :].T
    for panel, height, columns in panels(size):
        product = jnp.dot(xt_ref[:height, :depth], x[:, columns], preferred_element_type=F32).astype(BF16)
        for half in range(PANEL // CHUNK):
            column = panel * (PANEL // CHUNK) + half
            rows = (column + 1) * CHUNK
            packed_ref[tri(column) * CHUNK : tri(column) * CHUNK + rows, :] = product[
                :rows, half * CHUNK : (half + 1) * CHUNK
            ]


def gram_body(x_ref, packed_ref, xt_s):
    gram_packed(x_ref, xt_s, x_ref.shape[1], packed_ref)


def owned_gram_body(me_ref, *refs):
    early, late, (x_ref, packed_ref, xt_s) = refs[:5], refs[5:13], refs[13:]
    pieces = [late[at : at + 2] for at in range(0, 8, 2)]
    block = early[0].shape[0]

    @pl.when((me_ref[0] == 0) | (me_ref[0] == 3))
    def from_early():
        at = 0
        for one in early:
            x_ref[at : at + one.shape[0], :] = one[...]
            at += one.shape[0]

    for owner, share in ((1, 1), (2, 3)):

        @pl.when(me_ref[0] == owner)
        def from_late(share=share):
            rows = pieces[0][0].shape[0] // share
            for at, (total, got) in enumerate(pieces):
                x_ref[at * rows : (at + 1) * rows, :] = (total[:rows, :] + got[:rows, :].astype(F32)).astype(BF16)
            x_ref[4 * rows :, :] = jnp.zeros((4 * (block - rows), x_ref.shape[1]), BF16)

    gram_packed(x_ref, xt_s, x_ref.shape[1], packed_ref)


def unpack(packed_ref, size, scale, exact_s, low_s):
    per_panel = PANEL // CHUNK
    for column in range(size // CHUNK):
        rows = (column + 1) * CHUNK
        at = tri(column) * CHUNK
        panel, half = column // per_panel, column % per_panel
        base = tri(panel) * PANEL
        lanes = slice(half * CHUNK, (half + 1) * CHUNK)
        cols = slice(column * CHUNK, (column + 1) * CHUNK)
        values = packed_ref[at : at + rows, :].astype(F32) * scale
        exact_s[base : base + rows, lanes] = values
        low = values.astype(BF16)
        low_s[:rows, cols] = low
        if column:
            low_s[cols, : rows - CHUNK] = low[: rows - CHUNK, :].T
        for other in range(half):
            left = panel * per_panel + other
            exact_s[base + column * CHUNK : base + rows, other * CHUNK : (other + 1) * CHUNK] = values[
                left * CHUNK : (left + 1) * CHUNK, :
            ].T


def iterate(x_s, exact_s, low_s, poly_s, mix_s, size, count):
    def one(step, carry):
        source, target = step % 2, (step + 1) % 2

        def poly_end(panel, height, columns, product):
            at = tri(panel) * PANEL
            values = NS_B * exact_s[at : at + height, :] + NS_C * product
            put_mirrored(poly_s, height, columns, values.astype(BF16))

        symmetric(low_s, low_s, size, poly_end)

        def x_columns(panel, inner):
            columns = rows_at(panel, PANEL)
            product = jnp.dot(x_s[source], poly_s[:, columns], preferred_element_type=F32)
            x_s[target, :, columns] = (NS_A * x_s[source, :, columns].astype(F32) + product).astype(BF16)
            return inner

        lax.fori_loop(0, size // PANEL, x_columns, 0)

        @pl.when(step < count - 1)
        def next_gram():
            def mix_end(panel, height, columns, product):
                at = tri(panel) * PANEL
                exact_s[at : at + height, :] = (NS_A * NS_A) * exact_s[at : at + height, :] + (
                    2.0 * NS_A
                ) * product
                put_mirrored(mix_s, height, columns, product.astype(BF16))

            symmetric(low_s, poly_s, size, mix_end)

            def gram_end(panel, height, columns, product):
                at = tri(panel) * PANEL
                values = exact_s[at : at + height, :] + product
                exact_s[at : at + height, :] = values
                put_mirrored(low_s, height, columns, values.astype(BF16))

            symmetric(mix_s, poly_s, size, gram_end)

        return carry

    lax.fori_loop(0, count, one, 0)


def first_body(count, packed_ref, x_ref, x_out, packed_out, x_s, exact_s, low_s, poly_s, mix_s, packed_s, sems):
    size = x_ref.shape[1]
    load_x = pltpu.make_async_copy(x_ref, x_s.at[0], sems.at[0])
    load_packed = pltpu.make_async_copy(packed_ref, packed_s, sems.at[1])
    load_x.start()
    load_packed.start()
    load_packed.wait()
    trace = jnp.zeros((1, 1), F32)
    eye = lax.broadcasted_iota(jnp.int32, (CHUNK, CHUNK), 0) == lax.broadcasted_iota(
        jnp.int32, (CHUNK, CHUNK), 1
    )
    for column in range(size // CHUNK):
        at = tri(column) * CHUNK + column * CHUNK
        block = jnp.where(eye, packed_s[at : at + CHUNK, :].astype(F32), 0.0)
        trace = trace + jnp.sum(jnp.sum(block, axis=1, keepdims=True), axis=0, keepdims=True)
    inverse = 1.0 / (jnp.sqrt(trace) + 1e-7)
    unpack(packed_s, size, inverse * inverse, exact_s, low_s)
    load_x.wait()
    iterate(x_s, exact_s, low_s, poly_s, mix_s, size, count)
    depth = x_ref.shape[0]

    def scale_rows(block, carry):
        rows = rows_at(block, CHUNK)
        x_s[count % 2, rows, :] = (x_s[count % 2, rows, :].astype(F32) * inverse).astype(BF16)
        return carry

    lax.fori_loop(0, depth // CHUNK, scale_rows, 0)
    store_x = pltpu.make_async_copy(x_s.at[count % 2], x_out, sems.at[0])
    store_x.start()
    gram_packed(x_s.at[count % 2], poly_s, size, packed_s)
    store_packed = pltpu.make_async_copy(packed_s, packed_out, sems.at[1])
    store_packed.start()
    store_x.wait()
    store_packed.wait()


def second_body(count, from_ref, packed_ref, x_ref, *refs):
    outs, (x_s, exact_s, low_s, poly_s, mix_s, packed_s, sems, out_sems) = refs[:-8], refs[-8:]
    size = x_ref.shape[1]
    load_x = pltpu.make_async_copy(x_ref, x_s.at[0], sems.at[0])
    load_packed = pltpu.make_async_copy(packed_ref, packed_s, sems.at[1])
    load_x.start()
    load_packed.start()
    load_packed.wait()
    unpack(packed_s, size, 1.0, exact_s, low_s)
    load_x.wait()
    iterate(x_s, exact_s, low_s, poly_s, mix_s, size, count)
    stores = []
    for out in outs:
        unit = x_ref.shape[0] // out_sems.shape[0]
        for at in range(0, out.shape[0], unit):
            source = pl.ds(pl.multiple_of(from_ref[len(stores)], unit), unit)
            stores.append(
                pltpu.make_async_copy(
                    x_s.at[count % 2, source, :], out.at[at : at + unit, :], out_sems.at[len(stores)]
                )
            )
    for store in stores:
        store.start()
    for store in stores:
        store.wait()


def ns_scratch(depth, size):
    return [
        pltpu.VMEM((2, depth, size), BF16),
        pltpu.VMEM((tri(size // PANEL) * PANEL, PANEL), F32),
        pltpu.VMEM((size, size), BF16),
        pltpu.VMEM((size, size), BF16),
        pltpu.VMEM((size, size), BF16),
        pltpu.VMEM((packed_rows(size), CHUNK), BF16),
        pltpu.SemaphoreType.DMA((2,)),
    ]


def first_gram(rows, early=(), late=()):
    depth, size = rows
    vmem = pl.BlockSpec(memory_space=pltpu.VMEM)
    shapes = (jax.ShapeDtypeStruct((depth, size), BF16), jax.ShapeDtypeStruct((packed_rows(size), CHUNK), BF16))
    me = lax.axis_index("dp").astype(jnp.int32).reshape(1)
    return pl.pallas_call(
        owned_gram_body,
        out_shape=shapes,
        in_specs=[pl.BlockSpec(memory_space=pltpu.SMEM)] + [vmem] * (len(early) + len(late)),
        out_specs=(vmem, vmem),
        scratch_shapes=[pltpu.VMEM((size, depth), BF16)],
        compiler_params=pltpu.CompilerParams(vmem_limit_bytes=VMEM_BYTES),
        cost_estimate=NOTHING,
        name="gram",
    )(me, *early, *late)


def orthogonalize(rows, packed, source_rows, pieces, after_gram, beside_first, after_first_steps, after_first, beside_last):
    depth, size = rows.shape
    packed_shape = jax.ShapeDtypeStruct((packed_rows(size), CHUNK), BF16)
    x_shape = jax.ShapeDtypeStruct((depth, size), BF16)
    vmem = pl.BlockSpec(memory_space=pltpu.VMEM)
    hbm = pl.BlockSpec(memory_space=pl.ANY)
    params = pltpu.CompilerParams(vmem_limit_bytes=VMEM_BYTES)

    def gram_sum(packed, meanwhile):
        part = lax.psum_scatter(packed, "group", scatter_dimension=0, tiled=True)
        return lax.all_gather(after(part, *jax.tree.leaves(meanwhile)), "group", axis=0, tiled=True)

    if packed is None:
        packed = pl.pallas_call(
            gram_body,
            out_shape=packed_shape,
            in_specs=[vmem],
            out_specs=vmem,
            scratch_shapes=[pltpu.VMEM((size, depth), BF16)],
            compiler_params=params,
            cost_estimate=NOTHING,
            name="gram",
        )(rows)
    meanwhile = after_gram(packed)
    gathered = gram_sum(packed, meanwhile)
    first = beside_first(gathered, meanwhile)
    half_way, packed = pl.pallas_call(
        functools.partial(first_body, 2),
        out_shape=(x_shape, packed_shape),
        in_specs=[hbm, hbm],
        out_specs=(hbm, hbm),
        scratch_shapes=ns_scratch(depth, size),
        compiler_params=params,
        cost_estimate=NOTHING,
        name="first_steps",
    )(gathered, rows)
    first = after_first_steps(first, packed)
    packed = after(packed, *first)
    meanwhile = after_first(packed, first)
    gathered = gram_sum(packed, meanwhile)
    last = beside_last(gathered)
    results = pl.pallas_call(
        functools.partial(second_body, 3),
        out_shape=[jax.ShapeDtypeStruct((piece, size), BF16) for piece in pieces],
        in_specs=[pl.BlockSpec(memory_space=pltpu.SMEM), hbm, hbm],
        out_specs=[hbm] * len(pieces),
        scratch_shapes=ns_scratch(depth, size) + [pltpu.SemaphoreType.DMA((source_rows.shape[0],))],
        compiler_params=params,
        cost_estimate=NOTHING,
        name="last_steps",
    )(source_rows, gathered, half_way)
    return results, first, meanwhile, last


def two_by_two():
    return lax.axis_size("dp") == 4


def hop(values, bit, targets=range(4)):
    return lax.ppermute(values, "dp", [(t ^ bit, t) for t in targets])


def by_distance(parts):
    me = lax.axis_index("dp")
    return jnp.stack([lax.dynamic_index_in_dim(parts, me ^ r, 0, keepdims=False) for r in range(4)])


def gather_near(own):
    return own, hop(own, 1), hop(own, 2)


def gather_far(near):
    own, from_x, from_y = near
    half = own.shape[0] // 2
    first, second = hop(from_y[:half], 1), hop(from_x[half:], 2)
    return jnp.stack([own, from_x, from_y, jnp.concatenate([first, second], axis=0)])


def reduce_start(sent_x, kept_x, sent_y, kept_y):
    return kept_x, hop(sent_x, 1), kept_y, hop(sent_y, 2)


def reduce_next(state, *others):
    def body(*refs):
        outs = refs[4 + len(others) :]
        for k in range(2):
            total = refs[2 * k][...].astype(F32) + refs[2 * k + 1][...].astype(F32)
            outs[2 * k][...] = total
            outs[2 * k + 1][...] = total.astype(BF16)

    shapes = [(state[0].shape, dtype) for dtype in (F32, BF16)] * 2
    total_x, out_x, total_y, out_y = in_vmem(body, state, others, shapes, "reduce_next")
    return (total_x, hop(out_x, 2, [1, 2]), total_y, hop(out_y, 1, [1, 2])), (out_x, out_y)


def scatter_start(split):
    left_out, left, right_out, right = split
    return left, hop(left_out, 1), right, hop(right_out, 2)


def scatter_next(state, *others):
    half = state[0].shape[0] // 2

    def body(*refs):
        outs = refs[4 + len(others) :]
        for k in range(2):
            total = refs[2 * k][...].astype(F32) + refs[2 * k + 1][...].astype(F32)
            outs[2 * k][...] = total[:half]
            outs[2 * k + 1][...] = total[half:].astype(BF16)

    shapes = [((half, state[0].shape[1]), dtype) for dtype in (F32, BF16)] * 2
    left, left_out, right, right_out = in_vmem(body, state, others, shapes, "scatter_next")
    return (left, hop(left_out, 2), right, hop(right_out, 1)), (left_out, right_out)


def scatter_end(state):
    left, left_in, right, right_in = state
    return jnp.concatenate([left + left_in.astype(F32), right + right_in.astype(F32)], axis=0)


def scatter_momentum(state, moment, *others):
    rows, width = moment.shape
    half = rows // 2

    def body(*refs):
        left, left_in, right, right_in, moment_ref = refs[:5]
        own, full = refs[5 + len(others) :]
        for at, (one, got) in ((0, (left, left_in)), (half, (right, right_in))):
            total = one[...] + got[...].astype(F32)
            own[at : at + half, :] = total
            full[at : at + half, :] = (total + moment_ref[at : at + half, :]).astype(BF16)

    shapes = [((rows, width), F32), ((rows, width), BF16)]
    return in_vmem(body, [*state, moment], others, shapes, "momentum")


def owners_start(slots, owners, *others):
    rows, width = slots[0].shape
    half = rows // 2
    me = lax.axis_index("dp").astype(jnp.int32).reshape(1)

    def body(me_ref, first_ref, second_ref, *refs):
        outs = refs[len(others) :]
        for r in range(4):
            picked = jnp.where((me_ref[0] ^ r) == owners[0], first_ref[...], second_ref[...])
            if r < 3:
                outs[r][...] = picked
            else:
                outs[3][...], outs[4][...] = picked[:half], picked[half:]

    shapes = [((rows, width), BF16)] * 3 + [((half, width), BF16)] * 2
    own, to_x, to_y, first_hop, second_hop = sent = in_vmem(body, slots, others, shapes, "to_owners", me)
    first_hop, second_hop = hop(first_hop, 1, [t ^ 2 for t in owners]), hop(second_hop, 2, [t ^ 1 for t in owners])
    return (own, hop(to_x, 1, owners), hop(to_y, 2, owners), first_hop, second_hop), sent[1:]


def owners_end(state, owners, *others):
    own, from_x, from_y, first_hop, second_hop = state
    return own, from_x, from_y, hop(after(first_hop, *others), 2, owners), hop(second_hop, 1, owners)


def exchange_dp(own, to_x, to_y, first_hop, second_hop):
    first_hop, second_hop = hop(first_hop, 1), hop(second_hop, 2)
    from_x, from_y = hop(to_x, 1), hop(to_y, 2)
    first, second = hop(first_hop, 2), hop(second_hop, 1)
    return jnp.stack([own, from_x, from_y, jnp.concatenate([first, second], axis=0)])


def butterfly(values):
    for axis in ("group", "dp"):
        size, bit = lax.axis_size(axis), 1
        while bit < size:
            values = values + lax.ppermute(values, axis, [(i, i ^ bit) for i in range(size)])
            bit *= 2
    return values


def heads_aligned(unit):
    return unit == HEAD and lax.axis_size("group") % 3 != 0


def spread_qkv(own, unit):
    group_count = lax.axis_size("group")
    me = lax.axis_index("group")
    moved = jnp.stack(
        [
            lax.ppermute(
                own[j * unit : (j + 1) * unit], "group", [(g, (3 * g + j) % group_count) for g in range(group_count)]
            )
            for j in range(3)
        ]
    )
    return jnp.concatenate(
        [lax.dynamic_index_in_dim(moved, (me + group_count * i) % 3, 0, keepdims=False) for i in range(3)]
    )


def return_qkv(rows, unit):
    group_count = lax.axis_size("group")
    me = lax.axis_index("group")
    inverse = pow(group_count, -1, 3)
    parts = rows.reshape(3, unit, rows.shape[1])
    return jnp.concatenate(
        [
            lax.ppermute(
                lax.dynamic_index_in_dim(parts, ((j - me) * inverse) % 3, 0, keepdims=False),
                "group",
                [((3 * g + j) % group_count, g) for g in range(group_count)],
            )
            for j in range(3)
        ]
    )


def head_rows(matrix, heads):
    group_count = lax.axis_size("group")
    lead = matrix.shape[:-2]
    split = matrix.reshape(lead + (heads, group_count, HEAD, matrix.shape[-1]))
    picked = lax.dynamic_index_in_dim(split, lax.axis_index("group"), len(lead) + 1, keepdims=False)
    return picked.reshape(lead + (heads * HEAD, matrix.shape[-1]))


def spread_heads(rows, heads):
    group_count = lax.axis_size("group")
    lead = rows.shape[:-2]
    width = rows.shape[-1]
    part = rows.reshape(lead + (heads, 1, HEAD, width))
    empty = jnp.zeros(lead + (heads, group_count, HEAD, width), rows.dtype)
    placed = lax.dynamic_update_slice_in_dim(empty, part, lax.axis_index("group"), len(lead) + 1)
    return placed.reshape(lead + (heads * group_count * HEAD, width))


def shards(
    hidden_in,
    cotangent,
    segment_ids,
    weight_in,
    weight_back,
    moment_in,
    moment_back,
    norm_gain,
    norm_shift,
    bias_in,
    bias_out,
    vector_moment,
):
    model_width = hidden_in.shape[2]
    tokens = hidden_in.shape[1]
    data_count = lax.axis_size("dp")
    group_count = lax.axis_size("group")
    devices = data_count * group_count
    me_group = lax.axis_index("group")
    me = lax.axis_index("dp")
    unit = model_width // devices
    qkv_rows = 3 * unit
    ff_rows = FF // devices
    out_rows = unit
    heads = HEADS // group_count
    width = heads * HEAD
    fast = heads_aligned(unit) and two_by_two()
    everywhere = ("dp", "group")

    def dot(left, right):
        return jnp.dot(left, right, preferred_element_type=F32)

    def dot_last(left, right):
        return lax.dot_general(left, right, (((1,), (1,)), ((), ())), preferred_element_type=F32)

    def dot_first(left, right):
        return lax.dot_general(left, right, (((0,), (0,)), ((), ())), preferred_element_type=F32)

    x_float = hidden_in[0].astype(F32)
    centre = x_float - jnp.mean(x_float, axis=-1, keepdims=True)
    inverse_std = lax.rsqrt(jnp.mean(centre * centre, axis=-1, keepdims=True) + 1e-05)
    x_hat = centre * inverse_std
    normed_low = (x_hat * norm_gain + norm_shift).astype(BF16)
    grad_y = cotangent[0]
    parts = max(1, width // 128)
    lanes = width // parts
    w_in, w_back = weight_in[0], weight_back[0]
    m_in, m_back = MOMENTUM * moment_in[0], MOMENTUM * moment_back[0]
    position = positions(segment_ids[0])
    start = jnp.arange(position.shape[0], dtype=jnp.int32) - position
    tables = (start[::CHUNK] // CHUNK, start[:, None]) + rotary_lanes(position, lanes // HEAD)
    grad_y_float = grad_y.astype(F32)

    def to_parts(rows):
        split = rows.reshape((3, parts, lanes) + rows.shape[1:])
        return jnp.swapaxes(split, 0, 1).reshape(rows.shape)

    def from_parts(rows):
        split = rows.reshape((parts, 3, lanes) + rows.shape[1:])
        return jnp.swapaxes(split, 0, 1).reshape(rows.shape)

    normed_all = lax.all_gather(normed_low, "group", axis=0, tiled=True)
    if fast:
        w_up = gather_far(gather_near(w_in[qkv_rows:]))
        near_qkv = gather_near(spread_qkv(w_in[:qkv_rows], unit))
        grad_all = lax.all_gather(after(grad_y, normed_all, w_up, *near_qkv[1:], *tables), "group", axis=0, tiled=True)
    else:
        grad_all = lax.all_gather(grad_y, "group", axis=0, tiled=True)
        w_up = lax.all_gather(w_in[qkv_rows:], "dp", axis=0, tiled=True)
    w_up = w_up.reshape(data_count * ff_rows, model_width)

    bias_up = lax.dynamic_index_in_dim(
        bias_in[3 * model_width :].reshape(data_count, group_count, ff_rows), me_group, 1, keepdims=False
    )
    bias_up = (by_distance(bias_up) if fast else bias_up).reshape(data_count * ff_rows)
    bias_qkv = bias_in[: 3 * model_width].reshape(3 * heads, group_count, HEAD)
    bias_qkv = to_parts(lax.dynamic_index_in_dim(bias_qkv, me_group, 1, keepdims=False).reshape(3 * width))
    activated, slope = up_forward(normed_all, w_up, bias_up)
    if fast:
        near_back = gather_near(after(w_back, *near_qkv[1:]))
        own, from_x, from_y = near_qkv
        w_qkv = by_distance(gather_far((own, after(from_x, activated), from_y)))
        own, from_x, from_y = near_back
        all_back = gather_far((own, after(from_x, activated), from_y))
        w_out = by_distance(all_back[:, :out_rows]).reshape(width, model_width)
        w_down = all_back[:, out_rows:].reshape(data_count * ff_rows, model_width)
    else:
        all_qkv = lax.all_gather(w_in[:qkv_rows], everywhere, axis=0, tiled=True)
        w_qkv = head_rows(all_qkv.reshape(3, model_width, model_width), heads)
        w_out = head_rows(lax.all_gather(w_back[:out_rows], everywhere, axis=0, tiled=True), heads)
        w_down = lax.all_gather(w_back[out_rows:], "dp", axis=0, tiled=True)
    w_qkv = to_parts(w_qkv.reshape(3 * width, model_width))
    pre_qkv = project(normed_all, w_qkv, bias_qkv, F32, "project_qkv")
    grad_all = after(grad_all, activated, slope, pre_qkv, w_down, w_out)

    term_down = weight_grad(activated, grad_all, "grad_down", fast)
    if fast:
        m_qkv = spread_qkv(after(m_in[:qkv_rows], term_down[0]), unit)
        sum_down = scatter_start(term_down)
        slope = after(slope, *term_down)
    grad_pre_up = up_backward(grad_all, slope, w_down)
    term_up = weight_grad(grad_pre_up, normed_all, "grad_up", fast)
    late_w_out = w_out
    if fast:
        sum_up = scatter_start(term_up)
        sum_down, flying = scatter_next(sum_down, *term_up)
        late_w_out = after(w_out, *flying)
    grad_attended = project(grad_all, late_w_out, jnp.zeros((width,), F32), BF16, "project_grad")
    ready = ()

    attended, grad_pre_qkv, term_qkv, term_out, sum_att = [], [], [], [], []
    for part in range(parts):
        one, one_grad = attention(pre_qkv, after(grad_attended, *ready), tables, part, lanes)
        attended.append(one)
        grad_pre_qkv.append(one_grad)
        if not fast:
            ready = (one,)
            term_qkv.append(dot_first(one_grad, normed_all).astype(BF16))
            term_out.append(dot_first(one, grad_all).astype(BF16))
            continue
        if part == 0:
            sum_up, flying = scatter_next(sum_up, one)
            own_down, full_down = scatter_momentum(sum_down, m_back[out_rows:], one)
            one_grad = after(one_grad, full_down, *flying)
        one_qkv, one_out, *split = weight_grads_plus(
            one_grad,
            normed_all,
            one,
            grad_all,
            m_qkv,
            m_back[:out_rows],
            part,
            heads,
        )
        sum_att.append(reduce_start(*split))
        if part == 0:
            own_up, full_up = scatter_momentum(sum_up, m_in[qkv_rows:], split[0])
            early, ready = owners_start([full_up, full_down], [0, 3])
        term_qkv.append(one_qkv)
        term_out.append(one_out)

    if fast:
        first_half, flying = reduce_next(sum_att[0], split[0])
        early = owners_end(early, [0, 3], *flying)
        second_half, flying = reduce_next(sum_att[1], *flying)
        owned, packed = first_gram((data_count * ff_rows, model_width), early, (*first_half, *second_half))
    else:
        packed = None
        term_qkv = from_parts(jnp.concatenate(term_qkv))
        term_out = jnp.concatenate(term_out)
        grad_w_qkv = lax.psum_scatter(
            spread_heads(term_qkv.reshape(3, width, model_width), heads).reshape(3 * model_width, model_width),
            everywhere,
            scatter_dimension=0,
            tiled=True,
        ).astype(F32)
        grad_w_out = lax.psum_scatter(
            spread_heads(term_out, heads), everywhere, scatter_dimension=0, tiled=True
        ).astype(F32)
        own_up = lax.psum_scatter(term_up, "dp", scatter_dimension=0, tiled=True).astype(F32)
        own_down = lax.psum_scatter(term_down, "dp", scatter_dimension=0, tiled=True).astype(F32)
        slots = [m_in[qkv_rows:] + own_up, m_in[:qkv_rows] + grad_w_qkv, m_back[:out_rows] + grad_w_out]
        slots = slots + [m_back[out_rows:] + own_down] + [jnp.zeros((0, model_width))] * (data_count - 4)
        slots = [jnp.pad(rows.astype(BF16), ((0, ff_rows - rows.shape[0]), (0, 0))) for rows in slots]
        owned = lax.all_to_all(jnp.stack(slots), "dp", split_axis=0, concat_axis=0, tiled=True)
        owned = owned.reshape(data_count * ff_rows, model_width)

    def after_gram(packed):
        late_qkv, late_up = jnp.concatenate(grad_pre_qkv, axis=1), after(grad_pre_up, packed)
        late_qkv = after(late_qkv, packed)
        late_attended = after(jnp.concatenate(attended, axis=1), packed)
        normed_part = dot(late_qkv, w_qkv) + dot(late_up, w_up)
        branch_part = dot(late_attended, w_out) + dot(after(activated, packed), w_down)
        split = ()
        if fast:
            terms = [from_parts(jnp.concatenate(term_qkv)), jnp.concatenate(term_out)]
            terms = [after(one, packed).reshape(data_count, -1, model_width) for one in terms]
            terms = by_distance(jnp.concatenate(terms, axis=1)).reshape(2, 2, 2, unit * 2, model_width)
            split = terms[:, 1, 0], terms[:, 0, 0], terms[1, :, 1], terms[0, :, 1]
            split = [one.reshape(4 * unit, model_width) for one in split]
        return normed_part.astype(BF16), branch_part.astype(BF16), late_qkv, late_up, split

    kept = []

    def beside_first(gathered, meanwhile):
        kept.extend(meanwhile[1:])
        if fast:
            split = [after(one, gathered) for one in kept[3]]
            kept.append(scatter_start(split))
        return (lax.psum_scatter(after(meanwhile[0], gathered), "group", scatter_dimension=0, tiled=True),)

    def after_first_steps(first, packed):
        if not fast:
            return first
        state, flying = scatter_next(kept[4], packed)
        kept.append(state)
        return first + flying

    def after_first(packed, first):
        grad_normed = first[0].astype(F32)
        grad_x_hat = grad_normed * norm_gain
        grad_hidden = grad_y_float + inverse_std * (
            grad_x_hat
            - jnp.mean(grad_x_hat, axis=-1, keepdims=True)
            - x_hat * jnp.mean(grad_x_hat * x_hat, axis=-1, keepdims=True)
        )
        if fast:
            own = scatter_end(kept[5])
            own_qkv = return_qkv(own[:qkv_rows].astype(BF16), unit).astype(F32)
            own_out = own[qkv_rows:]
        else:
            own_qkv, own_out = grad_w_qkv, grad_w_out
        grad_in = jnp.concatenate([own_qkv, own_up])
        grad_back = jnp.concatenate([own_out, own_down])
        sums_up = jnp.sum(kept[2].astype(F32), axis=0).reshape(data_count, ff_rows)
        sums_qkv = jnp.sum(kept[1].astype(F32), axis=0)
        vector_local = jnp.concatenate(
            [
                jnp.sum(grad_normed * x_hat, axis=0),
                jnp.sum(grad_normed, axis=0),
                placed(from_parts(sums_qkv), 3 * heads, HEAD),
                placed(by_distance(sums_up) if fast else sums_up, data_count, ff_rows),
                jnp.sum(grad_y_float, axis=0),
            ]
        )
        vector_grad = butterfly(vector_local)
        return grad_hidden, grad_in, grad_back, m_in + grad_in, m_back + grad_back, vector_grad

    def beside_last(gathered):
        return (lax.psum_scatter(after(kept[0], gathered), "group", scatter_dimension=0, tiled=True),)

    def placed(sums, lead, size):
        empty = jnp.zeros((lead, group_count, size), F32)
        return lax.dynamic_update_slice_in_dim(empty, sums.reshape(lead, 1, size), me_group, 1).reshape(-1)

    if fast:
        distance, run = jnp.divmod(jnp.arange(4 * ff_rows // unit), ff_rows // unit)
        holder = me ^ distance
        kind, head = jnp.divmod(3 * holder + jnp.minimum(run, 2), heads)
        per_part = heads // parts
        of_qkv = (head // per_part) * 3 * lanes + kind * lanes + (head % per_part) * HEAD
        source_rows = jnp.where(me == 1, of_qkv, jnp.where(me == 2, holder * unit, distance * ff_rows + run * unit))
        pieces = [ff_rows] * 3 + [ff_rows // 2] * 2
    else:
        source_rows = jnp.arange(0, data_count * ff_rows, ff_rows)
        pieces = [data_count * ff_rows]
    results, _, meanwhile, (branch,) = orthogonalize(
        owned, packed, source_rows.astype(jnp.int32), pieces, after_gram, beside_first, after_first_steps, after_first, beside_last
    )
    grad_hidden, grad_in, grad_back, moment_in_new, moment_back_new, vector_grad = meanwhile
    block_out = (x_float + branch.astype(F32) + bias_out).astype(BF16)
    if fast:
        returned = by_distance(exchange_dp(*results))
        o_qkv = return_qkv(returned[1, :qkv_rows], unit)
    else:
        result = results[0].reshape(data_count, ff_rows, model_width)
        returned = lax.all_to_all(result, "dp", split_axis=0, concat_axis=0, tiled=True)
        o_qkv = returned[1, :qkv_rows]

    def step_of(rows, scale):
        return -scale * rows.astype(F32)

    scale_ff = math.sqrt(1.0 * FF)
    step_in = jnp.concatenate(
        [step_of(o_qkv, math.sqrt(3.0 * model_width)), step_of(returned[0], scale_ff)], axis=0
    )[None]
    step_back = jnp.concatenate(
        [step_of(returned[2, :out_rows], math.sqrt(1.0 * model_width)), step_of(returned[3], scale_ff)], axis=0
    )[None]
    bias_out_grad = vector_grad[vector_grad.shape[0] - model_width :]
    vector_moment_new = MOMENTUM * vector_moment + vector_grad
    vector_step = -(0.2 / math.sqrt(tokens * devices)) * vector_moment_new
    return (
        block_out[None],
        grad_hidden[None],
        grad_in[None],
        grad_back[None],
        moment_in_new[None],
        moment_back_new[None],
        step_in,
        step_back,
        vector_grad,
        vector_moment_new,
        vector_step,
        bias_out_grad,
    )


def solution(mesh):
    tokens_spec = P("dp", "group", None)
    blocks_spec = P(("dp", "group"), None, None)
    in_specs = (
        (tokens_spec, tokens_spec, P("dp", None))
        + (blocks_spec,) * 4
        + (P(),) * 5
    )
    out_specs = (tokens_spec, tokens_spec) + (blocks_spec,) * 6 + (P(),) * 4
    return jax.shard_map(shards, mesh=mesh, in_specs=in_specs, out_specs=out_specs, check_vma=False)
```

```python
import functools
import math

import jax
import jax.numpy as jnp
from jax import lax
from jax.experimental import pallas as pl
from jax.experimental.pallas import tpu as pltpu
from jax.sharding import PartitionSpec as P

HEADS = 32
HEAD = 64
ROT = 32
FF = 8192
SEQ_MAX = 1024
NEG = -1e30
NS_A = 3.4445
NS_B = -4.775
NS_C = 2.0315
MOMENTUM = 0.95
F32 = jnp.float32
BF16 = jnp.bfloat16
CHUNK = 256
PANEL = 512
VMEM_BYTES = 61 * 2**20
MATMUL_BYTES = 60 * 2**20


def positions(segments):
    index_all = jnp.arange(segments.shape[0], dtype=jnp.int32)
    previous = jnp.concatenate([jnp.full((1,), -1, jnp.int32), segments[:-1]])
    starts = jnp.where(segments != previous, index_all, 0)
    return index_all - lax.cummax(starts, axis=0)


def gelu_and_slope(values):
    square = values * values
    bent = jnp.tanh(0.7978845608028654 * (values + 0.044715 * values * square))
    inner_slope = 0.7978845608028654 * (1.0 + 3.0 * 0.044715 * square)
    half = 0.5 * (1.0 + bent)
    return values * half, half + 0.5 * values * (1.0 - bent * bent) * inner_slope


def rotary_lanes(position, heads):
    half_rot = ROT // 2
    freq = jnp.exp(jnp.arange(half_rot, dtype=F32) * (-2.0 * math.log(10000.0) / ROT))
    angle = position.astype(F32)[:, None] * freq[None, :]
    cos, sin = jnp.cos(angle), jnp.sin(angle)
    rest = (position.shape[0], HEAD - ROT)
    cos_head = jnp.concatenate([cos, cos, jnp.ones(rest, F32)], axis=1)
    sin_head = jnp.concatenate([-sin, sin, jnp.zeros(rest, F32)], axis=1)
    return jnp.tile(cos_head, (1, heads)), jnp.tile(sin_head, (1, heads))


def after(values, *others):
    return pl.pallas_call(
        lambda *refs: None,
        out_shape=jax.ShapeDtypeStruct(values.shape, values.dtype),
        in_specs=[pl.BlockSpec(memory_space=pl.ANY)] * (1 + len(others)),
        out_specs=pl.BlockSpec(memory_space=pl.ANY),
        input_output_aliases={0: 0},
        name="after",
    )(values, *others)


def over(left, right, axes):
    return lax.dot_general(left, right, (axes, ((), ())), preferred_element_type=F32)


NOTHING = pl.CostEstimate(flops=0, bytes_accessed=0, transcendentals=0)
ROWS = ((1,), (1,))
TOKENS = ((0,), (0,))


def by_rows(body, blocked, whole, outs, rows, name):
    steps = blocked[0].shape[0] // rows
    return pl.pallas_call(
        body,
        grid=(steps,),
        in_specs=[pl.BlockSpec((rows, one.shape[1]), lambda step: (step, 0)) for one in blocked]
        + [
            pl.BlockSpec(one.shape, lambda step, rank=one.ndim: (0,) * rank, pipeline_mode=pl.Buffered(1))
            for one in whole
        ],
        out_specs=tuple(pl.BlockSpec((rows, width), lambda step: (step, 0)) for width, _ in outs),
        out_shape=tuple(jax.ShapeDtypeStruct((steps * rows, width), dtype) for width, dtype in outs),
        compiler_params=pltpu.CompilerParams(vmem_limit_bytes=MATMUL_BYTES),
        cost_estimate=NOTHING,
        name=name,
    )(*blocked, *whole)


def by_columns(body, whole, blocked, outs, columns, name, scratch=(), scalar=None):
    steps = blocked[0].shape[1] // columns
    return pl.pallas_call(
        body,
        grid=(steps,),
        in_specs=([] if scalar is None else [pl.BlockSpec(memory_space=pltpu.SMEM)])
        + [pl.BlockSpec(one.shape, lambda step: (0, 0), pipeline_mode=pl.Buffered(1)) for one in whole]
        + [pl.BlockSpec((one.shape[0], columns), lambda step: (0, step)) for one in blocked],
        out_specs=tuple(pl.BlockSpec((rows, columns), lambda step: (0, step)) for rows, _ in outs),
        out_shape=tuple(jax.ShapeDtypeStruct((rows, steps * columns), dtype) for rows, dtype in outs),
        scratch_shapes=list(scratch),
        compiler_params=pltpu.CompilerParams(vmem_limit_bytes=MATMUL_BYTES),
        cost_estimate=NOTHING,
        name=name,
    )(*([] if scalar is None else [scalar]), *whole, *blocked)


def in_vmem(body, ins, others, outs, name, scalar=None):
    vmem = pl.BlockSpec(memory_space=pltpu.VMEM)
    first = [] if scalar is None else [pl.BlockSpec(memory_space=pltpu.SMEM)]
    return pl.pallas_call(
        body,
        in_specs=first + [vmem] * len(ins) + [pl.BlockSpec(memory_space=pl.ANY)] * len(others),
        out_specs=[vmem] * len(outs),
        out_shape=[jax.ShapeDtypeStruct(shape, dtype) for shape, dtype in outs],
        compiler_params=pltpu.CompilerParams(vmem_limit_bytes=MATMUL_BYTES),
        cost_estimate=NOTHING,
        name=name,
    )(*([] if scalar is None else [scalar]), *ins, *others)


def up_forward(normed, w_up, bias):
    def body(x_ref, w_ref, b_ref, act_ref, slope_ref):
        act, slope = gelu_and_slope(over(x_ref[...], w_ref[...], ROWS) + b_ref[...])
        act_ref[...] = act.astype(BF16)
        slope_ref[...] = slope.astype(BF16)

    units = w_up.shape[0]
    return by_rows(body, [normed], [w_up, bias[None]], [(units, BF16), (units, BF16)], 256, "up_forward")


def up_backward(grad, slope, w_down):
    def body(g_ref, s_ref, w_ref, out_ref):
        out_ref[...] = (over(g_ref[...], w_ref[...], ROWS) * s_ref[...].astype(F32)).astype(BF16)

    return by_rows(body, [grad, slope], [w_down], [(w_down.shape[0], BF16)], 512, "up_backward")[0]


def project(x, w, bias, dtype, name):
    def body(x_ref, w_ref, b_ref, out_ref):
        out_ref[...] = (over(x_ref[...], w_ref[...], ROWS) + b_ref[...]).astype(dtype)

    return by_rows(body, [x], [w, bias[None]], [(w.shape[0], dtype)], 512, name)[0]


def weight_grad(left, right, name, split=False):
    tokens, rows = left.shape
    quarter = rows // 8 if split else rows

    def body(l_ref, r_ref, *refs):
        t_s = refs[-1]

        @pl.when(pl.program_id(0) == 0)
        def turn_over():
            for block in range(0, tokens, 256):
                t_s[:, block : block + 256] = l_ref[block : block + 256, :].T

        product = jnp.dot(t_s[...], r_ref[...], preferred_element_type=F32).astype(BF16)
        if not split:
            refs[0][...] = product
            return
        for block in range(4):
            for half in range(2):
                y, x = block // 2, block % 2
                sent, at = (x, y) if half == 0 else (y, x)
                source = (2 * block + half) * quarter
                refs[2 * half + 1 - sent][at * quarter : (at + 1) * quarter, :] = product[source : source + quarter, :]

    scratch = [pltpu.VMEM((rows, tokens), BF16)]
    outs = [(2 * quarter, BF16)] * 4 if split else [(rows, BF16)]
    results = by_columns(body, [left], [right], outs, 512, name, scratch)
    return results if split else results[0]


def weight_grads_plus(left, right, other_left, other_right, moment, other_moment, part, heads):
    tokens = left.shape[0]
    rows, other_rows = left.shape[1], other_left.shape[1]
    half, other_half = rows // 2, other_rows // 2
    per_part = other_rows // HEAD
    me = lax.axis_index("dp").astype(jnp.int32).reshape(1)

    def body(
        me_ref, l_ref, o_ref, r_ref, q_ref, m_ref, n_ref, out_ref, other_ref, sent_x, kept_x, sent_y, kept_y, t_s, f_s, g_s
    ):
        @pl.when(pl.program_id(0) == 0)
        def turn_over():
            for block in range(0, tokens, 256):
                t_s[:rows, block : block + 256] = l_ref[block : block + 256, :].T
                t_s[rows:, block : block + 256] = o_ref[block : block + 256, :].T

        f_s[...] = jnp.dot(t_s[:rows, :], r_ref[...], preferred_element_type=F32)
        out_ref[...] = f_s[...].astype(BF16)
        g_s[...] = jnp.dot(t_s[rows:, :], q_ref[...], preferred_element_type=F32)
        other_ref[...] = g_s[...].astype(BF16)
        for i in range(3):
            chunk = 3 * me_ref[0] + i
            kind, head = chunk // heads, chunk % heads

            @pl.when(head // per_part == part)
            def add_qkv(i=i, kind=kind, head=head):
                at = pl.ds(pl.multiple_of(kind * other_rows + (head % per_part) * HEAD, HEAD), HEAD)
                f_s[at, :] += m_ref[i * HEAD : (i + 1) * HEAD, :]

        @pl.when(me_ref[0] // per_part == part)
        def add_out():
            at = pl.ds(pl.multiple_of((me_ref[0] % per_part) * HEAD, HEAD), HEAD)
            g_s[at, :] += n_ref[...]

        full, other = f_s[...].astype(BF16), g_s[...].astype(BF16)
        nothing = jnp.zeros((half - other_half, other.shape[1]), BF16)
        for at, (sent, kept, mine) in enumerate(
            ((sent_x, kept_x, (me_ref[0] & 1) == 1), (sent_y, kept_y, (me_ref[0] & 2) == 0))
        ):
            first = full[at * half : (at + 1) * half]
            second = jnp.concatenate([other[at * other_half : (at + 1) * other_half], nothing], axis=0)
            sent[...] = jnp.where(mine, second, first)
            kept[...] = jnp.where(mine, first, second)

    columns = 512
    return by_columns(
        body,
        [left, other_left],
        [right, other_right, moment, other_moment],
        [(rows, BF16), (other_rows, BF16)] + [(half, BF16)] * 4,
        columns,
        "weight_grads_plus",
        [
            pltpu.VMEM((rows + other_rows, tokens), BF16),
            pltpu.VMEM((rows, columns), F32),
            pltpu.VMEM((other_rows, columns), F32),
        ],
        me,
    )


def rows_at(index, size):
    return pl.ds(pl.multiple_of(index * size, size), size)


def attention_body(
    first_ref, pre_ref, grad_ref, start_ref, cos_ref, sin_ref, att_ref, out_ref, q_s, k_s, v_s, dk_s, dv_s
):
    pack_len, width = grad_ref.shape
    heads = width // HEAD
    blocks = pack_len // CHUNK
    lane = lax.broadcasted_iota(jnp.int32, (CHUNK, width), 1)
    low_half = lane % HEAD < ROT // 2
    head_of = lane // HEAD

    def turn(values, rows, sign):
        swapped = jnp.where(
            low_half, pltpu.roll(values, width - ROT // 2, 1), pltpu.roll(values, ROT // 2, 1)
        )
        return values * cos_ref[rows, :] + (sign * sin_ref[rows, :]) * swapped

    def prepare(block, carry):
        rows = rows_at(block, CHUNK)
        query = turn(pre_ref[rows, :width], rows, 1.0).astype(BF16)
        q_s[rows, :] = (query.astype(F32) * HEAD ** (-0.5)).astype(BF16)
        k_s[rows, :] = turn(pre_ref[rows, width : 2 * width], rows, 1.0).astype(BF16)
        v_s[rows, :] = pre_ref[rows, 2 * width :].astype(BF16)
        dk_s[rows, :] = jnp.zeros((CHUNK, width), F32)
        dv_s[rows, :] = jnp.zeros((CHUNK, width), F32)
        return carry

    lax.fori_loop(0, blocks, prepare, 0)
    over_last = (((1,), (1,)), ((), ()))
    over_first = (((0,), (0,)), ((), ()))

    def window(block, count):
        rows = rows_at(block, CHUNK)
        span = pl.ds(pl.multiple_of((block + 1 - count) * CHUNK, CHUNK), count * CHUNK)
        shape = (CHUNK, count * CHUNK)
        column = (block + 1 - count) * CHUNK + lax.broadcasted_iota(jnp.int32, shape, 1)
        row = block * CHUNK + lax.broadcasted_iota(jnp.int32, shape, 0)
        allowed = (column >= start_ref[rows, :]) & (column <= row)
        allowed = jnp.concatenate([allowed] * heads, axis=0)

        def one_by_one(values):
            return jnp.concatenate(
                [jnp.where(head_of == head, values, jnp.zeros((), BF16)) for head in range(heads)], axis=0
            )

        def side_by_side(values):
            total = values[:CHUNK]
            for head in range(1, heads):
                total = jnp.where(head_of == head, values[head * CHUNK : (head + 1) * CHUNK], total)
            return total

        query, grad = one_by_one(q_s[rows, :]), one_by_one(grad_ref[rows, :])
        keys, values = k_s[span, :], v_s[span, :]
        scores = lax.dot_general(query, keys, over_last, preferred_element_type=F32)
        scores = jnp.where(allowed, scores, NEG)
        prob = jnp.exp(scores - jnp.max(scores, axis=1, keepdims=True))
        prob = prob * (1.0 / jnp.sum(prob, axis=1, keepdims=True))
        prob_low = prob.astype(BF16)
        grad_prob = lax.dot_general(grad, values, over_last, preferred_element_type=F32)
        delta = jnp.sum(prob * grad_prob, axis=1, keepdims=True)
        grad_scores = (prob * (grad_prob - delta)).astype(BF16)
        dk_s[span, :] += lax.dot_general(grad_scores, query, over_first, preferred_element_type=F32)
        dv_s[span, :] += lax.dot_general(prob_low, grad, over_first, preferred_element_type=F32)
        att_ref[rows, :] = side_by_side(jnp.dot(prob_low, values, preferred_element_type=F32)).astype(BF16)
        grad_query = side_by_side(jnp.dot(grad_scores, keys, preferred_element_type=F32))
        out_ref[rows, :width] = turn(grad_query * HEAD ** (-0.5), rows, -1.0).astype(BF16)

    def one_block(block, carry):
        used = block + 1 - first_ref[block]
        for count in range(1, min(blocks, -(-(SEQ_MAX - 1) // CHUNK) + 1) + 1):
            pl.when(used == count)(functools.partial(window, block, count))
        return carry

    lax.fori_loop(0, blocks, one_block, 0)

    def finish(block, carry):
        rows = rows_at(block, CHUNK)
        out_ref[rows, width : 2 * width] = turn(dk_s[rows, :], rows, -1.0).astype(BF16)
        out_ref[rows, 2 * width :] = dv_s[rows, :].astype(BF16)
        return carry

    lax.fori_loop(0, blocks, finish, 0)


def attention(pre_qkv, grad_attended, tables, part, width):
    pack_len = grad_attended.shape[0]
    whole = pl.BlockSpec(memory_space=pltpu.VMEM)
    return pl.pallas_call(
        attention_body,
        grid=(1,),
        out_shape=(
            jax.ShapeDtypeStruct((pack_len, width), BF16),
            jax.ShapeDtypeStruct((pack_len, 3 * width), BF16),
        ),
        in_specs=[
            pl.BlockSpec(memory_space=pltpu.SMEM),
            pl.BlockSpec((pack_len, 3 * width), lambda step: (0, part), memory_space=pltpu.VMEM),
            pl.BlockSpec((pack_len, width), lambda step: (0, part), memory_space=pltpu.VMEM),
            whole,
            whole,
            whole,
        ],
        out_specs=(whole, whole),
        scratch_shapes=[pltpu.VMEM((pack_len, width), BF16)] * 3
        + [pltpu.VMEM((pack_len, width), F32)] * 2,
        compiler_params=pltpu.CompilerParams(vmem_limit_bytes=VMEM_BYTES),
        cost_estimate=NOTHING,
        name="attention",
    )(tables[0], pre_qkv, grad_attended, *tables[1:])


def tri(index):
    return index * (index + 1) // 2


def packed_rows(size):
    return tri(size // CHUNK) * CHUNK


def panels(size):
    for panel in range(size // PANEL):
        yield panel, (panel + 1) * PANEL, slice(panel * PANEL, (panel + 1) * PANEL)


def symmetric(lhs, rhs, size, epilogue):
    for panel, height, columns in panels(size):
        epilogue(
            panel, height, columns, jnp.dot(lhs[:height, :], rhs[:, columns], preferred_element_type=F32)
        )


def put_mirrored(ref, height, columns, values):
    ref[:height, columns] = values
    if height > PANEL:
        ref[columns, : height - PANEL] = values[: height - PANEL, :].T


def gram_packed(x, xt_ref, size, packed_ref):
    depth = x.shape[0]
    for block in range(depth // CHUNK):
        part = slice(block * CHUNK, (block + 1) * CHUNK)
        xt_ref[:, part] = x[part, :].T
    for panel, height, columns in panels(size):
        product = jnp.dot(xt_ref[:height, :depth], x[:, columns], preferred_element_type=F32).astype(BF16)
        for half in range(PANEL // CHUNK):
            column = panel * (PANEL // CHUNK) + half
            rows = (column + 1) * CHUNK
            packed_ref[tri(column) * CHUNK : tri(column) * CHUNK + rows, :] = product[
                :rows, half * CHUNK : (half + 1) * CHUNK
            ]


def gram_body(x_ref, packed_ref, xt_s):
    gram_packed(x_ref, xt_s, x_ref.shape[1], packed_ref)


def owned_gram_body(me_ref, *refs):
    early, late, (x_ref, packed_ref, xt_s) = refs[:5], refs[5:13], refs[13:]
    pieces = [late[at : at + 2] for at in range(0, 8, 2)]
    block = early[0].shape[0]

    @pl.when((me_ref[0] == 0) | (me_ref[0] == 3))
    def from_early():
        at = 0
        for one in early:
            x_ref[at : at + one.shape[0], :] = one[...]
            at += one.shape[0]

    for owner, share in ((1, 1), (2, 3)):

        @pl.when(me_ref[0] == owner)
        def from_late(share=share):
            rows = pieces[0][0].shape[0] // share
            for at, (total, got) in enumerate(pieces):
                x_ref[at * rows : (at + 1) * rows, :] = (total[:rows, :] + got[:rows, :].astype(F32)).astype(BF16)
            x_ref[4 * rows :, :] = jnp.zeros((4 * (block - rows), x_ref.shape[1]), BF16)

    gram_packed(x_ref, xt_s, x_ref.shape[1], packed_ref)


def unpack(packed_ref, size, scale, exact_s, low_s):
    per_panel = PANEL // CHUNK
    for column in range(size // CHUNK):
        rows = (column + 1) * CHUNK
        at = tri(column) * CHUNK
        panel, half = column // per_panel, column % per_panel
        base = tri(panel) * PANEL
        lanes = slice(half * CHUNK, (half + 1) * CHUNK)
        cols = slice(column * CHUNK, (column + 1) * CHUNK)
        values = packed_ref[at : at + rows, :].astype(F32) * scale
        exact_s[base : base + rows, lanes] = values
        low = values.astype(BF16)
        low_s[:rows, cols] = low
        if column:
            low_s[cols, : rows - CHUNK] = low[: rows - CHUNK, :].T
        for other in range(half):
            left = panel * per_panel + other
            exact_s[base + column * CHUNK : base + rows, other * CHUNK : (other + 1) * CHUNK] = values[
                left * CHUNK : (left + 1) * CHUNK, :
            ].T


def iterate(x_s, exact_s, low_s, poly_s, mix_s, size, count):
    def one(step, carry):
        source, target = step % 2, (step + 1) % 2

        def poly_end(panel, height, columns, product):
            at = tri(panel) * PANEL
            values = NS_B * exact_s[at : at + height, :] + NS_C * product
            put_mirrored(poly_s, height, columns, values.astype(BF16))

        symmetric(low_s, low_s, size, poly_end)

        def x_columns(panel, inner):
            columns = rows_at(panel, PANEL)
            product = jnp.dot(x_s[source], poly_s[:, columns], preferred_element_type=F32)
            x_s[target, :, columns] = (NS_A * x_s[source, :, columns].astype(F32) + product).astype(BF16)
            return inner

        lax.fori_loop(0, size // PANEL, x_columns, 0)

        @pl.when(step < count - 1)
        def next_gram():
            def mix_end(panel, height, columns, product):
                at = tri(panel) * PANEL
                exact_s[at : at + height, :] = (NS_A * NS_A) * exact_s[at : at + height, :] + (
                    2.0 * NS_A
                ) * product
                put_mirrored(mix_s, height, columns, product.astype(BF16))

            symmetric(low_s, poly_s, size, mix_end)

            def gram_end(panel, height, columns, product):
                at = tri(panel) * PANEL
                values = exact_s[at : at + height, :] + product
                exact_s[at : at + height, :] = values
                put_mirrored(low_s, height, columns, values.astype(BF16))

            symmetric(mix_s, poly_s, size, gram_end)

        return carry

    lax.fori_loop(0, count, one, 0)


def first_body(count, packed_ref, x_ref, x_out, packed_out, x_s, exact_s, low_s, poly_s, mix_s, packed_s, sems):
    size = x_ref.shape[1]
    load_x = pltpu.make_async_copy(x_ref, x_s.at[0], sems.at[0])
    load_packed = pltpu.make_async_copy(packed_ref, packed_s, sems.at[1])
    load_x.start()
    load_packed.start()
    load_packed.wait()
    trace = jnp.zeros((1, 1), F32)
    eye = lax.broadcasted_iota(jnp.int32, (CHUNK, CHUNK), 0) == lax.broadcasted_iota(
        jnp.int32, (CHUNK, CHUNK), 1
    )
    for column in range(size // CHUNK):
        at = tri(column) * CHUNK + column * CHUNK
        block = jnp.where(eye, packed_s[at : at + CHUNK, :].astype(F32), 0.0)
        trace = trace + jnp.sum(jnp.sum(block, axis=1, keepdims=True), axis=0, keepdims=True)
    inverse = 1.0 / (jnp.sqrt(trace) + 1e-7)
    unpack(packed_s, size, inverse * inverse, exact_s, low_s)
    load_x.wait()
    iterate(x_s, exact_s, low_s, poly_s, mix_s, size, count)
    depth = x_ref.shape[0]

    def scale_rows(block, carry):
        rows = rows_at(block, CHUNK)
        x_s[count % 2, rows, :] = (x_s[count % 2, rows, :].astype(F32) * inverse).astype(BF16)
        return carry

    lax.fori_loop(0, depth // CHUNK, scale_rows, 0)
    store_x = pltpu.make_async_copy(x_s.at[count % 2], x_out, sems.at[0])
    store_x.start()
    gram_packed(x_s.at[count % 2], poly_s, size, packed_s)
    store_packed = pltpu.make_async_copy(packed_s, packed_out, sems.at[1])
    store_packed.start()
    store_x.wait()
    store_packed.wait()


def second_body(count, from_ref, packed_ref, x_ref, *refs):
    outs, (x_s, exact_s, low_s, poly_s, mix_s, packed_s, sems, out_sems) = refs[:-8], refs[-8:]
    size = x_ref.shape[1]
    load_x = pltpu.make_async_copy(x_ref, x_s.at[0], sems.at[0])
    load_packed = pltpu.make_async_copy(packed_ref, packed_s, sems.at[1])
    load_x.start()
    load_packed.start()
    load_packed.wait()
    unpack(packed_s, size, 1.0, exact_s, low_s)
    load_x.wait()
    iterate(x_s, exact_s, low_s, poly_s, mix_s, size, count)
    stores = []
    for out in outs:
        unit = x_ref.shape[0] // out_sems.shape[0]
        for at in range(0, out.shape[0], unit):
            source = pl.ds(pl.multiple_of(from_ref[len(stores)], unit), unit)
            stores.append(
                pltpu.make_async_copy(
                    x_s.at[count % 2, source, :], out.at[at : at + unit, :], out_sems.at[len(stores)]
                )
            )
    for store in stores:
        store.start()
    for store in stores:
        store.wait()


def ns_scratch(depth, size):
    return [
        pltpu.VMEM((2, depth, size), BF16),
        pltpu.VMEM((tri(size // PANEL) * PANEL, PANEL), F32),
        pltpu.VMEM((size, size), BF16),
        pltpu.VMEM((size, size), BF16),
        pltpu.VMEM((size, size), BF16),
        pltpu.VMEM((packed_rows(size), CHUNK), BF16),
        pltpu.SemaphoreType.DMA((2,)),
    ]


def first_gram(rows, early=(), late=()):
    depth, size = rows
    vmem = pl.BlockSpec(memory_space=pltpu.VMEM)
    shapes = (jax.ShapeDtypeStruct((depth, size), BF16), jax.ShapeDtypeStruct((packed_rows(size), CHUNK), BF16))
    me = lax.axis_index("dp").astype(jnp.int32).reshape(1)
    return pl.pallas_call(
        owned_gram_body,
        out_shape=shapes,
        in_specs=[pl.BlockSpec(memory_space=pltpu.SMEM)] + [vmem] * (len(early) + len(late)),
        out_specs=(vmem, vmem),
        scratch_shapes=[pltpu.VMEM((size, depth), BF16)],
        compiler_params=pltpu.CompilerParams(vmem_limit_bytes=VMEM_BYTES),
        cost_estimate=NOTHING,
        name="gram",
    )(me, *early, *late)


def orthogonalize(rows, packed, source_rows, pieces, after_gram, beside_first, after_first_steps, after_first, beside_last):
    depth, size = rows.shape
    packed_shape = jax.ShapeDtypeStruct((packed_rows(size), CHUNK), BF16)
    x_shape = jax.ShapeDtypeStruct((depth, size), BF16)
    vmem = pl.BlockSpec(memory_space=pltpu.VMEM)
    hbm = pl.BlockSpec(memory_space=pl.ANY)
    params = pltpu.CompilerParams(vmem_limit_bytes=VMEM_BYTES)

    def gram_sum(packed, meanwhile):
        part = lax.psum_scatter(packed, "group", scatter_dimension=0, tiled=True)
        return lax.all_gather(after(part, *jax.tree.leaves(meanwhile)), "group", axis=0, tiled=True)

    if packed is None:
        packed = pl.pallas_call(
            gram_body,
            out_shape=packed_shape,
            in_specs=[vmem],
            out_specs=vmem,
            scratch_shapes=[pltpu.VMEM((size, depth), BF16)],
            compiler_params=params,
            cost_estimate=NOTHING,
            name="gram",
        )(rows)
    meanwhile = after_gram(packed)
    gathered = gram_sum(packed, meanwhile)
    first = beside_first(gathered, meanwhile)
    half_way, packed = pl.pallas_call(
        functools.partial(first_body, 2),
        out_shape=(x_shape, packed_shape),
        in_specs=[hbm, hbm],
        out_specs=(hbm, hbm),
        scratch_shapes=ns_scratch(depth, size),
        compiler_params=params,
        cost_estimate=NOTHING,
        name="first_steps",
    )(gathered, rows)
    first = after_first_steps(first, packed)
    packed = after(packed, *first)
    meanwhile = after_first(packed, first)
    gathered = gram_sum(packed, meanwhile)
    last = beside_last(gathered)
    results = pl.pallas_call(
        functools.partial(second_body, 3),
        out_shape=[jax.ShapeDtypeStruct((piece, size), BF16) for piece in pieces],
        in_specs=[pl.BlockSpec(memory_space=pltpu.SMEM), hbm, hbm],
        out_specs=[hbm] * len(pieces),
        scratch_shapes=ns_scratch(depth, size) + [pltpu.SemaphoreType.DMA((source_rows.shape[0],))],
        compiler_params=params,
        cost_estimate=NOTHING,
        name="last_steps",
    )(source_rows, gathered, half_way)
    return results, first, meanwhile, last


def two_by_two():
    return lax.axis_size("dp") == 4


def hop(values, bit, targets=range(4)):
    return lax.ppermute(values, "dp", [(t ^ bit, t) for t in targets])


def by_distance(parts):
    me = lax.axis_index("dp")
    return jnp.stack([lax.dynamic_index_in_dim(parts, me ^ r, 0, keepdims=False) for r in range(4)])


def gather_near(own):
    return own, hop(own, 1), hop(own, 2)


def gather_far(near):
    own, from_x, from_y = near
    half = own.shape[0] // 2
    first, second = hop(from_y[:half], 1), hop(from_x[half:], 2)
    return jnp.stack([own, from_x, from_y, jnp.concatenate([first, second], axis=0)])


def reduce_start(sent_x, kept_x, sent_y, kept_y):
    return kept_x, hop(sent_x, 1), kept_y, hop(sent_y, 2)


def reduce_next(state, *others):
    def body(*refs):
        outs = refs[4 + len(others) :]
        for k in range(2):
            total = refs[2 * k][...].astype(F32) + refs[2 * k + 1][...].astype(F32)
            outs[2 * k][...] = total
            outs[2 * k + 1][...] = total.astype(BF16)

    shapes = [(state[0].shape, dtype) for dtype in (F32, BF16)] * 2
    total_x, out_x, total_y, out_y = in_vmem(body, state, others, shapes, "reduce_next")
    return (total_x, hop(out_x, 2, [1, 2]), total_y, hop(out_y, 1, [1, 2])), (out_x, out_y)


def scatter_start(split):
    left_out, left, right_out, right = split
    return left, hop(left_out, 1), right, hop(right_out, 2)


def scatter_next(state, *others):
    half = state[0].shape[0] // 2

    def body(*refs):
        outs = refs[4 + len(others) :]
        for k in range(2):
            total = refs[2 * k][...].astype(F32) + refs[2 * k + 1][...].astype(F32)
            outs[2 * k][...] = total[:half]
            outs[2 * k + 1][...] = total[half:].astype(BF16)

    shapes = [((half, state[0].shape[1]), dtype) for dtype in (F32, BF16)] * 2
    left, left_out, right, right_out = in_vmem(body, state, others, shapes, "scatter_next")
    return (left, hop(left_out, 2), right, hop(right_out, 1)), (left_out, right_out)


def scatter_end(state, *others):
    left, left_in, right, right_in = state
    if others:
        left, right = after(left, *others), after(right, *others)
    return jnp.concatenate([left + left_in.astype(F32), right + right_in.astype(F32)], axis=0)


def scatter_momentum(state, moment, *others):
    rows, width = moment.shape
    half = rows // 2

    def body(*refs):
        left, left_in, right, right_in, moment_ref = refs[:5]
        own, full = refs[5 + len(others) :]
        for at, (one, got) in ((0, (left, left_in)), (half, (right, right_in))):
            total = one[...] + got[...].astype(F32)
            own[at : at + half, :] = total
            full[at : at + half, :] = (total + moment_ref[at : at + half, :]).astype(BF16)

    shapes = [((rows, width), F32), ((rows, width), BF16)]
    return in_vmem(body, [*state, moment], others, shapes, "momentum")


def owners_start(slots, owners, *others):
    rows, width = slots[0].shape
    half = rows // 2
    me = lax.axis_index("dp").astype(jnp.int32).reshape(1)

    def body(me_ref, first_ref, second_ref, *refs):
        outs = refs[len(others) :]
        for r in range(4):
            picked = jnp.where((me_ref[0] ^ r) == owners[0], first_ref[...], second_ref[...])
            if r < 3:
                outs[r][...] = picked
            else:
                outs[3][...], outs[4][...] = picked[:half], picked[half:]

    shapes = [((rows, width), BF16)] * 3 + [((half, width), BF16)] * 2
    own, to_x, to_y, first_hop, second_hop = sent = in_vmem(body, slots, others, shapes, "to_owners", me)
    first_hop, second_hop = hop(first_hop, 1, [t ^ 2 for t in owners]), hop(second_hop, 2, [t ^ 1 for t in owners])
    return (own, hop(to_x, 1, owners), hop(to_y, 2, owners), first_hop, second_hop), sent[1:]


def owners_end(state, owners, *others):
    own, from_x, from_y, first_hop, second_hop = state
    return own, from_x, from_y, hop(after(first_hop, *others), 2, owners), hop(second_hop, 1, owners)


def exchange_dp(own, to_x, to_y, first_hop, second_hop):
    first_hop, second_hop = hop(first_hop, 1), hop(second_hop, 2)
    from_x, from_y = hop(to_x, 1), hop(to_y, 2)
    first, second = hop(first_hop, 2), hop(second_hop, 1)
    return jnp.stack([own, from_x, from_y, jnp.concatenate([first, second], axis=0)])


def butterfly(values):
    for axis in ("group", "dp"):
        size, bit = lax.axis_size(axis), 1
        while bit < size:
            values = values + lax.ppermute(values, axis, [(i, i ^ bit) for i in range(size)])
            bit *= 2
    return values


def heads_aligned(unit):
    return unit == HEAD and lax.axis_size("group") % 3 != 0


def spread_qkv(own, unit):
    group_count = lax.axis_size("group")
    me = lax.axis_index("group")
    moved = jnp.stack(
        [
            lax.ppermute(
                own[j * unit : (j + 1) * unit], "group", [(g, (3 * g + j) % group_count) for g in range(group_count)]
            )
            for j in range(3)
        ]
    )
    return jnp.concatenate(
        [lax.dynamic_index_in_dim(moved, (me + group_count * i) % 3, 0, keepdims=False) for i in range(3)]
    )


def return_qkv(rows, unit):
    group_count = lax.axis_size("group")
    me = lax.axis_index("group")
    inverse = pow(group_count, -1, 3)
    parts = rows.reshape(3, unit, rows.shape[1])
    return jnp.concatenate(
        [
            lax.ppermute(
                lax.dynamic_index_in_dim(parts, ((j - me) * inverse) % 3, 0, keepdims=False),
                "group",
                [((3 * g + j) % group_count, g) for g in range(group_count)],
            )
            for j in range(3)
        ]
    )


def head_rows(matrix, heads):
    group_count = lax.axis_size("group")
    lead = matrix.shape[:-2]
    split = matrix.reshape(lead + (heads, group_count, HEAD, matrix.shape[-1]))
    picked = lax.dynamic_index_in_dim(split, lax.axis_index("group"), len(lead) + 1, keepdims=False)
    return picked.reshape(lead + (heads * HEAD, matrix.shape[-1]))


def spread_heads(rows, heads):
    group_count = lax.axis_size("group")
    lead = rows.shape[:-2]
    width = rows.shape[-1]
    part = rows.reshape(lead + (heads, 1, HEAD, width))
    empty = jnp.zeros(lead + (heads, group_count, HEAD, width), rows.dtype)
    placed = lax.dynamic_update_slice_in_dim(empty, part, lax.axis_index("group"), len(lead) + 1)
    return placed.reshape(lead + (heads * group_count * HEAD, width))


def shards(
    hidden_in,
    cotangent,
    segment_ids,
    weight_in,
    weight_back,
    moment_in,
    moment_back,
    norm_gain,
    norm_shift,
    bias_in,
    bias_out,
    vector_moment,
):
    model_width = hidden_in.shape[2]
    tokens = hidden_in.shape[1]
    data_count = lax.axis_size("dp")
    group_count = lax.axis_size("group")
    devices = data_count * group_count
    me_group = lax.axis_index("group")
    me = lax.axis_index("dp")
    unit = model_width // devices
    qkv_rows = 3 * unit
    ff_rows = FF // devices
    out_rows = unit
    heads = HEADS // group_count
    width = heads * HEAD
    fast = heads_aligned(unit) and two_by_two()
    everywhere = ("dp", "group")

    def dot(left, right):
        return jnp.dot(left, right, preferred_element_type=F32)

    def dot_last(left, right):
        return lax.dot_general(left, right, (((1,), (1,)), ((), ())), preferred_element_type=F32)

    def dot_first(left, right):
        return lax.dot_general(left, right, (((0,), (0,)), ((), ())), preferred_element_type=F32)

    x_float = hidden_in[0].astype(F32)
    centre = x_float - jnp.mean(x_float, axis=-1, keepdims=True)
    inverse_std = lax.rsqrt(jnp.mean(centre * centre, axis=-1, keepdims=True) + 1e-05)
    x_hat = centre * inverse_std
    normed_low = (x_hat * norm_gain + norm_shift).astype(BF16)
    grad_y = cotangent[0]
    parts = max(1, width // 128)
    lanes = width // parts
    w_in, w_back = weight_in[0], weight_back[0]
    m_in, m_back = MOMENTUM * moment_in[0], MOMENTUM * moment_back[0]
    position = positions(segment_ids[0])
    start = jnp.arange(position.shape[0], dtype=jnp.int32) - position
    tables = (start[::CHUNK] // CHUNK, start[:, None]) + rotary_lanes(position, lanes // HEAD)
    grad_y_float = grad_y.astype(F32)

    def to_parts(rows):
        split = rows.reshape((3, parts, lanes) + rows.shape[1:])
        return jnp.swapaxes(split, 0, 1).reshape(rows.shape)

    def from_parts(rows):
        split = rows.reshape((parts, 3, lanes) + rows.shape[1:])
        return jnp.swapaxes(split, 0, 1).reshape(rows.shape)

    normed_all = lax.all_gather(normed_low, "group", axis=0, tiled=True)
    if fast:
        w_up = gather_far(gather_near(w_in[qkv_rows:]))
        near_qkv = gather_near(spread_qkv(w_in[:qkv_rows], unit))
        grad_all = lax.all_gather(after(grad_y, normed_all, w_up, *near_qkv[1:], *tables), "group", axis=0, tiled=True)
    else:
        grad_all = lax.all_gather(grad_y, "group", axis=0, tiled=True)
        w_up = lax.all_gather(w_in[qkv_rows:], "dp", axis=0, tiled=True)
    w_up = w_up.reshape(data_count * ff_rows, model_width)

    bias_up = lax.dynamic_index_in_dim(
        bias_in[3 * model_width :].reshape(data_count, group_count, ff_rows), me_group, 1, keepdims=False
    )
    bias_up = (by_distance(bias_up) if fast else bias_up).reshape(data_count * ff_rows)
    bias_qkv = bias_in[: 3 * model_width].reshape(3 * heads, group_count, HEAD)
    bias_qkv = to_parts(lax.dynamic_index_in_dim(bias_qkv, me_group, 1, keepdims=False).reshape(3 * width))
    activated, slope = up_forward(normed_all, w_up, bias_up)
    if fast:
        near_back = gather_near(after(w_back, *near_qkv[1:]))
        own, from_x, from_y = near_qkv
        w_qkv = by_distance(gather_far((own, after(from_x, activated), after(from_y, activated))))
        own, from_x, from_y = near_back
        all_back = gather_far((own, after(from_x, activated), after(from_y, activated)))
        w_out = by_distance(all_back[:, :out_rows]).reshape(width, model_width)
        w_down = all_back[:, out_rows:].reshape(data_count * ff_rows, model_width)
    else:
        all_qkv = lax.all_gather(w_in[:qkv_rows], everywhere, axis=0, tiled=True)
        w_qkv = head_rows(all_qkv.reshape(3, model_width, model_width), heads)
        w_out = head_rows(lax.all_gather(w_back[:out_rows], everywhere, axis=0, tiled=True), heads)
        w_down = lax.all_gather(w_back[out_rows:], "dp", axis=0, tiled=True)
    w_qkv = to_parts(w_qkv.reshape(3 * width, model_width))
    pre_qkv = project(normed_all, w_qkv, bias_qkv, F32, "project_qkv")
    branch_up = dot(activated, w_down)
    grad_all = after(grad_all, activated, slope, pre_qkv, w_down, w_out, branch_up)

    term_down = weight_grad(activated, grad_all, "grad_down", fast)
    if fast:
        sum_down = scatter_start(term_down)
        m_qkv = spread_qkv(after(m_in[:qkv_rows], term_down[0]), unit)
        slope = after(slope, *term_down)
    grad_pre_up = up_backward(grad_all, slope, w_down)
    term_up = weight_grad(grad_pre_up, normed_all, "grad_up", fast)
    late_w_out = w_out
    if fast:
        sum_up = scatter_start(term_up)
        sum_down, flying = scatter_next(sum_down, *term_up)
        late_w_out = after(w_out, *flying)
    grad_attended = project(grad_all, late_w_out, jnp.zeros((width,), F32), BF16, "project_grad")
    ready = ()

    attended, grad_pre_qkv, term_qkv, term_out, sum_att = [], [], [], [], []
    for part in range(parts):
        one, one_grad = attention(pre_qkv, after(grad_attended, *ready), tables, part, lanes)
        attended.append(one)
        grad_pre_qkv.append(one_grad)
        if not fast:
            ready = (one,)
            term_qkv.append(dot_first(one_grad, normed_all).astype(BF16))
            term_out.append(dot_first(one, grad_all).astype(BF16))
            continue
        if part == 0:
            sum_up, flying = scatter_next(sum_up, one)
            own_down, full_down = scatter_momentum(sum_down, m_back[out_rows:], one)
            one_grad = after(one_grad, full_down, *flying)
        else:
            first_half, flying = reduce_next(sum_att[0], one)
            one_grad = after(one_grad, *flying)
        one_qkv, one_out, *split = weight_grads_plus(
            one_grad,
            normed_all,
            one,
            grad_all,
            m_qkv,
            m_back[:out_rows],
            part,
            heads,
        )
        sum_att.append(reduce_start(*split))
        if part == 0:
            own_up, full_up = scatter_momentum(sum_up, m_in[qkv_rows:], split[0])
            early, ready = owners_start([full_up, full_down], [0, 3])
        term_qkv.append(one_qkv)
        term_out.append(one_out)

    if fast:
        early = owners_end(early, [0, 3], split[0])
        second_half, _ = reduce_next(sum_att[1])
        owned, packed = first_gram((data_count * ff_rows, model_width), early, (*first_half, *second_half))
    else:
        packed = None
        term_qkv = from_parts(jnp.concatenate(term_qkv))
        term_out = jnp.concatenate(term_out)
        grad_w_qkv = lax.psum_scatter(
            spread_heads(term_qkv.reshape(3, width, model_width), heads).reshape(3 * model_width, model_width),
            everywhere,
            scatter_dimension=0,
            tiled=True,
        ).astype(F32)
        grad_w_out = lax.psum_scatter(
            spread_heads(term_out, heads), everywhere, scatter_dimension=0, tiled=True
        ).astype(F32)
        own_up = lax.psum_scatter(term_up, "dp", scatter_dimension=0, tiled=True).astype(F32)
        own_down = lax.psum_scatter(term_down, "dp", scatter_dimension=0, tiled=True).astype(F32)
        slots = [m_in[qkv_rows:] + own_up, m_in[:qkv_rows] + grad_w_qkv, m_back[:out_rows] + grad_w_out]
        slots = slots + [m_back[out_rows:] + own_down] + [jnp.zeros((0, model_width))] * (data_count - 4)
        slots = [jnp.pad(rows.astype(BF16), ((0, ff_rows - rows.shape[0]), (0, 0))) for rows in slots]
        owned = lax.all_to_all(jnp.stack(slots), "dp", split_axis=0, concat_axis=0, tiled=True)
        owned = owned.reshape(data_count * ff_rows, model_width)

    def after_gram(packed):
        late_qkv, late_up = jnp.concatenate(grad_pre_qkv, axis=1), after(grad_pre_up, packed)
        late_qkv = after(late_qkv, packed)
        normed_part = dot(late_qkv, w_qkv) + dot(late_up, w_up)
        split = ()
        if fast:
            terms = [from_parts(jnp.concatenate(term_qkv)), jnp.concatenate(term_out)]
            terms = [after(one, packed).reshape(data_count, -1, model_width) for one in terms]
            terms = by_distance(jnp.concatenate(terms, axis=1)).reshape(2, 2, 2, unit * 2, model_width)
            split = terms[:, 1, 0], terms[:, 0, 0], terms[1, :, 1], terms[0, :, 1]
            split = [one.reshape(4 * unit, model_width) for one in split]
        branch_part = dot(after(attended_all, packed), w_out) + branch_up
        return normed_part.astype(BF16), late_qkv, late_up, split, branch_part.astype(BF16)

    kept = [None]
    attended_all = jnp.concatenate(attended, axis=1)

    def beside_first(gathered, meanwhile):
        kept.extend(meanwhile[1:])
        if fast:
            split = [after(one, gathered) for one in kept[3]]
            kept.append(scatter_start(split))
        return (lax.psum_scatter(after(meanwhile[0], gathered), "group", scatter_dimension=0, tiled=True),)

    def after_first_steps(first, packed):
        if not fast:
            return first
        state, flying = scatter_next(kept[5], packed)
        kept.append(state)
        return first + flying

    def after_first(packed, first):
        grad_normed = first[0].astype(F32)
        grad_x_hat = grad_normed * norm_gain
        grad_hidden = grad_y_float + inverse_std * (
            grad_x_hat
            - jnp.mean(grad_x_hat, axis=-1, keepdims=True)
            - x_hat * jnp.mean(grad_x_hat * x_hat, axis=-1, keepdims=True)
        )
        if fast:
            own = scatter_end(kept[6])
            own_qkv = return_qkv(own[:qkv_rows].astype(BF16), unit).astype(F32)
            own_out = own[qkv_rows:]
        else:
            own_qkv, own_out = grad_w_qkv, grad_w_out
        grad_in = jnp.concatenate([own_qkv, own_up])
        grad_back = jnp.concatenate([own_out, own_down])
        grads = grad_in, grad_back, m_in + grad_in, m_back + grad_back
        sums_up = jnp.sum(kept[2].astype(F32), axis=0).reshape(data_count, ff_rows)
        sums_qkv = jnp.sum(kept[1].astype(F32), axis=0)
        vector_local = jnp.concatenate(
            [
                jnp.sum(grad_normed * x_hat, axis=0),
                jnp.sum(grad_normed, axis=0),
                placed(from_parts(sums_qkv), 3 * heads, HEAD),
                placed(by_distance(sums_up) if fast else sums_up, data_count, ff_rows),
                jnp.sum(grad_y_float, axis=0),
            ]
        )
        vector_grad = butterfly(vector_local)
        return grad_hidden, vector_grad, *grads

    def beside_last(gathered):
        return (lax.psum_scatter(after(kept[4], gathered), "group", scatter_dimension=0, tiled=True),)

    def placed(sums, lead, size):
        empty = jnp.zeros((lead, group_count, size), F32)
        return lax.dynamic_update_slice_in_dim(empty, sums.reshape(lead, 1, size), me_group, 1).reshape(-1)

    if fast:
        distance, run = jnp.divmod(jnp.arange(4 * ff_rows // unit), ff_rows // unit)
        holder = me ^ distance
        kind, head = jnp.divmod(3 * holder + jnp.minimum(run, 2), heads)
        per_part = heads // parts
        of_qkv = (head // per_part) * 3 * lanes + kind * lanes + (head % per_part) * HEAD
        source_rows = jnp.where(me == 1, of_qkv, jnp.where(me == 2, holder * unit, distance * ff_rows + run * unit))
        pieces = [ff_rows] * 3 + [ff_rows // 2] * 2
    else:
        source_rows = jnp.arange(0, data_count * ff_rows, ff_rows)
        pieces = [data_count * ff_rows]
    results, _, meanwhile, (branch,) = orthogonalize(
        owned, packed, source_rows.astype(jnp.int32), pieces, after_gram, beside_first, after_first_steps, after_first, beside_last
    )
    grad_hidden, vector_grad, grad_in, grad_back, moment_in_new, moment_back_new = meanwhile
    block_out = (x_float + branch.astype(F32) + bias_out).astype(BF16)
    if fast:
        returned = by_distance(exchange_dp(*results))
        o_qkv = return_qkv(returned[1, :qkv_rows], unit)
    else:
        result = results[0].reshape(data_count, ff_rows, model_width)
        returned = lax.all_to_all(result, "dp", split_axis=0, concat_axis=0, tiled=True)
        o_qkv = returned[1, :qkv_rows]

    def step_of(rows, scale):
        return -scale * rows.astype(F32)

    scale_ff = math.sqrt(1.0 * FF)
    step_in = jnp.concatenate(
        [step_of(o_qkv, math.sqrt(3.0 * model_width)), step_of(returned[0], scale_ff)], axis=0
    )[None]
    step_back = jnp.concatenate(
        [step_of(returned[2, :out_rows], math.sqrt(1.0 * model_width)), step_of(returned[3], scale_ff)], axis=0
    )[None]
    bias_out_grad = vector_grad[vector_grad.shape[0] - model_width :]
    vector_moment_new = MOMENTUM * vector_moment + vector_grad
    vector_step = -(0.2 / math.sqrt(tokens * devices)) * vector_moment_new
    return (
        block_out[None],
        grad_hidden[None],
        grad_in[None],
        grad_back[None],
        moment_in_new[None],
        moment_back_new[None],
        step_in,
        step_back,
        vector_grad,
        vector_moment_new,
        vector_step,
        bias_out_grad,
    )


def solution(mesh):
    tokens_spec = P("dp", "group", None)
    blocks_spec = P(("dp", "group"), None, None)
    in_specs = (
        (tokens_spec, tokens_spec, P("dp", None))
        + (blocks_spec,) * 4
        + (P(),) * 5
    )
    out_specs = (tokens_spec, tokens_spec) + (blocks_spec,) * 6 + (P(),) * 4
    return jax.shard_map(shards, mesh=mesh, in_specs=in_specs, out_specs=out_specs, check_vma=False)
```

```python
import functools
import math

import jax
import jax.numpy as jnp
from jax import lax
from jax.experimental import pallas as pl
from jax.experimental.pallas import tpu as pltpu
from jax.sharding import PartitionSpec as P

HEADS = 32
HEAD = 64
ROT = 32
FF = 8192
SEQ_MAX = 1024
NEG = -1e30
NS_A = 3.4445
NS_B = -4.775
NS_C = 2.0315
MOMENTUM = 0.95
F32 = jnp.float32
BF16 = jnp.bfloat16
CHUNK = 256
PANEL = 512
VMEM_BYTES = 61 * 2**20
MATMUL_BYTES = 60 * 2**20


def positions(segments):
    index_all = jnp.arange(segments.shape[0], dtype=jnp.int32)
    previous = jnp.concatenate([jnp.full((1,), -1, jnp.int32), segments[:-1]])
    starts = jnp.where(segments != previous, index_all, 0)
    return index_all - lax.cummax(starts, axis=0)


def gelu_and_slope(values):
    square = values * values
    bent = jnp.tanh(0.7978845608028654 * (values + 0.044715 * values * square))
    inner_slope = 0.7978845608028654 * (1.0 + 3.0 * 0.044715 * square)
    half = 0.5 * (1.0 + bent)
    return values * half, half + 0.5 * values * (1.0 - bent * bent) * inner_slope


def rotary_lanes(position, heads):
    half_rot = ROT // 2
    freq = jnp.exp(jnp.arange(half_rot, dtype=F32) * (-2.0 * math.log(10000.0) / ROT))
    angle = position.astype(F32)[:, None] * freq[None, :]
    cos, sin = jnp.cos(angle), jnp.sin(angle)
    rest = (position.shape[0], HEAD - ROT)
    cos_head = jnp.concatenate([cos, cos, jnp.ones(rest, F32)], axis=1)
    sin_head = jnp.concatenate([-sin, sin, jnp.zeros(rest, F32)], axis=1)
    return jnp.tile(cos_head, (1, heads)), jnp.tile(sin_head, (1, heads))


def after(values, *others):
    return pl.pallas_call(
        lambda *refs: None,
        out_shape=jax.ShapeDtypeStruct(values.shape, values.dtype),
        in_specs=[pl.BlockSpec(memory_space=pl.ANY)] * (1 + len(others)),
        out_specs=pl.BlockSpec(memory_space=pl.ANY),
        input_output_aliases={0: 0},
        name="after",
    )(values, *others)


def over(left, right, axes):
    return lax.dot_general(left, right, (axes, ((), ())), preferred_element_type=F32)


NOTHING = pl.CostEstimate(flops=0, bytes_accessed=0, transcendentals=0)
ROWS = ((1,), (1,))
TOKENS = ((0,), (0,))


def by_rows(body, blocked, whole, outs, rows, name):
    steps = blocked[0].shape[0] // rows
    return pl.pallas_call(
        body,
        grid=(steps,),
        in_specs=[pl.BlockSpec((rows, one.shape[1]), lambda step: (step, 0)) for one in blocked]
        + [
            pl.BlockSpec(one.shape, lambda step, rank=one.ndim: (0,) * rank, pipeline_mode=pl.Buffered(1))
            for one in whole
        ],
        out_specs=tuple(pl.BlockSpec((rows, width), lambda step: (step, 0)) for width, _ in outs),
        out_shape=tuple(jax.ShapeDtypeStruct((steps * rows, width), dtype) for width, dtype in outs),
        compiler_params=pltpu.CompilerParams(vmem_limit_bytes=MATMUL_BYTES),
        cost_estimate=NOTHING,
        name=name,
    )(*blocked, *whole)


def by_columns(body, whole, blocked, outs, columns, name, scratch=(), scalar=None):
    steps = blocked[0].shape[1] // columns
    return pl.pallas_call(
        body,
        grid=(steps,),
        in_specs=([] if scalar is None else [pl.BlockSpec(memory_space=pltpu.SMEM)])
        + [pl.BlockSpec(one.shape, lambda step: (0, 0), pipeline_mode=pl.Buffered(1)) for one in whole]
        + [pl.BlockSpec((one.shape[0], columns), lambda step: (0, step)) for one in blocked],
        out_specs=tuple(pl.BlockSpec((rows, columns), lambda step: (0, step)) for rows, _ in outs),
        out_shape=tuple(jax.ShapeDtypeStruct((rows, steps * columns), dtype) for rows, dtype in outs),
        scratch_shapes=list(scratch),
        compiler_params=pltpu.CompilerParams(vmem_limit_bytes=MATMUL_BYTES),
        cost_estimate=NOTHING,
        name=name,
    )(*([] if scalar is None else [scalar]), *whole, *blocked)


def in_vmem(body, ins, others, outs, name, scalar=None):
    vmem = pl.BlockSpec(memory_space=pltpu.VMEM)
    first = [] if scalar is None else [pl.BlockSpec(memory_space=pltpu.SMEM)]
    return pl.pallas_call(
        body,
        in_specs=first + [vmem] * len(ins) + [pl.BlockSpec(memory_space=pl.ANY)] * len(others),
        out_specs=[vmem] * len(outs),
        out_shape=[jax.ShapeDtypeStruct(shape, dtype) for shape, dtype in outs],
        compiler_params=pltpu.CompilerParams(vmem_limit_bytes=MATMUL_BYTES),
        cost_estimate=NOTHING,
        name=name,
    )(*([] if scalar is None else [scalar]), *ins, *others)


def up_forward(normed, w_up, bias):
    def body(x_ref, w_ref, b_ref, act_ref, slope_ref):
        act, slope = gelu_and_slope(over(x_ref[...], w_ref[...], ROWS) + b_ref[...])
        act_ref[...] = act.astype(BF16)
        slope_ref[...] = slope.astype(BF16)

    units = w_up.shape[0]
    return by_rows(body, [normed], [w_up, bias[None]], [(units, BF16), (units, BF16)], 256, "up_forward")


def up_backward(grad, slope, w_down):
    def body(g_ref, s_ref, w_ref, out_ref):
        out_ref[...] = (over(g_ref[...], w_ref[...], ROWS) * s_ref[...].astype(F32)).astype(BF16)

    return by_rows(body, [grad, slope], [w_down], [(w_down.shape[0], BF16)], 512, "up_backward")[0]


def project(x, w, bias, dtype, name):
    def body(x_ref, w_ref, b_ref, out_ref):
        out_ref[...] = (over(x_ref[...], w_ref[...], ROWS) + b_ref[...]).astype(dtype)

    return by_rows(body, [x], [w, bias[None]], [(w.shape[0], dtype)], 512, name)[0]


def weight_grad(left, right, name, split=False):
    tokens, rows = left.shape
    quarter = rows // 8 if split else rows

    def body(l_ref, r_ref, *refs):
        t_s = refs[-1]

        @pl.when(pl.program_id(0) == 0)
        def turn_over():
            for block in range(0, tokens, 256):
                t_s[:, block : block + 256] = l_ref[block : block + 256, :].T

        product = jnp.dot(t_s[...], r_ref[...], preferred_element_type=F32).astype(BF16)
        if not split:
            refs[0][...] = product
            return
        for block in range(4):
            for half in range(2):
                y, x = block // 2, block % 2
                sent, at = (x, y) if half == 0 else (y, x)
                source = (2 * block + half) * quarter
                refs[2 * half + 1 - sent][at * quarter : (at + 1) * quarter, :] = product[source : source + quarter, :]

    scratch = [pltpu.VMEM((rows, tokens), BF16)]
    outs = [(2 * quarter, BF16)] * 4 if split else [(rows, BF16)]
    results = by_columns(body, [left], [right], outs, 512, name, scratch)
    return results if split else results[0]


def weight_grads_plus(left, right, other_left, other_right, moment, other_moment, part, heads):
    tokens = left.shape[0]
    rows, other_rows = left.shape[1], other_left.shape[1]
    half, other_half = rows // 2, other_rows // 2
    per_part = other_rows // HEAD
    me = lax.axis_index("dp").astype(jnp.int32).reshape(1)

    def body(
        me_ref, l_ref, o_ref, r_ref, q_ref, m_ref, n_ref, out_ref, other_ref, sent_x, kept_x, sent_y, kept_y, t_s, f_s, g_s
    ):
        @pl.when(pl.program_id(0) == 0)
        def turn_over():
            for block in range(0, tokens, 256):
                t_s[:rows, block : block + 256] = l_ref[block : block + 256, :].T
                t_s[rows:, block : block + 256] = o_ref[block : block + 256, :].T

        f_s[...] = jnp.dot(t_s[:rows, :], r_ref[...], preferred_element_type=F32)
        out_ref[...] = f_s[...].astype(BF16)
        g_s[...] = jnp.dot(t_s[rows:, :], q_ref[...], preferred_element_type=F32)
        other_ref[...] = g_s[...].astype(BF16)
        for i in range(3):
            chunk = 3 * me_ref[0] + i
            kind, head = chunk // heads, chunk % heads

            @pl.when(head // per_part == part)
            def add_qkv(i=i, kind=kind, head=head):
                at = pl.ds(pl.multiple_of(kind * other_rows + (head % per_part) * HEAD, HEAD), HEAD)
                f_s[at, :] += m_ref[i * HEAD : (i + 1) * HEAD, :]

        @pl.when(me_ref[0] // per_part == part)
        def add_out():
            at = pl.ds(pl.multiple_of((me_ref[0] % per_part) * HEAD, HEAD), HEAD)
            g_s[at, :] += n_ref[...]

        full, other = f_s[...].astype(BF16), g_s[...].astype(BF16)
        nothing = jnp.zeros((half - other_half, other.shape[1]), BF16)
        for at, (sent, kept, mine) in enumerate(
            ((sent_x, kept_x, (me_ref[0] & 1) == 1), (sent_y, kept_y, (me_ref[0] & 2) == 0))
        ):
            first = full[at * half : (at + 1) * half]
            second = jnp.concatenate([other[at * other_half : (at + 1) * other_half], nothing], axis=0)
            sent[...] = jnp.where(mine, second, first)
            kept[...] = jnp.where(mine, first, second)

    columns = 512
    return by_columns(
        body,
        [left, other_left],
        [right, other_right, moment, other_moment],
        [(rows, BF16), (other_rows, BF16)] + [(half, BF16)] * 4,
        columns,
        "weight_grads_plus",
        [
            pltpu.VMEM((rows + other_rows, tokens), BF16),
            pltpu.VMEM((rows, columns), F32),
            pltpu.VMEM((other_rows, columns), F32),
        ],
        me,
    )


def rows_at(index, size):
    return pl.ds(pl.multiple_of(index * size, size), size)


def attention_body(
    first_ref, pre_ref, grad_ref, start_ref, cos_ref, sin_ref, att_ref, out_ref, q_s, k_s, v_s, dk_s, dv_s
):
    pack_len, width = grad_ref.shape
    heads = width // HEAD
    blocks = pack_len // CHUNK
    lane = lax.broadcasted_iota(jnp.int32, (CHUNK, width), 1)
    low_half = lane % HEAD < ROT // 2
    head_of = lane // HEAD

    def turn(values, rows, sign):
        swapped = jnp.where(
            low_half, pltpu.roll(values, width - ROT // 2, 1), pltpu.roll(values, ROT // 2, 1)
        )
        return values * cos_ref[rows, :] + (sign * sin_ref[rows, :]) * swapped

    def prepare(block, carry):
        rows = rows_at(block, CHUNK)
        query = turn(pre_ref[rows, :width], rows, 1.0).astype(BF16)
        q_s[rows, :] = (query.astype(F32) * HEAD ** (-0.5)).astype(BF16)
        k_s[rows, :] = turn(pre_ref[rows, width : 2 * width], rows, 1.0).astype(BF16)
        v_s[rows, :] = pre_ref[rows, 2 * width :].astype(BF16)
        dk_s[rows, :] = jnp.zeros((CHUNK, width), F32)
        dv_s[rows, :] = jnp.zeros((CHUNK, width), F32)
        return carry

    lax.fori_loop(0, blocks, prepare, 0)
    over_last = (((1,), (1,)), ((), ()))
    over_first = (((0,), (0,)), ((), ()))

    def window(block, count):
        rows = rows_at(block, CHUNK)
        span = pl.ds(pl.multiple_of((block + 1 - count) * CHUNK, CHUNK), count * CHUNK)
        shape = (CHUNK, count * CHUNK)
        column = (block + 1 - count) * CHUNK + lax.broadcasted_iota(jnp.int32, shape, 1)
        row = block * CHUNK + lax.broadcasted_iota(jnp.int32, shape, 0)
        allowed = (column >= start_ref[rows, :]) & (column <= row)
        allowed = jnp.concatenate([allowed] * heads, axis=0)

        def one_by_one(values):
            return jnp.concatenate(
                [jnp.where(head_of == head, values, jnp.zeros((), BF16)) for head in range(heads)], axis=0
            )

        def side_by_side(values):
            total = values[:CHUNK]
            for head in range(1, heads):
                total = jnp.where(head_of == head, values[head * CHUNK : (head + 1) * CHUNK], total)
            return total

        query, grad = one_by_one(q_s[rows, :]), one_by_one(grad_ref[rows, :])
        keys, values = k_s[span, :], v_s[span, :]
        scores = lax.dot_general(query, keys, over_last, preferred_element_type=F32)
        scores = jnp.where(allowed, scores, NEG)
        prob = jnp.exp(scores - jnp.max(scores, axis=1, keepdims=True))
        prob = prob * (1.0 / jnp.sum(prob, axis=1, keepdims=True))
        prob_low = prob.astype(BF16)
        grad_prob = lax.dot_general(grad, values, over_last, preferred_element_type=F32)
        delta = jnp.sum(prob * grad_prob, axis=1, keepdims=True)
        grad_scores = (prob * (grad_prob - delta)).astype(BF16)
        dk_s[span, :] += lax.dot_general(grad_scores, query, over_first, preferred_element_type=F32)
        dv_s[span, :] += lax.dot_general(prob_low, grad, over_first, preferred_element_type=F32)
        att_ref[rows, :] = side_by_side(jnp.dot(prob_low, values, preferred_element_type=F32)).astype(BF16)
        grad_query = side_by_side(jnp.dot(grad_scores, keys, preferred_element_type=F32))
        out_ref[rows, :width] = turn(grad_query * HEAD ** (-0.5), rows, -1.0).astype(BF16)

    def one_block(block, carry):
        used = block + 1 - first_ref[block]
        for count in range(1, min(blocks, -(-(SEQ_MAX - 1) // CHUNK) + 1) + 1):
            pl.when(used == count)(functools.partial(window, block, count))
        return carry

    lax.fori_loop(0, blocks, one_block, 0)

    def finish(block, carry):
        rows = rows_at(block, CHUNK)
        out_ref[rows, width : 2 * width] = turn(dk_s[rows, :], rows, -1.0).astype(BF16)
        out_ref[rows, 2 * width :] = dv_s[rows, :].astype(BF16)
        return carry

    lax.fori_loop(0, blocks, finish, 0)


def attention(pre_qkv, grad_attended, tables, part, width):
    pack_len = grad_attended.shape[0]
    whole = pl.BlockSpec(memory_space=pltpu.VMEM)
    return pl.pallas_call(
        attention_body,
        grid=(1,),
        out_shape=(
            jax.ShapeDtypeStruct((pack_len, width), BF16),
            jax.ShapeDtypeStruct((pack_len, 3 * width), BF16),
        ),
        in_specs=[
            pl.BlockSpec(memory_space=pltpu.SMEM),
            pl.BlockSpec((pack_len, 3 * width), lambda step: (0, part), memory_space=pltpu.VMEM),
            pl.BlockSpec((pack_len, width), lambda step: (0, part), memory_space=pltpu.VMEM),
            whole,
            whole,
            whole,
        ],
        out_specs=(whole, whole),
        scratch_shapes=[pltpu.VMEM((pack_len, width), BF16)] * 3
        + [pltpu.VMEM((pack_len, width), F32)] * 2,
        compiler_params=pltpu.CompilerParams(vmem_limit_bytes=VMEM_BYTES),
        cost_estimate=NOTHING,
        name="attention",
    )(tables[0], pre_qkv, grad_attended, *tables[1:])


def tri(index):
    return index * (index + 1) // 2


def packed_rows(size):
    return tri(size // CHUNK) * CHUNK


def panels(size):
    for panel in range(size // PANEL):
        yield panel, (panel + 1) * PANEL, slice(panel * PANEL, (panel + 1) * PANEL)


def symmetric(lhs, rhs, size, epilogue):
    for panel, height, columns in panels(size):
        top = height - CHUNK
        epilogue(
            panel, 0, top, columns, jnp.dot(lhs[:top, :], rhs[:, columns], preferred_element_type=F32)
        )
        right = slice(columns.stop - CHUNK, columns.stop)
        epilogue(
            panel, top, height, right, jnp.dot(lhs[top:height, :], rhs[:, right], preferred_element_type=F32)
        )


def put_mirrored(ref, top, height, columns, values):
    ref[top:height, columns] = values
    if top == 0:
        above = height - CHUNK
        if above:
            ref[columns, :above] = values[:above, :].T
        ref[columns.start + CHUNK : columns.stop, above : above + CHUNK] = values[above:, CHUNK:].T


def gram_packed(x, xt_ref, size, packed_ref):
    depth = x.shape[0]
    for block in range(depth // CHUNK):
        part = slice(block * CHUNK, (block + 1) * CHUNK)
        xt_ref[:, part] = x[part, :].T
    for panel, height, columns in panels(size):
        product = jnp.dot(xt_ref[:height, :depth], x[:, columns], preferred_element_type=F32).astype(BF16)
        for half in range(PANEL // CHUNK):
            column = panel * (PANEL // CHUNK) + half
            rows = (column + 1) * CHUNK
            packed_ref[tri(column) * CHUNK : tri(column) * CHUNK + rows, :] = product[
                :rows, half * CHUNK : (half + 1) * CHUNK
            ]


def gram_body(x_ref, packed_ref, xt_s):
    gram_packed(x_ref, xt_s, x_ref.shape[1], packed_ref)


def owned_gram_body(me_ref, *refs):
    early, late, (x_ref, packed_ref, xt_s) = refs[:5], refs[5:13], refs[13:]
    pieces = [late[at : at + 2] for at in range(0, 8, 2)]
    block = early[0].shape[0]

    @pl.when((me_ref[0] == 0) | (me_ref[0] == 3))
    def from_early():
        at = 0
        for one in early:
            x_ref[at : at + one.shape[0], :] = one[...]
            at += one.shape[0]

    for owner, share in ((1, 1), (2, 3)):

        @pl.when(me_ref[0] == owner)
        def from_late(share=share):
            rows = pieces[0][0].shape[0] // share
            for at, (total, got) in enumerate(pieces):
                x_ref[at * rows : (at + 1) * rows, :] = (total[:rows, :] + got[:rows, :].astype(F32)).astype(BF16)
            x_ref[4 * rows :, :] = jnp.zeros((4 * (block - rows), x_ref.shape[1]), BF16)

    gram_packed(x_ref, xt_s, x_ref.shape[1], packed_ref)


def unpack(packed_ref, size, scale, exact_s, low_s):
    per_panel = PANEL // CHUNK
    for column in range(size // CHUNK):
        rows = (column + 1) * CHUNK
        at = tri(column) * CHUNK
        panel, half = column // per_panel, column % per_panel
        base = tri(panel) * PANEL
        lanes = slice(half * CHUNK, (half + 1) * CHUNK)
        cols = slice(column * CHUNK, (column + 1) * CHUNK)
        values = packed_ref[at : at + rows, :].astype(F32) * scale
        exact_s[base : base + rows, lanes] = values
        low = values.astype(BF16)
        low_s[:rows, cols] = low
        if column:
            low_s[cols, : rows - CHUNK] = low[: rows - CHUNK, :].T
        for other in range(half):
            left = panel * per_panel + other
            exact_s[base + column * CHUNK : base + rows, other * CHUNK : (other + 1) * CHUNK] = values[
                left * CHUNK : (left + 1) * CHUNK, :
            ].T


def iterate(x_s, exact_s, low_s, poly_s, mix_s, size, count):
    def one(step, carry):
        source, target = step % 2, (step + 1) % 2

        def exact_at(panel, top, height, columns):
            first = columns.start % PANEL
            lanes = slice(first, first + columns.stop - columns.start)
            return slice(tri(panel) * PANEL + top, tri(panel) * PANEL + height), lanes

        def poly_end(panel, top, height, columns, product):
            values = NS_B * exact_s[exact_at(panel, top, height, columns)] + NS_C * product
            put_mirrored(poly_s, top, height, columns, values.astype(BF16))

        symmetric(low_s, low_s, size, poly_end)

        def x_columns(panel, inner):
            columns = rows_at(panel, PANEL)
            product = jnp.dot(x_s[source], poly_s[:, columns], preferred_element_type=F32)
            x_s[target, :, columns] = (NS_A * x_s[source, :, columns].astype(F32) + product).astype(BF16)
            return inner

        lax.fori_loop(0, size // PANEL, x_columns, 0)

        @pl.when(step < count - 1)
        def next_gram():
            def mix_end(panel, top, height, columns, product):
                at = exact_at(panel, top, height, columns)
                exact_s[at] = (NS_A * NS_A) * exact_s[at] + (2.0 * NS_A) * product
                put_mirrored(mix_s, top, height, columns, product.astype(BF16))

            symmetric(low_s, poly_s, size, mix_end)

            def gram_end(panel, top, height, columns, product):
                at = exact_at(panel, top, height, columns)
                values = exact_s[at] + product
                exact_s[at] = values
                put_mirrored(low_s, top, height, columns, values.astype(BF16))

            symmetric(mix_s, poly_s, size, gram_end)

        return carry

    lax.fori_loop(0, count, one, 0)


def first_body(count, packed_ref, x_ref, x_out, packed_out, x_s, exact_s, low_s, poly_s, mix_s, packed_s, sems):
    size = x_ref.shape[1]
    load_x = pltpu.make_async_copy(x_ref, x_s.at[0], sems.at[0])
    load_packed = pltpu.make_async_copy(packed_ref, packed_s, sems.at[1])
    load_x.start()
    load_packed.start()
    load_packed.wait()
    trace = jnp.zeros((1, 1), F32)
    eye = lax.broadcasted_iota(jnp.int32, (CHUNK, CHUNK), 0) == lax.broadcasted_iota(
        jnp.int32, (CHUNK, CHUNK), 1
    )
    for column in range(size // CHUNK):
        at = tri(column) * CHUNK + column * CHUNK
        block = jnp.where(eye, packed_s[at : at + CHUNK, :].astype(F32), 0.0)
        trace = trace + jnp.sum(jnp.sum(block, axis=1, keepdims=True), axis=0, keepdims=True)
    inverse = 1.0 / (jnp.sqrt(trace) + 1e-7)
    unpack(packed_s, size, inverse * inverse, exact_s, low_s)
    load_x.wait()
    iterate(x_s, exact_s, low_s, poly_s, mix_s, size, count)
    depth = x_ref.shape[0]

    def scale_rows(block, carry):
        rows = rows_at(block, CHUNK)
        x_s[count % 2, rows, :] = (x_s[count % 2, rows, :].astype(F32) * inverse).astype(BF16)
        return carry

    lax.fori_loop(0, depth // CHUNK, scale_rows, 0)
    store_x = pltpu.make_async_copy(x_s.at[count % 2], x_out, sems.at[0])
    store_x.start()
    gram_packed(x_s.at[count % 2], poly_s, size, packed_s)
    store_packed = pltpu.make_async_copy(packed_s, packed_out, sems.at[1])
    store_packed.start()
    store_x.wait()
    store_packed.wait()


def second_body(count, from_ref, packed_ref, x_ref, *refs):
    outs, (x_s, exact_s, low_s, poly_s, mix_s, packed_s, sems, out_sems) = refs[:-8], refs[-8:]
    size = x_ref.shape[1]
    load_x = pltpu.make_async_copy(x_ref, x_s.at[0], sems.at[0])
    load_packed = pltpu.make_async_copy(packed_ref, packed_s, sems.at[1])
    load_x.start()
    load_packed.start()
    load_packed.wait()
    unpack(packed_s, size, 1.0, exact_s, low_s)
    load_x.wait()
    iterate(x_s, exact_s, low_s, poly_s, mix_s, size, count)
    stores = []
    for out in outs:
        unit = x_ref.shape[0] // out_sems.shape[0]
        for at in range(0, out.shape[0], unit):
            source = pl.ds(pl.multiple_of(from_ref[len(stores)], unit), unit)
            stores.append(
                pltpu.make_async_copy(
                    x_s.at[count % 2, source, :], out.at[at : at + unit, :], out_sems.at[len(stores)]
                )
            )
    for store in stores:
        store.start()
    for store in stores:
        store.wait()


def ns_scratch(depth, size):
    return [
        pltpu.VMEM((2, depth, size), BF16),
        pltpu.VMEM((tri(size // PANEL) * PANEL, PANEL), F32),
        pltpu.VMEM((size, size), BF16),
        pltpu.VMEM((size, size), BF16),
        pltpu.VMEM((size, size), BF16),
        pltpu.VMEM((packed_rows(size), CHUNK), BF16),
        pltpu.SemaphoreType.DMA((2,)),
    ]


def first_gram(rows, early=(), late=()):
    depth, size = rows
    vmem = pl.BlockSpec(memory_space=pltpu.VMEM)
    shapes = (jax.ShapeDtypeStruct((depth, size), BF16), jax.ShapeDtypeStruct((packed_rows(size), CHUNK), BF16))
    me = lax.axis_index("dp").astype(jnp.int32).reshape(1)
    return pl.pallas_call(
        owned_gram_body,
        out_shape=shapes,
        in_specs=[pl.BlockSpec(memory_space=pltpu.SMEM)] + [vmem] * (len(early) + len(late)),
        out_specs=(vmem, vmem),
        scratch_shapes=[pltpu.VMEM((size, depth), BF16)],
        compiler_params=pltpu.CompilerParams(vmem_limit_bytes=VMEM_BYTES),
        cost_estimate=NOTHING,
        name="gram",
    )(me, *early, *late)


def orthogonalize(rows, packed, source_rows, pieces, after_gram, beside_first, after_first_steps, after_first, beside_last):
    depth, size = rows.shape
    packed_shape = jax.ShapeDtypeStruct((packed_rows(size), CHUNK), BF16)
    x_shape = jax.ShapeDtypeStruct((depth, size), BF16)
    vmem = pl.BlockSpec(memory_space=pltpu.VMEM)
    hbm = pl.BlockSpec(memory_space=pl.ANY)
    params = pltpu.CompilerParams(vmem_limit_bytes=VMEM_BYTES)

    def gram_sum(packed, meanwhile):
        part = lax.psum_scatter(packed, "group", scatter_dimension=0, tiled=True)
        return lax.all_gather(after(part, *jax.tree.leaves(meanwhile)), "group", axis=0, tiled=True)

    if packed is None:
        packed = pl.pallas_call(
            gram_body,
            out_shape=packed_shape,
            in_specs=[vmem],
            out_specs=vmem,
            scratch_shapes=[pltpu.VMEM((size, depth), BF16)],
            compiler_params=params,
            cost_estimate=NOTHING,
            name="gram",
        )(rows)
    meanwhile = after_gram(packed)
    gathered = gram_sum(packed, meanwhile)
    first = beside_first(gathered, meanwhile)
    half_way, packed = pl.pallas_call(
        functools.partial(first_body, 2),
        out_shape=(x_shape, packed_shape),
        in_specs=[hbm, hbm],
        out_specs=(hbm, hbm),
        scratch_shapes=ns_scratch(depth, size),
        compiler_params=params,
        cost_estimate=NOTHING,
        name="first_steps",
    )(gathered, rows)
    first = after_first_steps(first, packed)
    packed = after(packed, *first)
    meanwhile = after_first(packed, first)
    gathered = gram_sum(packed, meanwhile)
    last = beside_last(gathered)
    results = pl.pallas_call(
        functools.partial(second_body, 3),
        out_shape=[jax.ShapeDtypeStruct((piece, size), BF16) for piece in pieces],
        in_specs=[pl.BlockSpec(memory_space=pltpu.SMEM), hbm, hbm],
        out_specs=[hbm] * len(pieces),
        scratch_shapes=ns_scratch(depth, size) + [pltpu.SemaphoreType.DMA((source_rows.shape[0],))],
        compiler_params=params,
        cost_estimate=NOTHING,
        name="last_steps",
    )(source_rows, gathered, half_way)
    return results, first, meanwhile, last


def two_by_two():
    return lax.axis_size("dp") == 4


def hop(values, bit, targets=range(4)):
    return lax.ppermute(values, "dp", [(t ^ bit, t) for t in targets])


def by_distance(parts):
    me = lax.axis_index("dp")
    return jnp.stack([lax.dynamic_index_in_dim(parts, me ^ r, 0, keepdims=False) for r in range(4)])


def gather_near(own):
    return own, hop(own, 1), hop(own, 2)


def gather_far(near):
    own, from_x, from_y = near
    half = own.shape[0] // 2
    first, second = hop(from_y[:half], 1), hop(from_x[half:], 2)
    return jnp.stack([own, from_x, from_y, jnp.concatenate([first, second], axis=0)])


def reduce_start(sent_x, kept_x, sent_y, kept_y):
    return kept_x, hop(sent_x, 1), kept_y, hop(sent_y, 2)


def reduce_next(state, *others):
    def body(*refs):
        outs = refs[4 + len(others) :]
        for k in range(2):
            total = refs[2 * k][...].astype(F32) + refs[2 * k + 1][...].astype(F32)
            outs[2 * k][...] = total
            outs[2 * k + 1][...] = total.astype(BF16)

    shapes = [(state[0].shape, dtype) for dtype in (F32, BF16)] * 2
    total_x, out_x, total_y, out_y = in_vmem(body, state, others, shapes, "reduce_next")
    return (total_x, hop(out_x, 2, [1, 2]), total_y, hop(out_y, 1, [1, 2])), (out_x, out_y)


def scatter_start(split):
    left_out, left, right_out, right = split
    return left, hop(left_out, 1), right, hop(right_out, 2)


def scatter_next(state, *others):
    half = state[0].shape[0] // 2

    def body(*refs):
        outs = refs[4 + len(others) :]
        for k in range(2):
            total = refs[2 * k][...].astype(F32) + refs[2 * k + 1][...].astype(F32)
            outs[2 * k][...] = total[:half]
            outs[2 * k + 1][...] = total[half:].astype(BF16)

    shapes = [((half, state[0].shape[1]), dtype) for dtype in (F32, BF16)] * 2
    left, left_out, right, right_out = in_vmem(body, state, others, shapes, "scatter_next")
    return (left, hop(left_out, 2), right, hop(right_out, 1)), (left_out, right_out)


def scatter_end(state, *others):
    left, left_in, right, right_in = state
    if others:
        left, right = after(left, *others), after(right, *others)
    return jnp.concatenate([left + left_in.astype(F32), right + right_in.astype(F32)], axis=0)


def scatter_momentum(state, moment, *others):
    rows, width = moment.shape
    half = rows // 2

    def body(*refs):
        left, left_in, right, right_in, moment_ref = refs[:5]
        own, full = refs[5 + len(others) :]
        for at, (one, got) in ((0, (left, left_in)), (half, (right, right_in))):
            total = one[...] + got[...].astype(F32)
            own[at : at + half, :] = total
            full[at : at + half, :] = (total + moment_ref[at : at + half, :]).astype(BF16)

    shapes = [((rows, width), F32), ((rows, width), BF16)]
    return in_vmem(body, [*state, moment], others, shapes, "momentum")


def owners_start(slots, owners, *others):
    rows, width = slots[0].shape
    half = rows // 2
    me = lax.axis_index("dp").astype(jnp.int32).reshape(1)

    def body(me_ref, first_ref, second_ref, *refs):
        outs = refs[len(others) :]
        for r in range(4):
            picked = jnp.where((me_ref[0] ^ r) == owners[0], first_ref[...], second_ref[...])
            if r < 3:
                outs[r][...] = picked
            else:
                outs[3][...], outs[4][...] = picked[:half], picked[half:]

    shapes = [((rows, width), BF16)] * 3 + [((half, width), BF16)] * 2
    own, to_x, to_y, first_hop, second_hop = sent = in_vmem(body, slots, others, shapes, "to_owners", me)
    first_hop, second_hop = hop(first_hop, 1, [t ^ 2 for t in owners]), hop(second_hop, 2, [t ^ 1 for t in owners])
    return (own, hop(to_x, 1, owners), hop(to_y, 2, owners), first_hop, second_hop), sent[1:]


def owners_end(state, owners, *others):
    own, from_x, from_y, first_hop, second_hop = state
    return own, from_x, from_y, hop(after(first_hop, *others), 2, owners), hop(second_hop, 1, owners)


def exchange_dp(own, to_x, to_y, first_hop, second_hop):
    first_hop, second_hop = hop(first_hop, 1), hop(second_hop, 2)
    from_x, from_y = hop(to_x, 1), hop(to_y, 2)
    first, second = hop(first_hop, 2), hop(second_hop, 1)
    return jnp.stack([own, from_x, from_y, jnp.concatenate([first, second], axis=0)])


def butterfly(values):
    for axis in ("group", "dp"):
        size, bit = lax.axis_size(axis), 1
        while bit < size:
            values = values + lax.ppermute(values, axis, [(i, i ^ bit) for i in range(size)])
            bit *= 2
    return values


def heads_aligned(unit):
    return unit == HEAD and lax.axis_size("group") % 3 != 0


def spread_qkv(own, unit):
    group_count = lax.axis_size("group")
    me = lax.axis_index("group")
    moved = jnp.stack(
        [
            lax.ppermute(
                own[j * unit : (j + 1) * unit], "group", [(g, (3 * g + j) % group_count) for g in range(group_count)]
            )
            for j in range(3)
        ]
    )
    return jnp.concatenate(
        [lax.dynamic_index_in_dim(moved, (me + group_count * i) % 3, 0, keepdims=False) for i in range(3)]
    )


def return_qkv(rows, unit):
    group_count = lax.axis_size("group")
    me = lax.axis_index("group")
    inverse = pow(group_count, -1, 3)
    parts = rows.reshape(3, unit, rows.shape[1])
    return jnp.concatenate(
        [
            lax.ppermute(
                lax.dynamic_index_in_dim(parts, ((j - me) * inverse) % 3, 0, keepdims=False),
                "group",
                [((3 * g + j) % group_count, g) for g in range(group_count)],
            )
            for j in range(3)
        ]
    )


def head_rows(matrix, heads):
    group_count = lax.axis_size("group")
    lead = matrix.shape[:-2]
    split = matrix.reshape(lead + (heads, group_count, HEAD, matrix.shape[-1]))
    picked = lax.dynamic_index_in_dim(split, lax.axis_index("group"), len(lead) + 1, keepdims=False)
    return picked.reshape(lead + (heads * HEAD, matrix.shape[-1]))


def spread_heads(rows, heads):
    group_count = lax.axis_size("group")
    lead = rows.shape[:-2]
    width = rows.shape[-1]
    part = rows.reshape(lead + (heads, 1, HEAD, width))
    empty = jnp.zeros(lead + (heads, group_count, HEAD, width), rows.dtype)
    placed = lax.dynamic_update_slice_in_dim(empty, part, lax.axis_index("group"), len(lead) + 1)
    return placed.reshape(lead + (heads * group_count * HEAD, width))


def shards(
    hidden_in,
    cotangent,
    segment_ids,
    weight_in,
    weight_back,
    moment_in,
    moment_back,
    norm_gain,
    norm_shift,
    bias_in,
    bias_out,
    vector_moment,
):
    model_width = hidden_in.shape[2]
    tokens = hidden_in.shape[1]
    data_count = lax.axis_size("dp")
    group_count = lax.axis_size("group")
    devices = data_count * group_count
    me_group = lax.axis_index("group")
    me = lax.axis_index("dp")
    unit = model_width // devices
    qkv_rows = 3 * unit
    ff_rows = FF // devices
    out_rows = unit
    heads = HEADS // group_count
    width = heads * HEAD
    fast = heads_aligned(unit) and two_by_two()
    everywhere = ("dp", "group")

    def dot(left, right):
        return jnp.dot(left, right, preferred_element_type=F32)

    def dot_last(left, right):
        return lax.dot_general(left, right, (((1,), (1,)), ((), ())), preferred_element_type=F32)

    def dot_first(left, right):
        return lax.dot_general(left, right, (((0,), (0,)), ((), ())), preferred_element_type=F32)

    x_float = hidden_in[0].astype(F32)
    centre = x_float - jnp.mean(x_float, axis=-1, keepdims=True)
    inverse_std = lax.rsqrt(jnp.mean(centre * centre, axis=-1, keepdims=True) + 1e-05)
    x_hat = centre * inverse_std
    normed_low = (x_hat * norm_gain + norm_shift).astype(BF16)
    grad_y = cotangent[0]
    parts = max(1, width // 128)
    lanes = width // parts
    w_in, w_back = weight_in[0], weight_back[0]
    m_in, m_back = MOMENTUM * moment_in[0], MOMENTUM * moment_back[0]
    position = positions(segment_ids[0])
    start = jnp.arange(position.shape[0], dtype=jnp.int32) - position
    tables = (start[::CHUNK] // CHUNK, start[:, None]) + rotary_lanes(position, lanes // HEAD)
    grad_y_float = grad_y.astype(F32)

    def to_parts(rows):
        split = rows.reshape((3, parts, lanes) + rows.shape[1:])
        return jnp.swapaxes(split, 0, 1).reshape(rows.shape)

    def from_parts(rows):
        split = rows.reshape((parts, 3, lanes) + rows.shape[1:])
        return jnp.swapaxes(split, 0, 1).reshape(rows.shape)

    normed_all = lax.all_gather(normed_low, "group", axis=0, tiled=True)
    if fast:
        w_up = gather_far(gather_near(w_in[qkv_rows:]))
        near_qkv = gather_near(spread_qkv(w_in[:qkv_rows], unit))
        grad_all = lax.all_gather(after(grad_y, normed_all, w_up, *near_qkv[1:], *tables), "group", axis=0, tiled=True)
    else:
        grad_all = lax.all_gather(grad_y, "group", axis=0, tiled=True)
        w_up = lax.all_gather(w_in[qkv_rows:], "dp", axis=0, tiled=True)
    w_up = w_up.reshape(data_count * ff_rows, model_width)

    bias_up = lax.dynamic_index_in_dim(
        bias_in[3 * model_width :].reshape(data_count, group_count, ff_rows), me_group, 1, keepdims=False
    )
    bias_up = (by_distance(bias_up) if fast else bias_up).reshape(data_count * ff_rows)
    bias_qkv = bias_in[: 3 * model_width].reshape(3 * heads, group_count, HEAD)
    bias_qkv = to_parts(lax.dynamic_index_in_dim(bias_qkv, me_group, 1, keepdims=False).reshape(3 * width))
    activated, slope = up_forward(normed_all, w_up, bias_up)
    if fast:
        near_back = gather_near(after(w_back, *near_qkv[1:]))
        own, from_x, from_y = near_qkv
        w_qkv = by_distance(gather_far((own, after(from_x, activated), after(from_y, activated))))
        own, from_x, from_y = near_back
        all_back = gather_far((own, after(from_x, activated), after(from_y, activated)))
        w_out = by_distance(all_back[:, :out_rows]).reshape(width, model_width)
        w_down = all_back[:, out_rows:].reshape(data_count * ff_rows, model_width)
    else:
        all_qkv = lax.all_gather(w_in[:qkv_rows], everywhere, axis=0, tiled=True)
        w_qkv = head_rows(all_qkv.reshape(3, model_width, model_width), heads)
        w_out = head_rows(lax.all_gather(w_back[:out_rows], everywhere, axis=0, tiled=True), heads)
        w_down = lax.all_gather(w_back[out_rows:], "dp", axis=0, tiled=True)
    w_qkv = to_parts(w_qkv.reshape(3 * width, model_width))
    pre_qkv = project(normed_all, w_qkv, bias_qkv, F32, "project_qkv")
    branch_up = dot(activated, w_down)
    grad_all = after(grad_all, activated, slope, pre_qkv, w_down, w_out, branch_up)

    term_down = weight_grad(activated, grad_all, "grad_down", fast)
    if fast:
        sum_down = scatter_start(term_down)
        m_qkv = spread_qkv(after(m_in[:qkv_rows], term_down[0]), unit)
        slope = after(slope, *term_down)
    grad_pre_up = up_backward(grad_all, slope, w_down)
    term_up = weight_grad(grad_pre_up, normed_all, "grad_up", fast)
    late_w_out = w_out
    if fast:
        sum_up = scatter_start(term_up)
        sum_down, flying = scatter_next(sum_down, *term_up)
        late_w_out = after(w_out, *flying)
    grad_attended = project(grad_all, late_w_out, jnp.zeros((width,), F32), BF16, "project_grad")
    ready = ()

    attended, grad_pre_qkv, term_qkv, term_out, sum_att = [], [], [], [], []
    for part in range(parts):
        one, one_grad = attention(pre_qkv, after(grad_attended, *ready), tables, part, lanes)
        attended.append(one)
        grad_pre_qkv.append(one_grad)
        if not fast:
            ready = (one,)
            term_qkv.append(dot_first(one_grad, normed_all).astype(BF16))
            term_out.append(dot_first(one, grad_all).astype(BF16))
            continue
        if part == 0:
            sum_up, flying = scatter_next(sum_up, one)
            own_down, full_down = scatter_momentum(sum_down, m_back[out_rows:], one)
            one_grad = after(one_grad, full_down, *flying)
        else:
            first_half, flying = reduce_next(sum_att[0], one)
            one_grad = after(one_grad, *flying)
        one_qkv, one_out, *split = weight_grads_plus(
            one_grad,
            normed_all,
            one,
            grad_all,
            m_qkv,
            m_back[:out_rows],
            part,
            heads,
        )
        sum_att.append(reduce_start(*split))
        if part == 0:
            own_up, full_up = scatter_momentum(sum_up, m_in[qkv_rows:], split[0])
            early, ready = owners_start([full_up, full_down], [0, 3])
        term_qkv.append(one_qkv)
        term_out.append(one_out)

    if fast:
        early = owners_end(early, [0, 3], split[0])
        second_half, _ = reduce_next(sum_att[1])
        owned, packed = first_gram((data_count * ff_rows, model_width), early, (*first_half, *second_half))
    else:
        packed = None
        term_qkv = from_parts(jnp.concatenate(term_qkv))
        term_out = jnp.concatenate(term_out)
        grad_w_qkv = lax.psum_scatter(
            spread_heads(term_qkv.reshape(3, width, model_width), heads).reshape(3 * model_width, model_width),
            everywhere,
            scatter_dimension=0,
            tiled=True,
        ).astype(F32)
        grad_w_out = lax.psum_scatter(
            spread_heads(term_out, heads), everywhere, scatter_dimension=0, tiled=True
        ).astype(F32)
        own_up = lax.psum_scatter(term_up, "dp", scatter_dimension=0, tiled=True).astype(F32)
        own_down = lax.psum_scatter(term_down, "dp", scatter_dimension=0, tiled=True).astype(F32)
        slots = [m_in[qkv_rows:] + own_up, m_in[:qkv_rows] + grad_w_qkv, m_back[:out_rows] + grad_w_out]
        slots = slots + [m_back[out_rows:] + own_down] + [jnp.zeros((0, model_width))] * (data_count - 4)
        slots = [jnp.pad(rows.astype(BF16), ((0, ff_rows - rows.shape[0]), (0, 0))) for rows in slots]
        owned = lax.all_to_all(jnp.stack(slots), "dp", split_axis=0, concat_axis=0, tiled=True)
        owned = owned.reshape(data_count * ff_rows, model_width)

    def after_gram(packed):
        late_qkv, late_up = jnp.concatenate(grad_pre_qkv, axis=1), after(grad_pre_up, packed)
        late_qkv = after(late_qkv, packed)
        normed_part = dot(late_qkv, w_qkv) + dot(late_up, w_up)
        split = ()
        if fast:
            terms = [from_parts(jnp.concatenate(term_qkv)), jnp.concatenate(term_out)]
            terms = [after(one, packed).reshape(data_count, -1, model_width) for one in terms]
            terms = by_distance(jnp.concatenate(terms, axis=1)).reshape(2, 2, 2, unit * 2, model_width)
            split = terms[:, 1, 0], terms[:, 0, 0], terms[1, :, 1], terms[0, :, 1]
            split = [one.reshape(4 * unit, model_width) for one in split]
        branch_part = dot(after(attended_all, packed), w_out) + branch_up
        return normed_part.astype(BF16), late_qkv, late_up, split, branch_part.astype(BF16)

    kept = [None]
    attended_all = jnp.concatenate(attended, axis=1)

    def beside_first(gathered, meanwhile):
        kept.extend(meanwhile[1:])
        if fast:
            split = [after(one, gathered) for one in kept[3]]
            kept.append(scatter_start(split))
        return (lax.psum_scatter(after(meanwhile[0], gathered), "group", scatter_dimension=0, tiled=True),)

    def after_first_steps(first, packed):
        if not fast:
            return first
        state, flying = scatter_next(kept[5], packed)
        kept.append(state)
        return first + flying

    def after_first(packed, first):
        grad_normed = first[0].astype(F32)
        grad_x_hat = grad_normed * norm_gain
        grad_hidden = grad_y_float + inverse_std * (
            grad_x_hat
            - jnp.mean(grad_x_hat, axis=-1, keepdims=True)
            - x_hat * jnp.mean(grad_x_hat * x_hat, axis=-1, keepdims=True)
        )
        if fast:
            own = scatter_end(kept[6])
            own_qkv = return_qkv(own[:qkv_rows].astype(BF16), unit).astype(F32)
            own_out = own[qkv_rows:]
        else:
            own_qkv, own_out = grad_w_qkv, grad_w_out
        grad_in = jnp.concatenate([own_qkv, own_up])
        grad_back = jnp.concatenate([own_out, own_down])
        grads = grad_in, grad_back, m_in + grad_in, m_back + grad_back
        sums_up = jnp.sum(kept[2].astype(F32), axis=0).reshape(data_count, ff_rows)
        sums_qkv = jnp.sum(kept[1].astype(F32), axis=0)
        vector_local = jnp.concatenate(
            [
                jnp.sum(grad_normed * x_hat, axis=0),
                jnp.sum(grad_normed, axis=0),
                placed(from_parts(sums_qkv), 3 * heads, HEAD),
                placed(by_distance(sums_up) if fast else sums_up, data_count, ff_rows),
                jnp.sum(grad_y_float, axis=0),
            ]
        )
        vector_grad = butterfly(vector_local)
        return grad_hidden, vector_grad, *grads

    def beside_last(gathered):
        return (lax.psum_scatter(after(kept[4], gathered), "group", scatter_dimension=0, tiled=True),)

    def placed(sums, lead, size):
        empty = jnp.zeros((lead, group_count, size), F32)
        return lax.dynamic_update_slice_in_dim(empty, sums.reshape(lead, 1, size), me_group, 1).reshape(-1)

    if fast:
        distance, run = jnp.divmod(jnp.arange(4 * ff_rows // unit), ff_rows // unit)
        holder = me ^ distance
        kind, head = jnp.divmod(3 * holder + jnp.minimum(run, 2), heads)
        per_part = heads // parts
        of_qkv = (head // per_part) * 3 * lanes + kind * lanes + (head % per_part) * HEAD
        source_rows = jnp.where(me == 1, of_qkv, jnp.where(me == 2, holder * unit, distance * ff_rows + run * unit))
        pieces = [ff_rows] * 3 + [ff_rows // 2] * 2
    else:
        source_rows = jnp.arange(0, data_count * ff_rows, ff_rows)
        pieces = [data_count * ff_rows]
    results, _, meanwhile, (branch,) = orthogonalize(
        owned, packed, source_rows.astype(jnp.int32), pieces, after_gram, beside_first, after_first_steps, after_first, beside_last
    )
    grad_hidden, vector_grad, grad_in, grad_back, moment_in_new, moment_back_new = meanwhile
    block_out = (x_float + branch.astype(F32) + bias_out).astype(BF16)
    if fast:
        returned = by_distance(exchange_dp(*results))
        o_qkv = return_qkv(returned[1, :qkv_rows], unit)
    else:
        result = results[0].reshape(data_count, ff_rows, model_width)
        returned = lax.all_to_all(result, "dp", split_axis=0, concat_axis=0, tiled=True)
        o_qkv = returned[1, :qkv_rows]

    def step_of(rows, scale):
        return -scale * rows.astype(F32)

    scale_ff = math.sqrt(1.0 * FF)
    step_in = jnp.concatenate(
        [step_of(o_qkv, math.sqrt(3.0 * model_width)), step_of(returned[0], scale_ff)], axis=0
    )[None]
    step_back = jnp.concatenate(
        [step_of(returned[2, :out_rows], math.sqrt(1.0 * model_width)), step_of(returned[3], scale_ff)], axis=0
    )[None]
    bias_out_grad = vector_grad[vector_grad.shape[0] - model_width :]
    vector_moment_new = MOMENTUM * vector_moment + vector_grad
    vector_step = -(0.2 / math.sqrt(tokens * devices)) * vector_moment_new
    return (
        block_out[None],
        grad_hidden[None],
        grad_in[None],
        grad_back[None],
        moment_in_new[None],
        moment_back_new[None],
        step_in,
        step_back,
        vector_grad,
        vector_moment_new,
        vector_step,
        bias_out_grad,
    )


def solution(mesh):
    tokens_spec = P("dp", "group", None)
    blocks_spec = P(("dp", "group"), None, None)
    in_specs = (
        (tokens_spec, tokens_spec, P("dp", None))
        + (blocks_spec,) * 4
        + (P(),) * 5
    )
    out_specs = (tokens_spec, tokens_spec) + (blocks_spec,) * 6 + (P(),) * 4
    return jax.shard_map(shards, mesh=mesh, in_specs=in_specs, out_specs=out_specs, check_vma=False)
```

```python
import functools
import math

import jax
import jax.numpy as jnp
from jax import lax
from jax.experimental import pallas as pl
from jax.experimental.pallas import tpu as pltpu
from jax.sharding import PartitionSpec as P

HEADS = 32
HEAD = 64
ROT = 32
FF = 8192
SEQ_MAX = 1024
NEG = -1e30
NS_A = 3.4445
NS_B = -4.775
NS_C = 2.0315
MOMENTUM = 0.95
F32 = jnp.float32
BF16 = jnp.bfloat16
CHUNK = 256
PANEL = 512
VMEM_BYTES = 61 * 2**20
MATMUL_BYTES = 60 * 2**20


def positions(segments):
    index_all = jnp.arange(segments.shape[0], dtype=jnp.int32)
    previous = jnp.concatenate([jnp.full((1,), -1, jnp.int32), segments[:-1]])
    starts = jnp.where(segments != previous, index_all, 0)
    return index_all - lax.cummax(starts, axis=0)


def gelu_and_slope(values):
    square = values * values
    bent = jnp.tanh(0.7978845608028654 * (values + 0.044715 * values * square))
    inner_slope = 0.7978845608028654 * (1.0 + 3.0 * 0.044715 * square)
    half = 0.5 * (1.0 + bent)
    return values * half, half + 0.5 * values * (1.0 - bent * bent) * inner_slope


def rotary_lanes(position, heads):
    half_rot = ROT // 2
    freq = jnp.exp(jnp.arange(half_rot, dtype=F32) * (-2.0 * math.log(10000.0) / ROT))
    angle = position.astype(F32)[:, None] * freq[None, :]
    cos, sin = jnp.cos(angle), jnp.sin(angle)
    rest = (position.shape[0], HEAD - ROT)
    cos_head = jnp.concatenate([cos, cos, jnp.ones(rest, F32)], axis=1)
    sin_head = jnp.concatenate([-sin, sin, jnp.zeros(rest, F32)], axis=1)
    return jnp.tile(cos_head, (1, heads)), jnp.tile(sin_head, (1, heads))


def after(values, *others):
    return pl.pallas_call(
        lambda *refs: None,
        out_shape=jax.ShapeDtypeStruct(values.shape, values.dtype),
        in_specs=[pl.BlockSpec(memory_space=pl.ANY)] * (1 + len(others)),
        out_specs=pl.BlockSpec(memory_space=pl.ANY),
        input_output_aliases={0: 0},
        name="after",
    )(values, *others)


def over(left, right, axes):
    return lax.dot_general(left, right, (axes, ((), ())), preferred_element_type=F32)


NOTHING = pl.CostEstimate(flops=0, bytes_accessed=0, transcendentals=0)
ROWS = ((1,), (1,))
TOKENS = ((0,), (0,))


def by_rows(body, blocked, whole, outs, rows, name):
    steps = blocked[0].shape[0] // rows
    return pl.pallas_call(
        body,
        grid=(steps,),
        in_specs=[pl.BlockSpec((rows, one.shape[1]), lambda step: (step, 0)) for one in blocked]
        + [
            pl.BlockSpec(one.shape, lambda step, rank=one.ndim: (0,) * rank, pipeline_mode=pl.Buffered(1))
            for one in whole
        ],
        out_specs=tuple(pl.BlockSpec((rows, width), lambda step: (step, 0)) for width, _ in outs),
        out_shape=tuple(jax.ShapeDtypeStruct((steps * rows, width), dtype) for width, dtype in outs),
        compiler_params=pltpu.CompilerParams(vmem_limit_bytes=MATMUL_BYTES),
        cost_estimate=NOTHING,
        name=name,
    )(*blocked, *whole)


def by_columns(body, whole, blocked, outs, columns, name, scratch=(), scalar=None):
    steps = blocked[0].shape[1] // columns
    return pl.pallas_call(
        body,
        grid=(steps,),
        in_specs=([] if scalar is None else [pl.BlockSpec(memory_space=pltpu.SMEM)])
        + [pl.BlockSpec(one.shape, lambda step: (0, 0), pipeline_mode=pl.Buffered(1)) for one in whole]
        + [pl.BlockSpec((one.shape[0], columns), lambda step: (0, step)) for one in blocked],
        out_specs=tuple(pl.BlockSpec((rows, columns), lambda step: (0, step)) for rows, _ in outs),
        out_shape=tuple(jax.ShapeDtypeStruct((rows, steps * columns), dtype) for rows, dtype in outs),
        scratch_shapes=list(scratch),
        compiler_params=pltpu.CompilerParams(vmem_limit_bytes=MATMUL_BYTES),
        cost_estimate=NOTHING,
        name=name,
    )(*([] if scalar is None else [scalar]), *whole, *blocked)


def in_vmem(body, ins, others, outs, name, scalar=None):
    vmem = pl.BlockSpec(memory_space=pltpu.VMEM)
    first = [] if scalar is None else [pl.BlockSpec(memory_space=pltpu.SMEM)]
    return pl.pallas_call(
        body,
        in_specs=first + [vmem] * len(ins) + [pl.BlockSpec(memory_space=pl.ANY)] * len(others),
        out_specs=[vmem] * len(outs),
        out_shape=[jax.ShapeDtypeStruct(shape, dtype) for shape, dtype in outs],
        compiler_params=pltpu.CompilerParams(vmem_limit_bytes=MATMUL_BYTES),
        cost_estimate=NOTHING,
        name=name,
    )(*([] if scalar is None else [scalar]), *ins, *others)


def up_forward(normed, w_up, bias):
    def body(x_ref, w_ref, b_ref, act_ref, slope_ref):
        act, slope = gelu_and_slope(over(x_ref[...], w_ref[...], ROWS) + b_ref[...])
        act_ref[...] = act.astype(BF16)
        slope_ref[...] = slope.astype(BF16)

    units = w_up.shape[0]
    return by_rows(body, [normed], [w_up, bias[None]], [(units, BF16), (units, BF16)], 256, "up_forward")


def up_backward(grad, slope, w_down):
    def body(g_ref, s_ref, w_ref, out_ref):
        out_ref[...] = (over(g_ref[...], w_ref[...], ROWS) * s_ref[...].astype(F32)).astype(BF16)

    return by_rows(body, [grad, slope], [w_down], [(w_down.shape[0], BF16)], 512, "up_backward")[0]


def project(x, w, bias, dtype, name):
    def body(x_ref, w_ref, b_ref, out_ref):
        out_ref[...] = (over(x_ref[...], w_ref[...], ROWS) + b_ref[...]).astype(dtype)

    return by_rows(body, [x], [w, bias[None]], [(w.shape[0], dtype)], 512, name)[0]


def weight_grad(left, right, name, split=False):
    tokens, rows = left.shape
    quarter = rows // 8 if split else rows

    def body(l_ref, r_ref, *refs):
        t_s = refs[-1]

        @pl.when(pl.program_id(0) == 0)
        def turn_over():
            for block in range(0, tokens, 256):
                t_s[:, block : block + 256] = l_ref[block : block + 256, :].T

        product = jnp.dot(t_s[...], r_ref[...], preferred_element_type=F32).astype(BF16)
        if not split:
            refs[0][...] = product
            return
        for block in range(4):
            for half in range(2):
                y, x = block // 2, block % 2
                sent, at = (x, y) if half == 0 else (y, x)
                source = (2 * block + half) * quarter
                refs[2 * half + 1 - sent][at * quarter : (at + 1) * quarter, :] = product[source : source + quarter, :]

    scratch = [pltpu.VMEM((rows, tokens), BF16)]
    outs = [(2 * quarter, BF16)] * 4 if split else [(rows, BF16)]
    results = by_columns(body, [left], [right], outs, 512, name, scratch)
    return results if split else results[0]


def weight_grads_plus(left, right, other_left, other_right, moment, other_moment, part, heads):
    tokens = left.shape[0]
    rows, other_rows = left.shape[1], other_left.shape[1]
    half, other_half = rows // 2, other_rows // 2
    per_part = other_rows // HEAD
    me = lax.axis_index("dp").astype(jnp.int32).reshape(1)

    def body(
        me_ref, l_ref, o_ref, r_ref, q_ref, m_ref, n_ref, out_ref, other_ref, sent_x, kept_x, sent_y, kept_y, t_s, f_s, g_s
    ):
        @pl.when(pl.program_id(0) == 0)
        def turn_over():
            for block in range(0, tokens, 256):
                t_s[:rows, block : block + 256] = l_ref[block : block + 256, :].T
                t_s[rows:, block : block + 256] = o_ref[block : block + 256, :].T

        f_s[...] = jnp.dot(t_s[:rows, :], r_ref[...], preferred_element_type=F32)
        out_ref[...] = f_s[...].astype(BF16)
        g_s[...] = jnp.dot(t_s[rows:, :], q_ref[...], preferred_element_type=F32)
        other_ref[...] = g_s[...].astype(BF16)
        for i in range(3):
            chunk = 3 * me_ref[0] + i
            kind, head = chunk // heads, chunk % heads

            @pl.when(head // per_part == part)
            def add_qkv(i=i, kind=kind, head=head):
                at = pl.ds(pl.multiple_of(kind * other_rows + (head % per_part) * HEAD, HEAD), HEAD)
                f_s[at, :] += m_ref[i * HEAD : (i + 1) * HEAD, :]

        @pl.when(me_ref[0] // per_part == part)
        def add_out():
            at = pl.ds(pl.multiple_of((me_ref[0] % per_part) * HEAD, HEAD), HEAD)
            g_s[at, :] += n_ref[...]

        full, other = f_s[...].astype(BF16), g_s[...].astype(BF16)
        nothing = jnp.zeros((half - other_half, other.shape[1]), BF16)
        for at, (sent, kept, mine) in enumerate(
            ((sent_x, kept_x, (me_ref[0] & 1) == 1), (sent_y, kept_y, (me_ref[0] & 2) == 0))
        ):
            first = full[at * half : (at + 1) * half]
            second = jnp.concatenate([other[at * other_half : (at + 1) * other_half], nothing], axis=0)
            sent[...] = jnp.where(mine, second, first)
            kept[...] = jnp.where(mine, first, second)

    columns = 512
    return by_columns(
        body,
        [left, other_left],
        [right, other_right, moment, other_moment],
        [(rows, BF16), (other_rows, BF16)] + [(half, BF16)] * 4,
        columns,
        "weight_grads_plus",
        [
            pltpu.VMEM((rows + other_rows, tokens), BF16),
            pltpu.VMEM((rows, columns), F32),
            pltpu.VMEM((other_rows, columns), F32),
        ],
        me,
    )


def rows_at(index, size):
    return pl.ds(pl.multiple_of(index * size, size), size)


def attention_body(
    first_ref, pre_ref, grad_ref, start_ref, cos_ref, sin_ref, att_ref, out_ref, q_s, k_s, v_s, dk_s, dv_s
):
    pack_len, width = grad_ref.shape
    heads = width // HEAD
    blocks = pack_len // CHUNK
    lane = lax.broadcasted_iota(jnp.int32, (CHUNK, width), 1)
    low_half = lane % HEAD < ROT // 2
    head_of = lane // HEAD

    def turn(values, rows, sign):
        swapped = jnp.where(
            low_half, pltpu.roll(values, width - ROT // 2, 1), pltpu.roll(values, ROT // 2, 1)
        )
        return values * cos_ref[rows, :] + (sign * sin_ref[rows, :]) * swapped

    def prepare(block, carry):
        rows = rows_at(block, CHUNK)
        query = turn(pre_ref[rows, :width], rows, 1.0).astype(BF16)
        q_s[rows, :] = (query.astype(F32) * HEAD ** (-0.5)).astype(BF16)
        k_s[rows, :] = turn(pre_ref[rows, width : 2 * width], rows, 1.0).astype(BF16)
        v_s[rows, :] = pre_ref[rows, 2 * width :].astype(BF16)
        dk_s[rows, :] = jnp.zeros((CHUNK, width), F32)
        dv_s[rows, :] = jnp.zeros((CHUNK, width), F32)
        return carry

    lax.fori_loop(0, blocks, prepare, 0)
    over_last = (((1,), (1,)), ((), ()))
    over_first = (((0,), (0,)), ((), ()))

    def window(block, count):
        rows = rows_at(block, CHUNK)
        span = pl.ds(pl.multiple_of((block + 1 - count) * CHUNK, CHUNK), count * CHUNK)
        shape = (CHUNK, count * CHUNK)
        column = (block + 1 - count) * CHUNK + lax.broadcasted_iota(jnp.int32, shape, 1)
        row = block * CHUNK + lax.broadcasted_iota(jnp.int32, shape, 0)
        allowed = (column >= start_ref[rows, :]) & (column <= row)
        allowed = jnp.concatenate([allowed] * heads, axis=0)

        def one_by_one(values):
            return jnp.concatenate(
                [jnp.where(head_of == head, values, jnp.zeros((), BF16)) for head in range(heads)], axis=0
            )

        def side_by_side(values):
            total = values[:CHUNK]
            for head in range(1, heads):
                total = jnp.where(head_of == head, values[head * CHUNK : (head + 1) * CHUNK], total)
            return total

        query, grad = one_by_one(q_s[rows, :]), one_by_one(grad_ref[rows, :])
        keys, values = k_s[span, :], v_s[span, :]
        scores = lax.dot_general(query, keys, over_last, preferred_element_type=F32)
        scores = jnp.where(allowed, scores, NEG)
        prob = jnp.exp(scores - jnp.max(scores, axis=1, keepdims=True))
        prob = prob * (1.0 / jnp.sum(prob, axis=1, keepdims=True))
        prob_low = prob.astype(BF16)
        grad_prob = lax.dot_general(grad, values, over_last, preferred_element_type=F32)
        delta = jnp.sum(prob * grad_prob, axis=1, keepdims=True)
        grad_scores = (prob * (grad_prob - delta)).astype(BF16)
        dk_s[span, :] += lax.dot_general(grad_scores, query, over_first, preferred_element_type=F32)
        dv_s[span, :] += lax.dot_general(prob_low, grad, over_first, preferred_element_type=F32)
        att_ref[rows, :] = side_by_side(jnp.dot(prob_low, values, preferred_element_type=F32)).astype(BF16)
        grad_query = side_by_side(jnp.dot(grad_scores, keys, preferred_element_type=F32))
        out_ref[rows, :width] = turn(grad_query * HEAD ** (-0.5), rows, -1.0).astype(BF16)

    def one_block(block, carry):
        used = block + 1 - first_ref[block]
        for count in range(1, min(blocks, -(-(SEQ_MAX - 1) // CHUNK) + 1) + 1):
            pl.when(used == count)(functools.partial(window, block, count))
        return carry

    lax.fori_loop(0, blocks, one_block, 0)

    def finish(block, carry):
        rows = rows_at(block, CHUNK)
        out_ref[rows, width : 2 * width] = turn(dk_s[rows, :], rows, -1.0).astype(BF16)
        out_ref[rows, 2 * width :] = dv_s[rows, :].astype(BF16)
        return carry

    lax.fori_loop(0, blocks, finish, 0)


def attention(pre_qkv, grad_attended, tables, part, width):
    pack_len = grad_attended.shape[0]
    whole = pl.BlockSpec(memory_space=pltpu.VMEM)
    return pl.pallas_call(
        attention_body,
        grid=(1,),
        out_shape=(
            jax.ShapeDtypeStruct((pack_len, width), BF16),
            jax.ShapeDtypeStruct((pack_len, 3 * width), BF16),
        ),
        in_specs=[
            pl.BlockSpec(memory_space=pltpu.SMEM),
            pl.BlockSpec((pack_len, 3 * width), lambda step: (0, part), memory_space=pltpu.VMEM),
            pl.BlockSpec((pack_len, width), lambda step: (0, part), memory_space=pltpu.VMEM),
            whole,
            whole,
            whole,
        ],
        out_specs=(whole, whole),
        scratch_shapes=[pltpu.VMEM((pack_len, width), BF16)] * 3
        + [pltpu.VMEM((pack_len, width), F32)] * 2,
        compiler_params=pltpu.CompilerParams(vmem_limit_bytes=VMEM_BYTES),
        cost_estimate=NOTHING,
        name="attention",
    )(tables[0], pre_qkv, grad_attended, *tables[1:])


def tri(index):
    return index * (index + 1) // 2


def packed_rows(size):
    return tri(size // CHUNK) * CHUNK


def panels(size):
    for panel in range(size // PANEL):
        yield panel, (panel + 1) * PANEL, slice(panel * PANEL, (panel + 1) * PANEL)


def symmetric(lhs, rhs, size, epilogue):
    for panel, height, columns in panels(size):
        top = height - CHUNK
        epilogue(
            panel, 0, top, columns, jnp.dot(lhs[:top, :], rhs[:, columns], preferred_element_type=F32)
        )
        right = slice(columns.stop - CHUNK, columns.stop)
        epilogue(
            panel, top, height, right, jnp.dot(lhs[top:height, :], rhs[:, right], preferred_element_type=F32)
        )


def put_mirrored(ref, top, height, columns, values):
    ref[top:height, columns] = values
    if top == 0:
        above = height - CHUNK
        if above:
            ref[columns, :above] = values[:above, :].T
        ref[columns.start + CHUNK : columns.stop, above : above + CHUNK] = values[above:, CHUNK:].T


def gram_packed(x, xt_ref, size, packed_ref):
    depth = x.shape[0]
    for block in range(depth // CHUNK):
        part = slice(block * CHUNK, (block + 1) * CHUNK)
        xt_ref[:, part] = x[part, :].T
    for panel, height, columns in panels(size):
        product = jnp.dot(xt_ref[:height, :depth], x[:, columns], preferred_element_type=F32).astype(BF16)
        for half in range(PANEL // CHUNK):
            column = panel * (PANEL // CHUNK) + half
            rows = (column + 1) * CHUNK
            packed_ref[tri(column) * CHUNK : tri(column) * CHUNK + rows, :] = product[
                :rows, half * CHUNK : (half + 1) * CHUNK
            ]


def gram_body(x_ref, packed_ref, xt_s):
    gram_packed(x_ref, xt_s, x_ref.shape[1], packed_ref)


def owned_gram_body(me_ref, *refs):
    early, late, (x_ref, packed_ref, xt_s) = refs[:5], refs[5:13], refs[13:]
    pieces = [late[at : at + 2] for at in range(0, 8, 2)]
    block = early[0].shape[0]

    @pl.when((me_ref[0] == 0) | (me_ref[0] == 3))
    def from_early():
        at = 0
        for one in early:
            x_ref[at : at + one.shape[0], :] = one[...]
            at += one.shape[0]

    for owner, share in ((1, 1), (2, 3)):

        @pl.when(me_ref[0] == owner)
        def from_late(share=share):
            rows = pieces[0][0].shape[0] // share
            for at, (total, got) in enumerate(pieces):
                x_ref[at * rows : (at + 1) * rows, :] = (total[:rows, :] + got[:rows, :].astype(F32)).astype(BF16)
            x_ref[4 * rows :, :] = jnp.zeros((4 * (block - rows), x_ref.shape[1]), BF16)

    gram_packed(x_ref, xt_s, x_ref.shape[1], packed_ref)


def unpack(packed_ref, size, scale, exact_s, low_s):
    per_panel = PANEL // CHUNK
    for column in range(size // CHUNK):
        rows = (column + 1) * CHUNK
        at = tri(column) * CHUNK
        panel, half = column // per_panel, column % per_panel
        base = tri(panel) * PANEL
        lanes = slice(half * CHUNK, (half + 1) * CHUNK)
        cols = slice(column * CHUNK, (column + 1) * CHUNK)
        values = packed_ref[at : at + rows, :].astype(F32) * scale
        exact_s[base : base + rows, lanes] = values
        low = values.astype(BF16)
        low_s[:rows, cols] = low
        if column:
            low_s[cols, : rows - CHUNK] = low[: rows - CHUNK, :].T
        for other in range(half):
            left = panel * per_panel + other
            exact_s[base + column * CHUNK : base + rows, other * CHUNK : (other + 1) * CHUNK] = values[
                left * CHUNK : (left + 1) * CHUNK, :
            ].T


def iterate(x_s, exact_s, low_s, poly_s, mix_s, size, count):
    def one(step, carry):
        source, target = step % 2, (step + 1) % 2

        def exact_at(panel, top, height, columns):
            first = columns.start % PANEL
            lanes = slice(first, first + columns.stop - columns.start)
            return slice(tri(panel) * PANEL + top, tri(panel) * PANEL + height), lanes

        def poly_end(panel, top, height, columns, product):
            values = NS_B * exact_s[exact_at(panel, top, height, columns)] + NS_C * product
            put_mirrored(poly_s, top, height, columns, values.astype(BF16))

        symmetric(low_s, low_s, size, poly_end)

        def x_columns(panel, inner):
            columns = rows_at(panel, PANEL)
            product = jnp.dot(x_s[source], poly_s[:, columns], preferred_element_type=F32)
            x_s[target, :, columns] = (NS_A * x_s[source, :, columns].astype(F32) + product).astype(BF16)
            return inner

        lax.fori_loop(0, size // PANEL, x_columns, 0)

        @pl.when(step < count - 1)
        def next_gram():
            def mix_end(panel, top, height, columns, product):
                at = exact_at(panel, top, height, columns)
                exact_s[at] = (NS_A * NS_A) * exact_s[at] + (2.0 * NS_A) * product
                put_mirrored(mix_s, top, height, columns, product.astype(BF16))

            symmetric(low_s, poly_s, size, mix_end)

            def gram_end(panel, top, height, columns, product):
                at = exact_at(panel, top, height, columns)
                values = exact_s[at] + product
                exact_s[at] = values
                put_mirrored(low_s, top, height, columns, values.astype(BF16))

            symmetric(mix_s, poly_s, size, gram_end)

        return carry

    lax.fori_loop(0, count, one, 0)


def first_body(count, packed_ref, x_ref, x_out, packed_out, x_s, exact_s, low_s, poly_s, mix_s, packed_s, sems):
    size = x_ref.shape[1]
    load_x = pltpu.make_async_copy(x_ref, x_s.at[0], sems.at[0])
    load_packed = pltpu.make_async_copy(packed_ref, packed_s, sems.at[1])
    load_x.start()
    load_packed.start()
    load_packed.wait()
    trace = jnp.zeros((1, 1), F32)
    eye = lax.broadcasted_iota(jnp.int32, (CHUNK, CHUNK), 0) == lax.broadcasted_iota(
        jnp.int32, (CHUNK, CHUNK), 1
    )
    for column in range(size // CHUNK):
        at = tri(column) * CHUNK + column * CHUNK
        block = jnp.where(eye, packed_s[at : at + CHUNK, :].astype(F32), 0.0)
        trace = trace + jnp.sum(jnp.sum(block, axis=1, keepdims=True), axis=0, keepdims=True)
    inverse = 1.0 / (jnp.sqrt(trace) + 1e-7)
    unpack(packed_s, size, inverse * inverse, exact_s, low_s)
    load_x.wait()
    iterate(x_s, exact_s, low_s, poly_s, mix_s, size, count)
    depth = x_ref.shape[0]

    def scale_rows(block, carry):
        rows = rows_at(block, CHUNK)
        x_s[count % 2, rows, :] = (x_s[count % 2, rows, :].astype(F32) * inverse).astype(BF16)
        return carry

    lax.fori_loop(0, depth // CHUNK, scale_rows, 0)
    store_x = pltpu.make_async_copy(x_s.at[count % 2], x_out, sems.at[0])
    store_x.start()
    gram_packed(x_s.at[count % 2], poly_s, size, packed_s)
    store_packed = pltpu.make_async_copy(packed_s, packed_out, sems.at[1])
    store_packed.start()
    store_x.wait()
    store_packed.wait()


def second_body(count, from_ref, packed_ref, x_ref, *refs):
    outs, (x_s, exact_s, low_s, poly_s, mix_s, packed_s, sems, out_sems) = refs[:-8], refs[-8:]
    size = x_ref.shape[1]
    load_x = pltpu.make_async_copy(x_ref, x_s.at[0], sems.at[0])
    load_packed = pltpu.make_async_copy(packed_ref, packed_s, sems.at[1])
    load_x.start()
    load_packed.start()
    load_packed.wait()
    unpack(packed_s, size, 1.0, exact_s, low_s)
    load_x.wait()
    iterate(x_s, exact_s, low_s, poly_s, mix_s, size, count)
    stores = []
    for out in outs:
        unit = x_ref.shape[0] // out_sems.shape[0]
        for at in range(0, out.shape[0], unit):
            source = pl.ds(pl.multiple_of(from_ref[len(stores)], unit), unit)
            stores.append(
                pltpu.make_async_copy(
                    x_s.at[count % 2, source, :], out.at[at : at + unit, :], out_sems.at[len(stores)]
                )
            )
    for store in stores:
        store.start()
    for store in stores:
        store.wait()


def ns_scratch(depth, size):
    return [
        pltpu.VMEM((2, depth, size), BF16),
        pltpu.VMEM((tri(size // PANEL) * PANEL, PANEL), F32),
        pltpu.VMEM((size, size), BF16),
        pltpu.VMEM((size, size), BF16),
        pltpu.VMEM((size, size), BF16),
        pltpu.VMEM((packed_rows(size), CHUNK), BF16),
        pltpu.SemaphoreType.DMA((2,)),
    ]


def first_gram(rows, early=(), late=()):
    depth, size = rows
    vmem = pl.BlockSpec(memory_space=pltpu.VMEM)
    shapes = (jax.ShapeDtypeStruct((depth, size), BF16), jax.ShapeDtypeStruct((packed_rows(size), CHUNK), BF16))
    me = lax.axis_index("dp").astype(jnp.int32).reshape(1)
    return pl.pallas_call(
        owned_gram_body,
        out_shape=shapes,
        in_specs=[pl.BlockSpec(memory_space=pltpu.SMEM)] + [vmem] * (len(early) + len(late)),
        out_specs=(vmem, vmem),
        scratch_shapes=[pltpu.VMEM((size, depth), BF16)],
        compiler_params=pltpu.CompilerParams(vmem_limit_bytes=VMEM_BYTES),
        cost_estimate=NOTHING,
        name="gram",
    )(me, *early, *late)


def orthogonalize(rows, packed, source_rows, pieces, after_gram, beside_first, after_first_steps, after_first, beside_last):
    depth, size = rows.shape
    packed_shape = jax.ShapeDtypeStruct((packed_rows(size), CHUNK), BF16)
    x_shape = jax.ShapeDtypeStruct((depth, size), BF16)
    vmem = pl.BlockSpec(memory_space=pltpu.VMEM)
    hbm = pl.BlockSpec(memory_space=pl.ANY)
    params = pltpu.CompilerParams(vmem_limit_bytes=VMEM_BYTES)

    def gram_sum(packed, meanwhile):
        part = lax.psum_scatter(packed, "group", scatter_dimension=0, tiled=True)
        return lax.all_gather(after(part, *jax.tree.leaves(meanwhile)), "group", axis=0, tiled=True)

    if packed is None:
        packed = pl.pallas_call(
            gram_body,
            out_shape=packed_shape,
            in_specs=[vmem],
            out_specs=vmem,
            scratch_shapes=[pltpu.VMEM((size, depth), BF16)],
            compiler_params=params,
            cost_estimate=NOTHING,
            name="gram",
        )(rows)
    meanwhile = after_gram(packed)
    gathered = gram_sum(packed, meanwhile)
    first = beside_first(gathered, meanwhile)
    half_way, packed = pl.pallas_call(
        functools.partial(first_body, 2),
        out_shape=(x_shape, packed_shape),
        in_specs=[hbm, hbm],
        out_specs=(hbm, hbm),
        scratch_shapes=ns_scratch(depth, size),
        compiler_params=params,
        cost_estimate=NOTHING,
        name="first_steps",
    )(gathered, rows)
    first = after_first_steps(first, packed)
    packed = after(packed, *first)
    meanwhile = after_first(packed, first)
    gathered = gram_sum(packed, meanwhile)
    last = beside_last(gathered)
    results = pl.pallas_call(
        functools.partial(second_body, 3),
        out_shape=[jax.ShapeDtypeStruct((piece, size), BF16) for piece in pieces],
        in_specs=[pl.BlockSpec(memory_space=pltpu.SMEM), hbm, hbm],
        out_specs=[hbm] * len(pieces),
        scratch_shapes=ns_scratch(depth, size) + [pltpu.SemaphoreType.DMA((source_rows.shape[0],))],
        compiler_params=params,
        cost_estimate=NOTHING,
        name="last_steps",
    )(source_rows, gathered, half_way)
    return results, first, meanwhile, last


def two_by_two():
    return lax.axis_size("dp") == 4


def hop(values, bit, targets=range(4)):
    return lax.ppermute(values, "dp", [(t ^ bit, t) for t in targets])


def by_distance(parts):
    me = lax.axis_index("dp")
    return jnp.stack([lax.dynamic_index_in_dim(parts, me ^ r, 0, keepdims=False) for r in range(4)])


def gather_near(own):
    return own, hop(own, 1), hop(own, 2)


def gather_far(near):
    own, from_x, from_y = near
    half = own.shape[0] // 2
    first, second = hop(from_y[:half], 1), hop(from_x[half:], 2)
    return jnp.stack([own, from_x, from_y, jnp.concatenate([first, second], axis=0)])


def reduce_start(sent_x, kept_x, sent_y, kept_y):
    return kept_x, hop(sent_x, 1), kept_y, hop(sent_y, 2)


def reduce_next(state, *others):
    def body(*refs):
        outs = refs[4 + len(others) :]
        for k in range(2):
            total = refs[2 * k][...].astype(F32) + refs[2 * k + 1][...].astype(F32)
            outs[2 * k][...] = total
            outs[2 * k + 1][...] = total.astype(BF16)

    shapes = [(state[0].shape, dtype) for dtype in (F32, BF16)] * 2
    total_x, out_x, total_y, out_y = in_vmem(body, state, others, shapes, "reduce_next")
    return (total_x, hop(out_x, 2, [1, 2]), total_y, hop(out_y, 1, [1, 2])), (out_x, out_y)


def scatter_start(split):
    left_out, left, right_out, right = split
    return left, hop(left_out, 1), right, hop(right_out, 2)


def scatter_next(state, *others):
    half = state[0].shape[0] // 2

    def body(*refs):
        outs = refs[4 + len(others) :]
        for k in range(2):
            total = refs[2 * k][...].astype(F32) + refs[2 * k + 1][...].astype(F32)
            outs[2 * k][...] = total[:half]
            outs[2 * k + 1][...] = total[half:].astype(BF16)

    shapes = [((half, state[0].shape[1]), dtype) for dtype in (F32, BF16)] * 2
    left, left_out, right, right_out = in_vmem(body, state, others, shapes, "scatter_next")
    return (left, hop(left_out, 2), right, hop(right_out, 1)), (left_out, right_out)


def scatter_end(state, *others):
    left, left_in, right, right_in = state
    if others:
        left, right = after(left, *others), after(right, *others)
    return jnp.concatenate([left + left_in.astype(F32), right + right_in.astype(F32)], axis=0)


def scatter_momentum(state, moment, *others):
    rows, width = moment.shape
    half = rows // 2

    def body(*refs):
        left, left_in, right, right_in, moment_ref = refs[:5]
        own, full = refs[5 + len(others) :]
        for at, (one, got) in ((0, (left, left_in)), (half, (right, right_in))):
            total = one[...] + got[...].astype(F32)
            own[at : at + half, :] = total
            full[at : at + half, :] = (total + moment_ref[at : at + half, :]).astype(BF16)

    shapes = [((rows, width), F32), ((rows, width), BF16)]
    return in_vmem(body, [*state, moment], others, shapes, "momentum")


def owners_start(slots, owners, *others):
    rows, width = slots[0].shape
    half = rows // 2
    me = lax.axis_index("dp").astype(jnp.int32).reshape(1)

    def body(me_ref, first_ref, second_ref, *refs):
        outs = refs[len(others) :]
        for r in range(4):
            picked = jnp.where((me_ref[0] ^ r) == owners[0], first_ref[...], second_ref[...])
            if r < 3:
                outs[r][...] = picked
            else:
                outs[3][...], outs[4][...] = picked[:half], picked[half:]

    shapes = [((rows, width), BF16)] * 3 + [((half, width), BF16)] * 2
    own, to_x, to_y, first_hop, second_hop = sent = in_vmem(body, slots, others, shapes, "to_owners", me)
    first_hop, second_hop = hop(first_hop, 1, [t ^ 2 for t in owners]), hop(second_hop, 2, [t ^ 1 for t in owners])
    return (own, hop(to_x, 1, owners), hop(to_y, 2, owners), first_hop, second_hop), sent[1:]


def owners_end(state, owners, *others):
    own, from_x, from_y, first_hop, second_hop = state
    return own, from_x, from_y, hop(after(first_hop, *others), 2, owners), hop(second_hop, 1, owners)


def exchange_dp(own, to_x, to_y, first_hop, second_hop):
    first_hop, second_hop = hop(first_hop, 1), hop(second_hop, 2)
    from_x, from_y = hop(to_x, 1), hop(to_y, 2)
    first, second = hop(first_hop, 2), hop(second_hop, 1)
    return jnp.stack([own, from_x, from_y, jnp.concatenate([first, second], axis=0)])


def butterfly_steps():
    return [
        (axis, 1 << bit) for axis in ("dp", "group") for bit in range((lax.axis_size(axis) - 1).bit_length())
    ]


def partner(values, axis, bit):
    return lax.ppermute(values, axis, [(i, i ^ bit) for i in range(lax.axis_size(axis))])


def heads_aligned(unit):
    return unit == HEAD and lax.axis_size("group") % 3 != 0


def spread_qkv(own, unit):
    group_count = lax.axis_size("group")
    me = lax.axis_index("group")
    moved = jnp.stack(
        [
            lax.ppermute(
                own[j * unit : (j + 1) * unit], "group", [(g, (3 * g + j) % group_count) for g in range(group_count)]
            )
            for j in range(3)
        ]
    )
    return jnp.concatenate(
        [lax.dynamic_index_in_dim(moved, (me + group_count * i) % 3, 0, keepdims=False) for i in range(3)]
    )


def return_qkv(rows, unit):
    group_count = lax.axis_size("group")
    me = lax.axis_index("group")
    inverse = pow(group_count, -1, 3)
    parts = rows.reshape(3, unit, rows.shape[1])
    return jnp.concatenate(
        [
            lax.ppermute(
                lax.dynamic_index_in_dim(parts, ((j - me) * inverse) % 3, 0, keepdims=False),
                "group",
                [((3 * g + j) % group_count, g) for g in range(group_count)],
            )
            for j in range(3)
        ]
    )


def head_rows(matrix, heads):
    group_count = lax.axis_size("group")
    lead = matrix.shape[:-2]
    split = matrix.reshape(lead + (heads, group_count, HEAD, matrix.shape[-1]))
    picked = lax.dynamic_index_in_dim(split, lax.axis_index("group"), len(lead) + 1, keepdims=False)
    return picked.reshape(lead + (heads * HEAD, matrix.shape[-1]))


def spread_heads(rows, heads):
    group_count = lax.axis_size("group")
    lead = rows.shape[:-2]
    width = rows.shape[-1]
    part = rows.reshape(lead + (heads, 1, HEAD, width))
    empty = jnp.zeros(lead + (heads, group_count, HEAD, width), rows.dtype)
    placed = lax.dynamic_update_slice_in_dim(empty, part, lax.axis_index("group"), len(lead) + 1)
    return placed.reshape(lead + (heads * group_count * HEAD, width))


def shards(
    hidden_in,
    cotangent,
    segment_ids,
    weight_in,
    weight_back,
    moment_in,
    moment_back,
    norm_gain,
    norm_shift,
    bias_in,
    bias_out,
    vector_moment,
):
    model_width = hidden_in.shape[2]
    tokens = hidden_in.shape[1]
    data_count = lax.axis_size("dp")
    group_count = lax.axis_size("group")
    devices = data_count * group_count
    me_group = lax.axis_index("group")
    me = lax.axis_index("dp")
    unit = model_width // devices
    qkv_rows = 3 * unit
    ff_rows = FF // devices
    out_rows = unit
    heads = HEADS // group_count
    width = heads * HEAD
    fast = heads_aligned(unit) and two_by_two()
    everywhere = ("dp", "group")

    def dot(left, right):
        return jnp.dot(left, right, preferred_element_type=F32)

    def dot_last(left, right):
        return lax.dot_general(left, right, (((1,), (1,)), ((), ())), preferred_element_type=F32)

    def dot_first(left, right):
        return lax.dot_general(left, right, (((0,), (0,)), ((), ())), preferred_element_type=F32)

    x_float = hidden_in[0].astype(F32)
    centre = x_float - jnp.mean(x_float, axis=-1, keepdims=True)
    inverse_std = lax.rsqrt(jnp.mean(centre * centre, axis=-1, keepdims=True) + 1e-05)
    x_hat = centre * inverse_std
    normed_low = (x_hat * norm_gain + norm_shift).astype(BF16)
    grad_y = cotangent[0]
    parts = max(1, width // 128)
    lanes = width // parts
    w_in, w_back = weight_in[0], weight_back[0]
    m_in, m_back = MOMENTUM * moment_in[0], MOMENTUM * moment_back[0]
    position = positions(segment_ids[0])
    start = jnp.arange(position.shape[0], dtype=jnp.int32) - position
    tables = (start[::CHUNK] // CHUNK, start[:, None]) + rotary_lanes(position, lanes // HEAD)
    grad_y_float = grad_y.astype(F32)

    def to_parts(rows):
        split = rows.reshape((3, parts, lanes) + rows.shape[1:])
        return jnp.swapaxes(split, 0, 1).reshape(rows.shape)

    def from_parts(rows):
        split = rows.reshape((parts, 3, lanes) + rows.shape[1:])
        return jnp.swapaxes(split, 0, 1).reshape(rows.shape)

    normed_all = lax.all_gather(normed_low, "group", axis=0, tiled=True)
    if fast:
        w_up = gather_far(gather_near(w_in[qkv_rows:]))
        near_qkv = gather_near(spread_qkv(w_in[:qkv_rows], unit))
        grad_all = lax.all_gather(after(grad_y, normed_all, w_up, *near_qkv[1:], *tables), "group", axis=0, tiled=True)
    else:
        grad_all = lax.all_gather(grad_y, "group", axis=0, tiled=True)
        w_up = lax.all_gather(w_in[qkv_rows:], "dp", axis=0, tiled=True)
    w_up = w_up.reshape(data_count * ff_rows, model_width)

    bias_up = lax.dynamic_index_in_dim(
        bias_in[3 * model_width :].reshape(data_count, group_count, ff_rows), me_group, 1, keepdims=False
    )
    bias_up = (by_distance(bias_up) if fast else bias_up).reshape(data_count * ff_rows)
    bias_qkv = bias_in[: 3 * model_width].reshape(3 * heads, group_count, HEAD)
    bias_qkv = to_parts(lax.dynamic_index_in_dim(bias_qkv, me_group, 1, keepdims=False).reshape(3 * width))
    activated, slope = up_forward(normed_all, w_up, bias_up)
    if fast:
        near_back = gather_near(after(w_back, *near_qkv[1:]))
        own, from_x, from_y = near_qkv
        w_qkv = by_distance(gather_far((own, after(from_x, activated), after(from_y, activated))))
        own, from_x, from_y = near_back
        all_back = gather_far((own, after(from_x, activated), after(from_y, activated)))
        w_out = by_distance(all_back[:, :out_rows]).reshape(width, model_width)
        w_down = all_back[:, out_rows:].reshape(data_count * ff_rows, model_width)
    else:
        all_qkv = lax.all_gather(w_in[:qkv_rows], everywhere, axis=0, tiled=True)
        w_qkv = head_rows(all_qkv.reshape(3, model_width, model_width), heads)
        w_out = head_rows(lax.all_gather(w_back[:out_rows], everywhere, axis=0, tiled=True), heads)
        w_down = lax.all_gather(w_back[out_rows:], "dp", axis=0, tiled=True)
    w_qkv = to_parts(w_qkv.reshape(3 * width, model_width))
    pre_qkv = project(normed_all, w_qkv, bias_qkv, F32, "project_qkv")
    branch_up = dot(activated, w_down)
    grad_all = after(grad_all, activated, slope, pre_qkv, w_down, w_out, branch_up)

    term_down = weight_grad(activated, grad_all, "grad_down", fast)
    if fast:
        sum_down = scatter_start(term_down)
        m_qkv = spread_qkv(after(m_in[:qkv_rows], term_down[0]), unit)
        slope = after(slope, *term_down)
    grad_pre_up = up_backward(grad_all, slope, w_down)
    term_up = weight_grad(grad_pre_up, normed_all, "grad_up", fast)
    late_w_out = w_out
    if fast:
        sum_up = scatter_start(term_up)
        sum_down, flying = scatter_next(sum_down, *term_up)
        late_w_out = after(w_out, *flying)
    grad_attended = project(grad_all, late_w_out, jnp.zeros((width,), F32), BF16, "project_grad")
    ready = ()

    attended, grad_pre_qkv, term_qkv, term_out, sum_att = [], [], [], [], []
    for part in range(parts):
        one, one_grad = attention(pre_qkv, after(grad_attended, *ready), tables, part, lanes)
        attended.append(one)
        grad_pre_qkv.append(one_grad)
        if not fast:
            ready = (one,)
            term_qkv.append(dot_first(one_grad, normed_all).astype(BF16))
            term_out.append(dot_first(one, grad_all).astype(BF16))
            continue
        if part == 0:
            sum_up, flying = scatter_next(sum_up, one)
            own_down, full_down = scatter_momentum(sum_down, m_back[out_rows:], one)
            one_grad = after(one_grad, full_down, *flying)
        else:
            first_half, flying = reduce_next(sum_att[0], one)
            one_grad = after(one_grad, *flying)
        one_qkv, one_out, *split = weight_grads_plus(
            one_grad,
            normed_all,
            one,
            grad_all,
            m_qkv,
            m_back[:out_rows],
            part,
            heads,
        )
        sum_att.append(reduce_start(*split))
        if part == 0:
            own_up, full_up = scatter_momentum(sum_up, m_in[qkv_rows:], split[0])
            early, ready = owners_start([full_up, full_down], [0, 3])
        term_qkv.append(one_qkv)
        term_out.append(one_out)

    if fast:
        early = owners_end(early, [0, 3], split[0])
        second_half, _ = reduce_next(sum_att[1])
        owned, packed = first_gram((data_count * ff_rows, model_width), early, (*first_half, *second_half))
    else:
        packed = None
        term_qkv = from_parts(jnp.concatenate(term_qkv))
        term_out = jnp.concatenate(term_out)
        grad_w_qkv = lax.psum_scatter(
            spread_heads(term_qkv.reshape(3, width, model_width), heads).reshape(3 * model_width, model_width),
            everywhere,
            scatter_dimension=0,
            tiled=True,
        ).astype(F32)
        grad_w_out = lax.psum_scatter(
            spread_heads(term_out, heads), everywhere, scatter_dimension=0, tiled=True
        ).astype(F32)
        own_up = lax.psum_scatter(term_up, "dp", scatter_dimension=0, tiled=True).astype(F32)
        own_down = lax.psum_scatter(term_down, "dp", scatter_dimension=0, tiled=True).astype(F32)
        slots = [m_in[qkv_rows:] + own_up, m_in[:qkv_rows] + grad_w_qkv, m_back[:out_rows] + grad_w_out]
        slots = slots + [m_back[out_rows:] + own_down] + [jnp.zeros((0, model_width))] * (data_count - 4)
        slots = [jnp.pad(rows.astype(BF16), ((0, ff_rows - rows.shape[0]), (0, 0))) for rows in slots]
        owned = lax.all_to_all(jnp.stack(slots), "dp", split_axis=0, concat_axis=0, tiled=True)
        owned = owned.reshape(data_count * ff_rows, model_width)

    def after_gram(packed):
        late_qkv, late_up = jnp.concatenate(grad_pre_qkv, axis=1), after(grad_pre_up, packed)
        late_qkv = after(late_qkv, packed)
        normed_part = dot(late_qkv, w_qkv) + dot(late_up, w_up)
        split = ()
        if fast:
            terms = [from_parts(jnp.concatenate(term_qkv)), jnp.concatenate(term_out)]
            terms = [after(one, packed).reshape(data_count, -1, model_width) for one in terms]
            terms = by_distance(jnp.concatenate(terms, axis=1)).reshape(2, 2, 2, unit * 2, model_width)
            split = terms[:, 1, 0], terms[:, 0, 0], terms[1, :, 1], terms[0, :, 1]
            split = [one.reshape(4 * unit, model_width) for one in split]
        branch_part = dot(after(attended_all, packed), w_out) + branch_up
        return normed_part.astype(BF16), late_qkv, late_up, split, branch_part.astype(BF16)

    kept = [None]
    attended_all = jnp.concatenate(attended, axis=1)

    def beside_first(gathered, meanwhile):
        kept.extend(meanwhile[1:])
        if fast:
            split = [after(one, gathered) for one in kept[3]]
            kept.append(scatter_start(split))
        return (lax.psum_scatter(after(meanwhile[0], gathered), "group", scatter_dimension=0, tiled=True),)

    def after_first_steps(first, packed):
        if not fast:
            return first
        state, flying = scatter_next(kept[5], packed)
        kept.append(state)
        return first + flying

    def after_first(packed, first):
        grad_normed = first[0].astype(F32)
        grad_x_hat = grad_normed * norm_gain
        grad_hidden = grad_y_float + inverse_std * (
            grad_x_hat
            - jnp.mean(grad_x_hat, axis=-1, keepdims=True)
            - x_hat * jnp.mean(grad_x_hat * x_hat, axis=-1, keepdims=True)
        )
        if fast:
            own = scatter_end(kept[6])
            own_qkv = return_qkv(own[:qkv_rows].astype(BF16), unit).astype(F32)
            own_out = own[qkv_rows:]
        else:
            own_qkv, own_out = grad_w_qkv, grad_w_out
        grad_in = jnp.concatenate([own_qkv, own_up])
        grad_back = jnp.concatenate([own_out, own_down])
        grads = grad_in, grad_back, m_in + grad_in, m_back + grad_back
        sums_up = jnp.sum(kept[2].astype(F32), axis=0).reshape(data_count, ff_rows)
        sums_qkv = jnp.sum(kept[1].astype(F32), axis=0)
        vector_local = jnp.concatenate(
            [
                jnp.sum(grad_normed * x_hat, axis=0),
                jnp.sum(grad_normed, axis=0),
                placed(from_parts(sums_qkv), 3 * heads, HEAD),
                placed(by_distance(sums_up) if fast else sums_up, data_count, ff_rows),
                jnp.sum(grad_y_float, axis=0),
            ]
        )
        for step in butterfly_steps()[:-1]:
            vector_local = vector_local + partner(vector_local, *step)
        return grad_hidden, vector_local, *grads

    def beside_last(gathered):
        return (lax.psum_scatter(after(kept[4], gathered), "group", scatter_dimension=0, tiled=True),)

    def placed(sums, lead, size):
        empty = jnp.zeros((lead, group_count, size), F32)
        return lax.dynamic_update_slice_in_dim(empty, sums.reshape(lead, 1, size), me_group, 1).reshape(-1)

    if fast:
        distance, run = jnp.divmod(jnp.arange(4 * ff_rows // unit), ff_rows // unit)
        holder = me ^ distance
        kind, head = jnp.divmod(3 * holder + jnp.minimum(run, 2), heads)
        per_part = heads // parts
        of_qkv = (head // per_part) * 3 * lanes + kind * lanes + (head % per_part) * HEAD
        source_rows = jnp.where(me == 1, of_qkv, jnp.where(me == 2, holder * unit, distance * ff_rows + run * unit))
        pieces = [ff_rows] * 3 + [ff_rows // 2] * 2
    else:
        source_rows = jnp.arange(0, data_count * ff_rows, ff_rows)
        pieces = [data_count * ff_rows]
    results, _, meanwhile, (branch,) = orthogonalize(
        owned, packed, source_rows.astype(jnp.int32), pieces, after_gram, beside_first, after_first_steps, after_first, beside_last
    )
    grad_hidden, vector_half, grad_in, grad_back, moment_in_new, moment_back_new = meanwhile
    vector_grad = vector_half + partner(after(vector_half, results[0]), *butterfly_steps()[-1])
    block_out = (x_float + branch.astype(F32) + bias_out).astype(BF16)
    if fast:
        returned = by_distance(exchange_dp(*results))
        o_qkv = return_qkv(returned[1, :qkv_rows], unit)
    else:
        result = results[0].reshape(data_count, ff_rows, model_width)
        returned = lax.all_to_all(result, "dp", split_axis=0, concat_axis=0, tiled=True)
        o_qkv = returned[1, :qkv_rows]

    def step_of(rows, scale):
        return -scale * rows.astype(F32)

    scale_ff = math.sqrt(1.0 * FF)
    step_in = jnp.concatenate(
        [step_of(o_qkv, math.sqrt(3.0 * model_width)), step_of(returned[0], scale_ff)], axis=0
    )[None]
    step_back = jnp.concatenate(
        [step_of(returned[2, :out_rows], math.sqrt(1.0 * model_width)), step_of(returned[3], scale_ff)], axis=0
    )[None]
    bias_out_grad = vector_grad[vector_grad.shape[0] - model_width :]
    vector_moment_new = MOMENTUM * vector_moment + vector_grad
    vector_step = -(0.2 / math.sqrt(tokens * devices)) * vector_moment_new
    return (
        block_out[None],
        grad_hidden[None],
        grad_in[None],
        grad_back[None],
        moment_in_new[None],
        moment_back_new[None],
        step_in,
        step_back,
        vector_grad,
        vector_moment_new,
        vector_step,
        bias_out_grad,
    )


def solution(mesh):
    tokens_spec = P("dp", "group", None)
    blocks_spec = P(("dp", "group"), None, None)
    in_specs = (
        (tokens_spec, tokens_spec, P("dp", None))
        + (blocks_spec,) * 4
        + (P(),) * 5
    )
    out_specs = (tokens_spec, tokens_spec) + (blocks_spec,) * 6 + (P(),) * 4
    return jax.shard_map(shards, mesh=mesh, in_specs=in_specs, out_specs=out_specs, check_vma=False)
```
